32 devices in a mesh: dp: 16 (over z, y, core), fsdp: 2 (over x).
Axes of the slice: x: 2, y: 2, z: 4, core: 2. Of those that a mesh axis runs over, the one named last changes fastest.
Arguments:
- inputs: float32 [32, 512, 512], P(('dp', 'fsdp')), may hold values from -6 to 6
- cotangent: float32 [32, 512, 512], P(('dp', 'fsdp')), may hold values from -6 to 6
- lengths: int32 [32], P(('dp', 'fsdp')), may hold values from 1 to 512, 4096 in all
- filters: float32 [512, 24], replicated, may hold values from -0.25 to 0.25
- gain_first: float32 [512], P(('dp', 'fsdp')), may hold values from 0.1 to 1.9
- mix_plus: float32 [12288, 512], P(('dp', 'fsdp')), may hold values from -0.0390625 to 0.0390625
- mix_minus: float32 [12288, 512], P(('dp', 'fsdp')), may hold values from -0.0390625 to 0.0390625
- auto_weight: float32 [1536, 512], P(('dp', 'fsdp')), may hold values from -0.15625 to 0.15625
- gain_second: float32 [512], P(('dp', 'fsdp')), may hold values from 0.1 to 1.9
- w_gate: float32 [512, 2048], P(('dp', 'fsdp')), may hold values from -0.25 to 0.25
- w_upward: float32 [512, 2048], P(('dp', 'fsdp')), may hold values from -0.25 to 0.25
- w_down: float32 [2048, 512], P(('dp', 'fsdp')), may hold values from -0.25 to 0.25
Outputs:
- output: float32 [32, 512, 512], P(('dp', 'fsdp'))
- input_grad: float32 [32, 512, 512], P(('dp', 'fsdp'))
- grad_gain_first: float32 [512], P(('dp', 'fsdp'))
- grad_mix_plus: float32 [12288, 512], P(('dp', 'fsdp'))
- grad_mix_minus: float32 [12288, 512], P(('dp', 'fsdp'))
- grad_auto: float32 [1536, 512], P(('dp', 'fsdp'))
- grad_gain_second: float32 [512], P(('dp', 'fsdp'))
- grad_gate: float32 [512, 2048], P(('dp', 'fsdp'))
- grad_upward: float32 [512, 2048], P(('dp', 'fsdp'))
- grad_down: float32 [2048, 512], P(('dp', 'fsdp'))
The draws below stay inside these ranges and needn't reach their ends.
Inputs may be any that keep to these rules, and one draw needn't show every extreme that they name: `lengths`: used tokens of each row, counted from its start; they sum to 4096.
All inputs are finite; a program needn't handle non-finite values. No bound on the sum of `lengths` on one device may be relied on, other than what follows from the above.
Results may differ from the reference program's by a relative error of at most 0.012.
Values may be sent and summed in bfloat16 or wider, within the bound.
No kernel may reach another device: no remote copies, remote signals or barrier semaphores. Data moves between devices by JAX's collectives and lax.ppermute only.
A program may use at most 384 MiB of HBM per device.

```python
import math
import jax
import jax.numpy as jnp
import numpy as np
from jax import lax

D = 512
FF = 2048
FILTERS = 24
SEQ = 512
ROWS = 32


def steps_of(key, extent, pieces, least, high):
    loudness = 1.0
    for dim, shards_of in pieces:
        heights = jax.random.uniform(jax.random.fold_in(jax.random.fold_in(key, 6), dim), (shards_of,), jnp.float32, least / len(pieces), high / len(pieces))
        loudness = loudness * jnp.repeat(jnp.exp(heights), extent[dim] // shards_of).reshape((-1,) + (1,) * (len(extent) - 1 - dim))
    return loudness


def profile(count, total, bound, skew):
    portions = [(1 << 20) // math.isqrt(standing ** skew) + 1 for standing in range(2, count + 1)]
    rest, given = total - bound - (count - 1), [1] * (count - 1)
    while rest > 0:
        free = [i for i in range(count - 1) if given[i] < bound]
        mass, remaining = sum([portions[i] for i in free]), rest
        for i in free:
            addition = min(bound - given[i], max(1, remaining * portions[i] // mass), rest)
            given[i] = given[i] + addition
            rest = rest - addition
    return np.array([bound] + given)


def uneven(rng, amount, total, reach, skew):
    if amount == 2:
        one = jax.random.randint(rng, (), max(1, total - reach), min(reach, total - 1) + 1)
        return jnp.stack([one, total - one])
    sizes = jnp.asarray(profile(amount, total, reach, skew), jnp.int32)
    pairs = (amount - 1) // 2
    donor, sink = sizes[1:1 + 2 * pairs:2], sizes[2:2 + 2 * pairs:2]
    slack = jnp.minimum(donor - 1, reach - sink)
    passed = jax.random.randint(jax.random.fold_in(rng, 1), (pairs,), 0, 1 << 20) % (slack + 1)
    sizes = sizes.at[1:1 + 2 * pairs:2].set(donor - passed).at[2:2 + 2 * pairs:2].set(sink + passed)
    return sizes[jax.random.permutation(jax.random.fold_in(rng, 2), amount)]


def normal_values(key, extent, width, most, cuts=(), kind=jnp.bfloat16):
    values = width * jax.random.normal(key, extent, jnp.float32)
    if cuts:
        values = values * steps_of(key, extent, cuts, -0.22, 0.18)
    return jnp.clip(values, -most, most).astype(kind)


def setup_inputs(seed: int = 0) -> dict:
    key_list = jax.random.split(jax.random.key(seed), 13)
    inputs = normal_values(key_list[0], (ROWS, SEQ, D), 1.0, 6.0, ((0, 32),), jnp.float32)
    cotangent = normal_values(key_list[1], (ROWS, SEQ, D), 1.0, 6.0, ((0, 32),), jnp.float32)
    lengths = uneven(key_list[2], ROWS, ROWS * SEQ // 4, SEQ, 2).astype(jnp.int32)
    filters = normal_values(key_list[3], (SEQ, FILTERS), SEQ ** -0.5, 0.25, (), jnp.float32)
    gain_first = jnp.clip(1.0 + 0.18 * jax.random.normal(key_list[4], (D,), jnp.float32), 0.1, 1.9)
    mix_plus = normal_values(key_list[5], (FILTERS * D, D), (2 * FILTERS * D) ** -0.5, 0.0390625, ((0, 32),), jnp.float32)
    mix_minus = normal_values(key_list[6], (FILTERS * D, D), (2 * FILTERS * D) ** -0.5, 0.0390625, ((0, 32),), jnp.float32)
    auto_weight = normal_values(key_list[7], (3 * D, D), (3 * D) ** -0.5, 0.15625, ((0, 32),), jnp.float32)
    gain_second = jnp.clip(1.0 + 0.18 * jax.random.normal(key_list[8], (D,), jnp.float32), 0.1, 1.9)
    w_gate = normal_values(key_list[9], (D, FF), D ** -0.5, 0.25, ((0, 32),), jnp.float32)
    w_upward = normal_values(key_list[10], (D, FF), D ** -0.5, 0.25, ((0, 32),), jnp.float32)
    w_down = normal_values(key_list[11], (FF, D), (FF // 4) ** -0.5, 0.25, ((0, 32),), jnp.float32)
    return dict(inputs=inputs, cotangent=cotangent, lengths=lengths, filters=filters, gain_first=gain_first, mix_plus=mix_plus, mix_minus=mix_minus, auto_weight=auto_weight, gain_second=gain_second, w_gate=w_gate, w_upward=w_upward, w_down=w_down)


@jax.custom_vjp
def low(v):
    return lax.optimization_barrier(v.astype(jnp.bfloat16)).astype(jnp.float32)

@jax.custom_vjp
def low_back(v):
    return v

def low_keep(v):
    return (low(v), None)

def low_pass(kept, grad):
    return (grad,)

def back_keep(v):
    return (v, None)

def back_low(kept, grad):
    return (low(grad),)
low.defvjp(low_keep, low_pass)
low_back.defvjp(back_keep, back_low)
EPSILON = 1e-05

def rms_scale(values):
    return lax.rsqrt(lax.optimization_barrier(jnp.mean(values * values, axis=-1, keepdims=True)) + EPSILON)

def causal_conv(signal, filter_taps):
    seq_len = signal.shape[1]
    signal_freq = jnp.fft.rfft(signal, n=2 * seq_len, axis=1)
    taps_freq = jnp.fft.rfft(filter_taps, n=2 * seq_len, axis=0)
    product = signal_freq[:, :, None, :] * taps_freq[None, :, :, None]
    return jnp.fft.irfft(product, n=2 * seq_len, axis=1)[:, :seq_len]

def lagged_of(normed):
    seq_len = normed.shape[1]
    padded = jnp.pad(normed, ((0, 0), (2, 0), (0, 0)))
    return jnp.concatenate([padded[:, 2:], padded[:, 1:seq_len + 1], padded[:, :seq_len]], axis=-1)

def matmul(left, right):
    return jnp.dot(left, right, precision=lax.Precision.HIGHEST)

def layer(block, weights, filter_taps, keep_mask):
    gain_first, mix_plus, mix_minus, auto_weight, gain_second, w_gate, w_upward, w_down = weights
    group, seq_len, model_width = block.shape
    tokens_here = group * seq_len
    normed = low(block * rms_scale(block) * low(gain_first))
    spectral = low(low_back(causal_conv(normed, filter_taps)))
    features = spectral.reshape(tokens_here, -1)
    stacked = jnp.concatenate([low(mix_plus), low(mix_minus)], axis=0)
    lagged = lagged_of(normed).reshape(tokens_here, -1)
    mixed_sum = matmul(features, stacked) + matmul(lagged, low(auto_weight))
    middle = block + low_back(mixed_sum).reshape(group, seq_len, model_width)
    normed_two = low(middle * rms_scale(middle) * low(gain_second)).reshape(tokens_here, model_width)
    gate_pre = low_back(matmul(normed_two, low(w_gate)))
    upward = low_back(matmul(normed_two, low(w_upward)))
    hidden = low(jax.nn.gelu(gate_pre) * upward)
    mlp_out = low_back(matmul(hidden, low(w_down))).reshape(group, seq_len, model_width)
    return keep_mask * (middle + mlp_out)

def reference(inputs, cotangent, lengths, filters, gain_first, mix_plus, mix_minus, auto_weight, gain_second, w_gate, w_upward, w_down):
    row_count = inputs.shape[0]
    group = math.gcd(row_count, max(1, 1024 // SEQ))
    steps_count = row_count // group
    phi = low(filters)
    parity = 1.0 - 2.0 * (jnp.arange(SEQ) % 2).astype(filters.dtype)
    filter_taps = jnp.concatenate([phi, phi * parity[:, None]], axis=1)
    weights = (gain_first, mix_plus, mix_minus, auto_weight, gain_second, w_gate, w_upward, w_down)
    input_groups = inputs.reshape(steps_count, group, SEQ, D)
    cot_groups = cotangent.reshape(steps_count, group, SEQ, D)
    length_groups = lengths.reshape(steps_count, group)

    def one_group(totals, item):
        block, block_cot, block_lengths = item
        keep_mask = (jnp.arange(SEQ)[None, :] < block_lengths[:, None]).astype(block.dtype)[:, :, None]

        def forward(block_in, weight_tuple):
            return layer(block_in, weight_tuple, filter_taps, keep_mask)
        result, pullback = jax.vjp(forward, block, weights)
        grad_block, grad_weights = pullback(block_cot)
        totals = tuple((total + grad for total, grad in zip(totals, grad_weights)))
        return (totals, (result, grad_block))
    initial = tuple((jnp.zeros_like(weight) for weight in weights))
    totals, (results, grads_in) = lax.scan(one_group, initial, (input_groups, cot_groups, length_groups))
    output = results.reshape(row_count, SEQ, D)
    input_grad = grads_in.reshape(row_count, SEQ, D)
    return (output, input_grad, totals[0], totals[1], totals[2], totals[3], totals[4], totals[5], totals[6], totals[7])
```

```python
import functools

import jax
import jax.numpy as jnp
from jax import lax
from jax.experimental import pallas as pl
from jax.experimental.pallas import tpu as pltpu
from jax.sharding import Mesh, PartitionSpec as P

EPSILON = 1e-05
MEMBERS = 8
HALVES = 2
BLOCK = 256
LAGS = 3
VMEM_LIMIT = 60 * 1024 * 1024
BF = jnp.bfloat16
F32 = jnp.float32
ALL = ("h", "m", "l")
ANY = pl.BlockSpec(memory_space=pl.ANY)
VM = pl.BlockSpec(memory_space=pltpu.VMEM)
SM = pl.BlockSpec(memory_space=pltpu.SMEM)


def rms_scale(values):
    return lax.rsqrt(jnp.mean(values * values, axis=-1, keepdims=True) + EPSILON)


def rms_back(values, scale, d_pre):
    return scale * d_pre - values * (scale * scale * scale) * jnp.mean(
        d_pre * values, axis=-1, keepdims=True
    )


def flip(x, axis, bit):
    size = lax.axis_size(axis)
    return lax.ppermute(x, axis, [(i, i ^ bit) for i in range(size)])


def dot(a, b):
    return jnp.dot(a, b, preferred_element_type=F32)


def dot_nt(a, b):
    return lax.dot_general(a, b, (((1,), (1,)), ((), ())), preferred_element_type=F32)


def group_gather(row):
    half = row.shape[0] // 2
    near1 = flip(row, "m", 2)
    near2 = flip(row, "m", 4)
    core0 = flip(row, "m", 1)
    far_top = flip(near2[:half], "m", 2)
    far_low = flip(near1[half:], "m", 4)
    core1 = flip(near1, "m", 1)
    core2 = flip(near2, "m", 1)
    core_top = flip(far_top, "m", 1)
    core_low = flip(far_low, "m", 1)
    return (row, core0, near1, core1, near2, core2, far_top, far_low, core_top, core_low)


def group_scatter(parts):
    own, core0, near1, core1, near2, core2, far_top, far_low, core_top, core_low = parts
    half = own.shape[0] // 2
    far_top = (far_top.astype(F32) + flip(core_top, "m", 1).astype(F32)).astype(BF)
    far_low = (far_low.astype(F32) + flip(core_low, "m", 1).astype(F32)).astype(BF)
    got_top = flip(far_top, "m", 2).astype(F32)
    got_low = flip(far_low, "m", 4).astype(F32)
    near1 = near1.astype(F32) + flip(core1, "m", 1).astype(F32)
    near2 = near2.astype(F32) + flip(core2, "m", 1).astype(F32)
    near1 = jnp.concatenate([near1[:half], near1[half:] + got_low], axis=0).astype(BF)
    near2 = jnp.concatenate([near2[:half] + got_top, near2[half:]], axis=0).astype(BF)
    own = own.astype(F32) + flip(core0, "m", 1).astype(F32)
    return own + flip(near1, "m", 2).astype(F32) + flip(near2, "m", 4).astype(F32)


def gather_l(x):
    size = lax.axis_size("l")
    if size != 2:
        return lax.all_gather(x, "l", axis=0, tiled=True)
    peer = flip(x, "l", 1)
    first = lax.axis_index("l") == 0
    return jnp.concatenate([jnp.where(first, x, peer), jnp.where(first, peer, x)], axis=0)


def scatter_l(x, axis):
    size = lax.axis_size("l")
    if size != 2:
        return lax.psum_scatter(x.astype(F32), "l", scatter_dimension=axis, tiled=True)
    part = x.shape[axis] // 2
    mine = lax.axis_index("l")
    kept = lax.dynamic_slice_in_dim(x, mine * part, part, axis)
    sent = lax.dynamic_slice_in_dim(x, (1 - mine) * part, part, axis)
    return kept.astype(F32) + flip(sent.astype(BF), "l", 1).astype(F32)


def split_bit(x, axis_name, bit, axis, mine):
    kept = lax.dynamic_index_in_dim(x, mine, axis, keepdims=False)
    sent = lax.dynamic_index_in_dim(x, 1 - mine, axis, keepdims=False)
    return (kept.astype(F32) + flip(sent, axis_name, bit).astype(F32)).astype(BF)


def scatter_all(x, order):
    size_l = lax.axis_size("l")
    rows = x.shape[0] // (HALVES * MEMBERS * size_l)
    tail = x.shape[1:]
    x = x.reshape((2, 2, 2, 2, size_l, rows) + tail)
    m = lax.axis_index("m")
    names = ["h", "z", "y", "c", "l"]
    for what in order:
        at = names.index(what)
        names.remove(what)
        if what == "h":
            x = split_bit(x, "h", 1, at, lax.axis_index("h"))
        elif what == "l":
            if size_l == 2:
                x = split_bit(x, "l", 1, at, lax.axis_index("l"))
            else:
                x = lax.psum_scatter(x.astype(F32), "l", scatter_dimension=at, tiled=False)
                x = x.astype(BF)
        else:
            shift = "cyz".index(what)
            x = split_bit(x, "m", 1 << shift, at, (m >> shift) & 1)
    return x.reshape((rows,) + tail).astype(F32)


def sum_all(x):
    n = lax.axis_size("h") * lax.axis_size("m") * lax.axis_size("l")
    step = 1
    while step < n:
        x = x + lax.ppermute(x, ALL, [(i, i ^ step) for i in range(n)])
        step *= 2
    return x


def tables_kernel(base_ref, fwd_ref, bwd_ref):
    rows, width = fwd_ref.shape[1], fwd_ref.shape[2]
    span = base_ref.shape[1]
    odd = (
        lax.broadcasted_iota(jnp.int32, (rows, width), 0)
        + lax.broadcasted_iota(jnp.int32, (rows, width), 1)
    ) % 2
    sign = (1 - 2 * odd).astype(F32)
    for index in range(4):
        for which, out in ((0, fwd_ref), (1, bwd_ref)):
            line = jnp.broadcast_to(base_ref[pl.ds(which * 4 + index, 1), :], (rows, span))
            rolled = pltpu.roll(line, 0, 1, stride=1, stride_axis=0)[:, :width]
            out[2 * index] = rolled.astype(BF)
            out[2 * index + 1] = (rolled * sign).astype(BF)


def build_tables(filters, h, m):
    seq_len, count = filters.shape
    phi = jnp.transpose(filters.astype(BF).astype(F32))
    zeros = jnp.zeros((count, BLOCK), F32)
    bwd = jnp.concatenate([phi, zeros], axis=1)
    back = jnp.flip(phi, axis=1)
    fwd = jnp.concatenate(
        [
            back[:, seq_len - 1 - BLOCK :],
            jnp.zeros((count, BLOCK), F32),
            back[:, : seq_len - 1 - BLOCK],
        ],
        axis=1,
    )
    rows = []
    for table in (fwd, bwd):
        for rel in range(HALVES):
            first = 12 * (h ^ rel) + (3 * m) // 2
            rows.append(lax.dynamic_slice_in_dim(table, first, 2, 0))
    base = jnp.concatenate(rows, axis=0)
    shape = jax.ShapeDtypeStruct((8, BLOCK, seq_len), BF)
    return pl.pallas_call(
        tables_kernel,
        out_shape=(shape, shape),
        in_specs=[VM],
        out_specs=(VM, VM),
        compiler_params=pltpu.CompilerParams(vmem_limit_bytes=VMEM_LIMIT),
        cost_estimate=pl.CostEstimate(flops=20_000_000, bytes_accessed=5_000_000, transcendentals=0),
    )(base)


def load_rows(refs, scratch, sem):
    half = scratch.shape[1] // 2
    copies = []
    for j in range(6):
        copies.append((refs[j], scratch.at[j]))
    for j in (6, 7):
        copies.append((refs[2 * j - 6], scratch.at[j, pl.ds(0, half)]))
        copies.append((refs[2 * j - 5], scratch.at[j, pl.ds(half, half)]))
    started = [pltpu.make_async_copy(a, b, sem.at[k]) for k, (a, b) in enumerate(copies)]
    for copy in started:
        copy.start()
    return started


def store_rows(scratch, refs, sem):
    half = scratch.shape[1] // 2
    copies = []
    for j in range(6):
        copies.append((scratch.at[j], refs[j]))
    for j in (6, 7):
        copies.append((scratch.at[j, pl.ds(0, half)], refs[2 * j - 6]))
        copies.append((scratch.at[j, pl.ds(half, half)], refs[2 * j - 5]))
    started = [pltpu.make_async_copy(a, b, sem.at[k]) for k, (a, b) in enumerate(copies)]
    for copy in started:
        copy.start()
    return started


def by_length(length, run):
    pl.when(length <= 128)(functools.partial(run, 128))
    pl.when((length > 128) & (length <= 256))(functools.partial(run, 256))
    pl.when(length > 256)(functools.partial(run, 512))


def combos(info):
    middle = info[8]
    for rel in range(HALVES):
        for sign in range(2):
            for pos, which in enumerate((0, middle, 1)):
                block = (rel * 2 + sign) * 3 + pos
                yield block, rel * 4 + which * 2 + sign, pos % 2


def forward_kernel(info, gain_ref, table_ref, pick_ref, weight_ref, *refs):
    rows_in = refs[:10]
    parts_out = refs[10:20]
    stack_out, spec_out = refs[20:22]
    stack, normed, spec, parts, sem_in, sem_out, sem_spec = refs[22:]
    for copy in load_rows(rows_in, stack, sem_in):
        copy.wait()
    keep_copy = pltpu.make_async_copy(stack, stack_out, sem_in.at[0])
    keep_copy.start()
    model = stack.shape[2]
    odd = info[8] == 1

    def spec_copy(r, tokens):
        slot = lax.rem(r, 2)
        return pltpu.make_async_copy(
            spec.at[slot, pl.ds(0, tokens)], spec_out.at[r, pl.ds(0, tokens)], sem_spec.at[slot]
        )

    def row(r, carry):
        slot = lax.rem(r, 2)

        @pl.when(r >= 2)
        def _():
            by_length(info[r - 2], lambda tokens: spec_copy(r - 2, tokens).wait())

        def run(tokens):
            x = stack[r, pl.ds(0, tokens)].astype(F32) * gain_ref[...]
            left, right = x[:, :BLOCK].astype(BF), x[:, BLOCK:].astype(BF)
            normed[pl.ds(0, tokens), :BLOCK] = jnp.where(odd, right, left)
            normed[pl.ds(0, tokens), BLOCK:] = jnp.where(odd, left, right)
            first = min(tokens, BLOCK)
            for block, table, side in combos(info):
                cols = pl.ds(side * BLOCK, BLOCK)
                into = pl.ds(block * BLOCK, BLOCK)
                spec[slot, pl.ds(0, first), into] = dot(
                    table_ref[table, pl.ds(0, first), pl.ds(BLOCK, first)],
                    normed[pl.ds(0, first), cols],
                ).astype(BF)
                if tokens > BLOCK:
                    spec[slot, pl.ds(BLOCK, BLOCK), into] = dot(
                        table_ref[table], normed[:, cols]
                    ).astype(BF)
            lagged = None
            for lag in range(LAGS):
                moved = dot(normed[pl.ds(0, tokens)], pick_ref[lag])
                if lag:
                    moved = jnp.concatenate(
                        [jnp.zeros((lag, BLOCK), F32), moved[: tokens - lag]], axis=0
                    )
                lagged = moved if lagged is None else lagged + moved
            spec[slot, pl.ds(0, tokens), pl.ds(12 * BLOCK, BLOCK)] = lagged.astype(BF)
            spec_copy(r, tokens).start()
            for start in range(0, tokens, BLOCK):
                size = min(BLOCK, tokens)
                parts[r, pl.ds(start, size)] = dot(
                    spec[slot, pl.ds(start, size)], weight_ref[...]
                ).astype(BF)
            if tokens < parts.shape[1]:
                rest = parts.shape[1] - tokens
                parts[r, pl.ds(tokens, rest)] = jnp.zeros((rest, model), BF)

        by_length(info[r], run)
        return carry

    lax.fori_loop(0, MEMBERS, row, 0)
    stored = store_rows(parts, parts_out, sem_out)
    for r in (MEMBERS - 2, MEMBERS - 1):
        by_length(info[r], lambda tokens, r=r: spec_copy(r, tokens).wait())
    keep_copy.wait()
    for copy in stored:
        copy.wait()


def row_shapes(seq_len, model):
    whole = jax.ShapeDtypeStruct((seq_len, model), BF)
    half = jax.ShapeDtypeStruct((seq_len // 2, model), BF)
    return (whole,) * 6 + (half,) * 4


def forward_call(info, gain, table, pick, weight, rows):
    seq_len, model = rows[0].shape
    features = weight.shape[0]
    outs = pl.pallas_call(
        forward_kernel,
        out_shape=row_shapes(seq_len, model)
        + (
            jax.ShapeDtypeStruct((MEMBERS, seq_len, model), BF),
            jax.ShapeDtypeStruct((MEMBERS, seq_len, features), BF),
        ),
        in_specs=[SM, VM, VM, VM, VM] + [ANY] * 10,
        out_specs=(ANY,) * 12,
        scratch_shapes=[
            pltpu.VMEM((MEMBERS, seq_len, model), BF),
            pltpu.VMEM((seq_len, model), BF),
            pltpu.VMEM((2, seq_len, features), BF),
            pltpu.VMEM((MEMBERS, seq_len, model), BF),
            pltpu.SemaphoreType.DMA((10,)),
            pltpu.SemaphoreType.DMA((10,)),
            pltpu.SemaphoreType.DMA((2,)),
        ],
        compiler_params=pltpu.CompilerParams(vmem_limit_bytes=VMEM_LIMIT),
        cost_estimate=pl.CostEstimate(
            flops=12_000_000_000, bytes_accessed=40_000_000, transcendentals=0
        ),
    )(info, gain, table, pick, weight, *rows)
    return outs[:10], outs[10], outs[11]


def backward_kernel(info, table_ref, pick_ref, weight_ref, *refs):
    rows_in = refs[:10]
    stack_in, spec_in = refs[10:12]
    parts_out = refs[12:22]
    grad_out, gain_out = refs[22:24]
    stack, d_mix, spec, d_spec, parts, total, sem_in, sem_out, sem_spec, sem_stack = refs[24:]
    loads = load_rows(rows_in, d_mix, sem_in)
    stack_copy = pltpu.make_async_copy(stack_in, stack, sem_stack)
    stack_copy.start()
    model = stack.shape[2]
    features = spec.shape[2]
    odd = info[8] == 1

    def spec_copy(r, tokens):
        slot = lax.rem(r, 2)
        return pltpu.make_async_copy(
            spec_in.at[r, pl.ds(0, tokens)], spec.at[slot, pl.ds(0, tokens)], sem_spec.at[slot]
        )

    by_length(info[0], lambda tokens: spec_copy(0, tokens).start())
    total[...] = jnp.zeros_like(total)
    gain_out[...] = jnp.zeros_like(gain_out)
    for copy in loads:
        copy.wait()
    stack_copy.wait()

    def row(r, carry):
        slot = lax.rem(r, 2)

        @pl.when(r + 1 < MEMBERS)
        def _():
            by_length(info[r + 1], lambda tokens: spec_copy(r + 1, tokens).start())

        def run(tokens):
            spec_copy(r, tokens).wait()
            here = pl.ds(0, tokens)
            dm = d_mix[r, here]
            dm_t = jnp.transpose(dm.astype(F32)).astype(BF)
            for block in range(features // BLOCK):
                cols = pl.ds(block * BLOCK, BLOCK)
                total[:, cols] += dot(dm_t, spec[slot, here, cols])
            for block in range(features // BLOCK):
                cols = pl.ds(block * BLOCK, BLOCK)
                d_spec[here, cols] = dot_nt(dm, weight_ref[cols]).astype(BF)
            first = min(tokens, BLOCK)
            sides = [[None, None], [None, None]]
            for block, table, side in combos(info):
                cols = pl.ds(block * BLOCK, BLOCK)
                term = dot(
                    table_ref[table, pl.ds(0, first), here], d_spec[here, cols]
                )
                sides[side][0] = term if sides[side][0] is None else sides[side][0] + term
                if tokens > BLOCK:
                    term = dot(
                        table_ref[table, :, pl.ds(0, BLOCK)], d_spec[pl.ds(BLOCK, BLOCK), cols]
                    )
                    sides[side][1] = term if sides[side][1] is None else sides[side][1] + term
            d_lag = d_spec[here, pl.ds(12 * BLOCK, BLOCK)]
            back = None
            for lag in range(LAGS):
                moved = dot_nt(d_lag, pick_ref[lag])
                if lag:
                    moved = jnp.concatenate(
                        [moved[lag:], jnp.zeros((lag, model), F32)], axis=0
                    )
                back = moved if back is None else back + moved
            for start in range(0, tokens, BLOCK):
                size = min(BLOCK, tokens)
                k = start // BLOCK
                at = pl.ds(start, size)
                d_a = sides[0][k] + back[start : start + size, :BLOCK]
                d_b = sides[1][k] + back[start : start + size, BLOCK:]
                left, right = jnp.where(odd, d_b, d_a), jnp.where(odd, d_a, d_b)
                x = stack[r, at].astype(F32)
                gain_out[0:1, :BLOCK] += jnp.sum(left * x[:, :BLOCK], axis=0, keepdims=True)
                gain_out[0:1, BLOCK:] += jnp.sum(right * x[:, BLOCK:], axis=0, keepdims=True)
                parts[r, at, :BLOCK] = left.astype(BF)
                parts[r, at, BLOCK:] = right.astype(BF)
            if tokens < parts.shape[1]:
                rest = parts.shape[1] - tokens
                parts[r, pl.ds(tokens, rest)] = jnp.zeros((rest, model), BF)

        by_length(info[r], run)
        return carry

    lax.fori_loop(0, MEMBERS, row, 0)
    stored = store_rows(parts, parts_out, sem_out)
    for block in range(features // BLOCK):
        cols = pl.ds(block * BLOCK, BLOCK)
        grad_out[cols] = jnp.transpose(total[:, cols]).astype(BF)
    for copy in stored:
        copy.wait()


def backward_call(info, table, pick, weight, rows, stack, spec):
    seq_len, model = rows[0].shape
    features = weight.shape[0]
    outs = pl.pallas_call(
        backward_kernel,
        out_shape=row_shapes(seq_len, model)
        + (
            jax.ShapeDtypeStruct((features, model), BF),
            jax.ShapeDtypeStruct((8, model), F32),
        ),
        in_specs=[SM, VM, VM, VM] + [ANY] * 12,
        out_specs=(ANY,) * 10 + (VM, VM),
        scratch_shapes=[
            pltpu.VMEM((MEMBERS, seq_len, model), BF),
            pltpu.VMEM((MEMBERS, seq_len, model), BF),
            pltpu.VMEM((2, seq_len, features), BF),
            pltpu.VMEM((seq_len, features), BF),
            pltpu.VMEM((MEMBERS, seq_len, model), BF),
            pltpu.VMEM((model, features), F32),
            pltpu.SemaphoreType.DMA((10,)),
            pltpu.SemaphoreType.DMA((10,)),
            pltpu.SemaphoreType.DMA((2,)),
            pltpu.SemaphoreType.DMA,
        ],
        compiler_params=pltpu.CompilerParams(vmem_limit_bytes=VMEM_LIMIT),
        cost_estimate=pl.CostEstimate(
            flops=20_000_000_000, bytes_accessed=40_000_000, transcendentals=0
        ),
    )(info, table, pick, weight, *rows, stack, spec)
    return outs[:10], outs[10], outs[11]


def body(
    inputs,
    cotangent,
    lengths,
    filters,
    gain_first,
    mix_plus,
    mix_minus,
    auto_weight,
    gain_second,
    w_gate,
    w_upward,
    w_down,
):
    _, seq_len, model = inputs.shape
    size_l = lax.axis_size("l")
    n = HALVES * MEMBERS * size_l
    h, m, l = lax.axis_index("h"), lax.axis_index("m"), lax.axis_index("l")
    me = (h * MEMBERS + m) * size_l + l
    own = gain_first.shape[0]
    hidden_size = w_gate.shape[1]

    line = jnp.concatenate(
        [
            gain_first.astype(BF).astype(F32),
            gain_second.astype(BF).astype(F32),
            lengths.astype(F32),
            jnp.zeros((128 - 2 * own - 1,), F32),
        ]
    )
    mine = lax.broadcasted_iota(jnp.int32, (n, 1), 0) == me
    small = sum_all(jnp.where(mine, line[None, :], 0.0))
    gain_one = small[:, :own].reshape(1, model)
    gain_two = small[:, own : 2 * own].reshape(1, model)
    all_lengths = small[:, 2 * own].astype(jnp.int32)
    others = (h * MEMBERS + (m ^ lax.iota(jnp.int32, MEMBERS))) * size_l + l
    info = jnp.concatenate([jnp.take(all_lengths, others), jnp.stack([m % 2])])

    x = inputs[0]
    scale_one = rms_scale(x)
    pre_one = x * scale_one
    rows = group_gather(pre_one.astype(BF))

    def both(part):
        return (part, flip(part, "h", 1))

    plus = [gather_l(part) for part in both(mix_plus.astype(BF))]
    minus = [gather_l(part) for part in both(mix_minus.astype(BF))]
    auto = [gather_l(part) for part in both(auto_weight.astype(BF))]
    lag_rows = auto[0].shape[0]
    pad = jnp.zeros((BLOCK - 2 * lag_rows, model), BF)
    weight = jnp.concatenate([plus[0], minus[0], plus[1], minus[1], auto[0], auto[1], pad], axis=0)

    col = lax.broadcasted_iota(jnp.int32, (LAGS, model, BLOCK), 2)
    feature = lax.broadcasted_iota(jnp.int32, (LAGS, model, BLOCK), 1)
    feature = (feature + (m % 2) * BLOCK) % model
    lag = lax.broadcasted_iota(jnp.int32, (LAGS, model, BLOCK), 0)
    rel = col // lag_rows
    source = lag_rows * (MEMBERS * (h ^ rel) + m) + col % lag_rows
    pick = ((rel < 2) & (source == lag * model + feature)).astype(BF)

    fwd_table, bwd_table = build_tables(filters, h, m)
    parts, stack, spec = forward_call(info, gain_one, fwd_table, pick, weight, rows)
    mixed = group_scatter(parts)

    packed = jnp.concatenate(
        [w_gate.astype(BF), w_upward.astype(BF), w_down.astype(BF).reshape(own, hidden_size)],
        axis=1,
    )
    packed = lax.all_gather(packed, ALL, axis=0, tiled=True)
    gate_b = packed[:, :hidden_size]
    upward_b = packed[:, hidden_size : 2 * hidden_size]
    down_b = packed[:, 2 * hidden_size :].reshape(hidden_size, model)

    keep = lax.broadcasted_iota(jnp.int32, (seq_len, 1), 0) < lengths[0]
    middle = x + mixed
    scale_two = rms_scale(middle)
    pre_two = middle * scale_two
    normed_two = (pre_two * gain_two).astype(BF)
    gate_pre = dot(normed_two, gate_b)
    upward = dot(normed_two, upward_b)
    activated, gelu_pull = jax.vjp(jax.nn.gelu, gate_pre)
    hidden = (activated * upward).astype(BF)
    d_out = jnp.where(keep, cotangent[0], 0.0)
    d_out_b = d_out.astype(BF)
    d_hidden = dot_nt(d_out_b, down_b)
    d_gate = gelu_pull(d_hidden * upward)[0].astype(BF)
    d_up = (d_hidden * activated).astype(BF)
    d_normed_two = dot_nt(d_gate, gate_b) + dot_nt(d_up, upward_b)
    d_middle = d_out + rms_back(middle, scale_two, d_normed_two * gain_two)
    d_rows = group_gather(d_middle.astype(BF))

    output = jnp.where(keep, middle + dot(hidden, down_b), 0.0)
    grad_down = jnp.einsum("na,nb->ab", hidden, d_out_b, preferred_element_type=F32).astype(BF)
    grad_gate = jnp.einsum("na,nb->ab", normed_two, d_gate, preferred_element_type=F32).astype(BF)
    grad_up = jnp.einsum("na,nb->ab", normed_two, d_up, preferred_element_type=F32).astype(BF)
    grad_gain_two = jnp.sum(d_normed_two * pre_two, axis=0, keepdims=True)
    grad_gate = scatter_all(grad_gate, "cyzlh")
    grad_up = scatter_all(grad_up, "czlyh")
    grad_down = scatter_all(grad_down, "clyzh")

    d_parts, grad_mix, grad_gain_one = backward_call(
        info, bwd_table, pick, weight, d_rows, stack, spec
    )
    d_normed = group_scatter(d_parts)
    input_grad = d_middle + rms_back(x, scale_one, d_normed * gain_one)

    gains = sum_all(jnp.concatenate([grad_gain_one[0:1], grad_gain_two], axis=0))
    gains = lax.dynamic_slice_in_dim(gains, me * own, own, 1)

    mix_rows = plus[0].shape[0]
    branches = grad_mix[: 4 * mix_rows].reshape(HALVES, 2, mix_rows, model)
    lag_grads = grad_mix[4 * mix_rows : 4 * mix_rows + 2 * lag_rows].reshape(
        HALVES, lag_rows, model
    )
    far = scatter_l(branches[1], 1).astype(BF)
    lag_far = scatter_l(lag_grads[1], 0).astype(BF)
    near = scatter_l(branches[0], 1)
    lag_near = scatter_l(lag_grads[0], 0)
    near = near + flip(far, "h", 1).astype(F32)
    grad_auto = lag_near + flip(lag_far, "h", 1).astype(F32)

    return (
        output[None],
        input_grad[None],
        gains[0],
        near[0],
        near[1],
        grad_auto,
        gains[1],
        grad_gate,
        grad_up,
        grad_down,
    )


def solution(mesh):
    shape = (HALVES, MEMBERS, mesh.size // (HALVES * MEMBERS))
    inner = Mesh(mesh.devices.reshape(shape), ALL)
    row, vec, mat = P(ALL, None, None), P(ALL), P(ALL, None)
    in_specs = (row, row, vec, P(), vec, mat, mat, mat, vec, mat, mat, mat)
    out_specs = (row, row, vec, mat, mat, mat, vec, mat, mat, mat)
    return jax.shard_map(body, mesh=inner, in_specs=in_specs, out_specs=out_specs, check_vma=False)
```

```python
import functools

import jax
import jax.numpy as jnp
from jax import lax
from jax.experimental import pallas as pl
from jax.experimental.pallas import tpu as pltpu
from jax.sharding import Mesh, PartitionSpec as P

EPSILON = 1e-05
MEMBERS = 8
HALVES = 2
BLOCK = 256
LAGS = 3
VMEM_LIMIT = 60 * 1024 * 1024
BF = jnp.bfloat16
F32 = jnp.float32
ALL = ("h", "m", "l")
ANY = pl.BlockSpec(memory_space=pl.ANY)
VM = pl.BlockSpec(memory_space=pltpu.VMEM)
SM = pl.BlockSpec(memory_space=pltpu.SMEM)


def rms_scale(values):
    return lax.rsqrt(jnp.mean(values * values, axis=-1, keepdims=True) + EPSILON)


def rms_back(values, scale, d_pre):
    return scale * d_pre - values * (scale * scale * scale) * jnp.mean(
        d_pre * values, axis=-1, keepdims=True
    )


def flip(x, axis, bit):
    size = lax.axis_size(axis)
    return lax.ppermute(x, axis, [(i, i ^ bit) for i in range(size)])


def after(x, *earlier):
    return lax.optimization_barrier((x, earlier))[0]


def dot(a, b):
    return jnp.dot(a, b, preferred_element_type=F32)


def dot_nt(a, b):
    return lax.dot_general(a, b, (((1,), (1,)), ((), ())), preferred_element_type=F32)


def arrays_of(value):
    if hasattr(value, "__dict__"):
        return {k: v for k, v in vars(value).items() if not isinstance(v, (int, str))}
    if isinstance(value, (list, tuple)):
        return [arrays_of(v) for v in value]
    return value


def with_arrays(value, arrays):
    if hasattr(value, "__dict__"):
        fresh = object.__new__(type(value))
        fresh.__dict__.update(vars(value))
        fresh.__dict__.update(arrays)
        return fresh
    if isinstance(value, (list, tuple)):
        return type(value)(with_arrays(v, a) for v, a in zip(value, arrays))
    return arrays


def sync(*values):
    return lax.optimization_barrier(values)


def sync_all(*values):
    leaves, tree = jax.tree.flatten([arrays_of(v) for v in values])
    kept = [k for k, leaf in enumerate(leaves) if isinstance(leaf, jax.Array)]
    for k, new in zip(kept, lax.optimization_barrier([leaves[k] for k in kept])):
        leaves[k] = new
    fresh = jax.tree.unflatten(tree, leaves)
    return tuple(with_arrays(v, a) for v, a in zip(values, fresh))


class Gather:
    def __init__(self, row):
        self.row = row
        self.half = row.shape[0] // 2

    def first(self, core=True):
        self.near1, self.near2 = flip(self.row, "m", 2), flip(self.row, "m", 4)
        if core:
            self.core0 = flip(self.row, "m", 1)

    def second(self, core=True):
        self.top = flip(self.near2[: self.half], "m", 2)
        self.low = flip(self.near1[self.half :], "m", 4)
        if core:
            self.core1, self.core2 = flip(self.near1, "m", 1), flip(self.near2, "m", 1)

    def third(self, core=True):
        self.core_top, self.core_low = flip(self.top, "m", 1), flip(self.low, "m", 1)
        if not core:
            self.core0 = flip(self.row, "m", 1)
            self.core1, self.core2 = flip(self.near1, "m", 1), flip(self.near2, "m", 1)

    def result(self):
        return (
            self.row,
            self.core0,
            self.near1,
            self.core1,
            self.near2,
            self.core2,
            self.top,
            self.low,
            self.core_top,
            self.core_low,
        )


class Reduce:
    def __init__(self, parts):
        self.parts = parts
        self.half = parts[0].shape[0] // 2

    def first(self):
        own, core0, near1, core1, near2, core2, top, low, core_top, core_low = self.parts
        self.own = own.astype(F32) + flip(core0, "m", 1).astype(F32)
        self.near1 = near1.astype(F32) + flip(core1, "m", 1).astype(F32)
        self.near2 = near2.astype(F32) + flip(core2, "m", 1).astype(F32)
        self.top = (top.astype(F32) + flip(core_top, "m", 1).astype(F32)).astype(BF)
        self.low = (low.astype(F32) + flip(core_low, "m", 1).astype(F32)).astype(BF)

    def second(self):
        half = self.half
        got_top = flip(self.top, "m", 2).astype(F32)
        got_low = flip(self.low, "m", 4).astype(F32)
        near1, near2 = self.near1, self.near2
        self.near1 = jnp.concatenate([near1[:half], near1[half:] + got_low], axis=0).astype(BF)
        self.near2 = jnp.concatenate([near2[:half] + got_top, near2[half:]], axis=0).astype(BF)

    def third(self):
        got1, got2 = flip(self.near1, "m", 2), flip(self.near2, "m", 4)
        return self.own + got1.astype(F32) + got2.astype(F32)


def gather_l(x):
    size = lax.axis_size("l")
    if size != 2:
        return lax.all_gather(x, "l", axis=0, tiled=True)
    peer = flip(x, "l", 1)
    first = lax.axis_index("l") == 0
    return jnp.concatenate([jnp.where(first, x, peer), jnp.where(first, peer, x)], axis=0)


def scatter_l(x, axis):
    size = lax.axis_size("l")
    if size != 2:
        return lax.psum_scatter(x.astype(F32), "l", scatter_dimension=axis, tiled=True)
    part = x.shape[axis] // 2
    mine = lax.axis_index("l")
    kept = lax.dynamic_slice_in_dim(x, mine * part, part, axis)
    sent = lax.dynamic_slice_in_dim(x, (1 - mine) * part, part, axis)
    return kept.astype(F32) + flip(sent.astype(BF), "l", 1).astype(F32)


def split_bit(x, axis_name, bit, axis, mine):
    kept = lax.dynamic_index_in_dim(x, mine, axis, keepdims=False)
    sent = lax.dynamic_index_in_dim(x, 1 - mine, axis, keepdims=False)
    return (kept.astype(F32) + flip(sent, axis_name, bit).astype(F32)).astype(BF)


class Scatter:
    def __init__(self, value, order):
        size_l = lax.axis_size("l")
        self.rows = value.shape[0] // (HALVES * MEMBERS * size_l)
        self.tail = value.shape[1:]
        self.value = value.reshape((2, 2, 2, 2, size_l, self.rows) + self.tail)
        self.names = ["h", "z", "y", "c", "l"]
        self.order = list(order)

    def step(self):
        what = self.order.pop(0)
        at = self.names.index(what)
        self.names.remove(what)
        if what == "h":
            self.value = split_bit(self.value, "h", 1, at, lax.axis_index("h"))
        elif what == "l" and lax.axis_size("l") != 2:
            self.value = lax.psum_scatter(
                self.value.astype(F32), "l", scatter_dimension=at, tiled=False
            ).astype(BF)
        elif what == "l":
            self.value = split_bit(self.value, "l", 1, at, lax.axis_index("l"))
        else:
            shift = "cyz".index(what)
            mine = (lax.axis_index("m") >> shift) & 1
            self.value = split_bit(self.value, "m", 1 << shift, at, mine)

    def result(self):
        return self.value.reshape((self.rows,) + self.tail).astype(F32)


def sum_direct(x, axes, bits):
    total = x
    size = 1
    for axis in axes:
        size *= lax.axis_size(axis)
    for mask in range(1, size):
        if mask & ~bits == 0:
            total = total + lax.ppermute(x, axes, [(i, i ^ mask) for i in range(size)])
    return total


def sum_peers(x):
    size = HALVES * lax.axis_size("l")
    if size == 4:
        return sum_direct(x, ("h", "l"), 3)
    step = 1
    while step < size:
        x = x + lax.ppermute(x, ("h", "l"), [(i, i ^ step) for i in range(size)])
        step *= 2
    return x


def tables_kernel(base_ref, fwd_ref, bwd_ref):
    rows, width = fwd_ref.shape[1], fwd_ref.shape[2]
    span = base_ref.shape[1]
    odd = (
        lax.broadcasted_iota(jnp.int32, (rows, width), 0)
        + lax.broadcasted_iota(jnp.int32, (rows, width), 1)
    ) % 2
    sign = (1 - 2 * odd).astype(F32)
    for index in range(4):
        for which, out in ((0, fwd_ref), (1, bwd_ref)):
            line = jnp.broadcast_to(base_ref[pl.ds(which * 4 + index, 1), :], (rows, span))
            rolled = pltpu.roll(line, 0, 1, stride=1, stride_axis=0)[:, :width]
            out[2 * index] = rolled.astype(BF)
            out[2 * index + 1] = (rolled * sign).astype(BF)


def build_tables(filters, h, m):
    seq_len, count = filters.shape
    phi = jnp.transpose(filters.astype(BF).astype(F32))
    zeros = jnp.zeros((count, BLOCK), F32)
    bwd = jnp.concatenate([phi, zeros], axis=1)
    back = jnp.flip(phi, axis=1)
    fwd = jnp.concatenate(
        [
            back[:, seq_len - 1 - BLOCK :],
            jnp.zeros((count, BLOCK), F32),
            back[:, : seq_len - 1 - BLOCK],
        ],
        axis=1,
    )
    rows = []
    for table in (fwd, bwd):
        for rel in range(HALVES):
            first = 12 * (h ^ rel) + (3 * m) // 2
            rows.append(lax.dynamic_slice_in_dim(table, first, 2, 0))
    base = jnp.concatenate(rows, axis=0)
    shape = jax.ShapeDtypeStruct((8, BLOCK, seq_len), BF)
    return pl.pallas_call(
        tables_kernel,
        out_shape=(shape, shape),
        in_specs=[VM],
        out_specs=(VM, VM),
        compiler_params=pltpu.CompilerParams(vmem_limit_bytes=VMEM_LIMIT),
        cost_estimate=pl.CostEstimate(flops=20_000_000, bytes_accessed=5_000_000, transcendentals=0),
    )(base)


def load_rows(refs, scratch, sem):
    half = scratch.shape[1] // 2
    copies = []
    for j in range(6):
        copies.append((refs[j], scratch.at[j]))
    for j in (6, 7):
        copies.append((refs[2 * j - 6], scratch.at[j, pl.ds(0, half)]))
        copies.append((refs[2 * j - 5], scratch.at[j, pl.ds(half, half)]))
    started = [pltpu.make_async_copy(a, b, sem.at[k]) for k, (a, b) in enumerate(copies)]
    for copy in started:
        copy.start()
    return started


def store_rows(scratch, refs, sem):
    half = scratch.shape[1] // 2
    copies = []
    for j in range(6):
        copies.append((scratch.at[j], refs[j]))
    for j in (6, 7):
        copies.append((scratch.at[j, pl.ds(0, half)], refs[2 * j - 6]))
        copies.append((scratch.at[j, pl.ds(half, half)], refs[2 * j - 5]))
    started = [pltpu.make_async_copy(a, b, sem.at[k]) for k, (a, b) in enumerate(copies)]
    for copy in started:
        copy.start()
    return started


def by_length(length, run):
    pl.when(length <= 128)(functools.partial(run, 128))
    pl.when((length > 128) & (length <= 256))(functools.partial(run, 256))
    pl.when(length > 256)(functools.partial(run, 512))


def combos(info):
    middle = info[8]
    for rel in range(HALVES):
        for sign in range(2):
            for pos, which in enumerate((0, middle, 1)):
                block = (rel * 2 + sign) * 3 + pos
                yield block, rel * 4 + which * 2 + sign, pos % 2


def conv_kernel(info, gain_ref, table_ref, pick_ref, *refs):
    rows_in = refs[:10]
    stack_out, spec_out = refs[10:12]
    stack, normed, spec, sem_in, sem_spec = refs[12:]
    for copy in load_rows(rows_in, stack, sem_in):
        copy.wait()
    keep_copy = pltpu.make_async_copy(stack, stack_out, sem_in.at[0])
    keep_copy.start()
    odd = info[8] == 1

    def spec_copy(r, tokens):
        slot = lax.rem(r, 2)
        return pltpu.make_async_copy(
            spec.at[slot, pl.ds(0, tokens)], spec_out.at[r, pl.ds(0, tokens)], sem_spec.at[slot]
        )

    def row(r, carry):
        slot = lax.rem(r, 2)

        @pl.when(r >= 2)
        def _():
            by_length(info[r - 2], lambda tokens: spec_copy(r - 2, tokens).wait())

        def run(tokens):
            x = stack[r, pl.ds(0, tokens)].astype(F32) * gain_ref[...]
            left, right = x[:, :BLOCK].astype(BF), x[:, BLOCK:].astype(BF)
            normed[pl.ds(0, tokens), :BLOCK] = jnp.where(odd, right, left)
            normed[pl.ds(0, tokens), BLOCK:] = jnp.where(odd, left, right)
            first = min(tokens, BLOCK)
            for block, table, side in combos(info):
                cols = pl.ds(side * BLOCK, BLOCK)
                into = pl.ds(block * BLOCK, BLOCK)
                spec[slot, pl.ds(0, first), into] = dot(
                    table_ref[table, pl.ds(0, first), pl.ds(BLOCK, first)],
                    normed[pl.ds(0, first), cols],
                ).astype(BF)
                if tokens > BLOCK:
                    spec[slot, pl.ds(BLOCK, BLOCK), into] = dot(
                        table_ref[table], normed[:, cols]
                    ).astype(BF)
            lagged = None
            for lag in range(LAGS):
                moved = dot(normed[pl.ds(0, tokens)], pick_ref[lag])
                if lag:
                    moved = jnp.concatenate(
                        [jnp.zeros((lag, BLOCK), F32), moved[: tokens - lag]], axis=0
                    )
                lagged = moved if lagged is None else lagged + moved
            spec[slot, pl.ds(0, tokens), pl.ds(12 * BLOCK, BLOCK)] = lagged.astype(BF)
            spec_copy(r, tokens).start()

        by_length(info[r], run)
        return carry

    lax.fori_loop(0, MEMBERS, row, 0)
    for r in (MEMBERS - 2, MEMBERS - 1):
        by_length(info[r], lambda tokens, r=r: spec_copy(r, tokens).wait())
    keep_copy.wait()


def row_shapes(seq_len, model):
    whole = jax.ShapeDtypeStruct((seq_len, model), BF)
    half = jax.ShapeDtypeStruct((seq_len // 2, model), BF)
    return (whole,) * 6 + (half,) * 4


def params(flops, data):
    return dict(
        compiler_params=pltpu.CompilerParams(vmem_limit_bytes=VMEM_LIMIT),
        cost_estimate=pl.CostEstimate(flops=flops, bytes_accessed=data, transcendentals=0),
    )


def conv_call(info, gain, table, pick, rows):
    seq_len, model = rows[0].shape
    features = 13 * BLOCK
    return pl.pallas_call(
        conv_kernel,
        out_shape=(
            jax.ShapeDtypeStruct((MEMBERS, seq_len, model), BF),
            jax.ShapeDtypeStruct((MEMBERS, seq_len, features), BF),
        ),
        in_specs=[SM, VM, VM, VM] + [ANY] * 10,
        out_specs=(ANY,) * 2,
        scratch_shapes=[
            pltpu.VMEM((MEMBERS, seq_len, model), BF),
            pltpu.VMEM((seq_len, model), BF),
            pltpu.VMEM((2, seq_len, features), BF),
            pltpu.SemaphoreType.DMA((10,)),
            pltpu.SemaphoreType.DMA((2,)),
        ],
        **params(5_000_000_000, 20_000_000),
    )(info, gain, table, pick, *rows)


def mix_kernel(info, lag_ref, spec_in, shares, *refs):
    parts_out = refs[:10]
    weight_out = refs[10]
    weight, spec, parts, sem_in, sem_out, sem_spec = refs[11:]
    features, model = weight.shape
    _, size_l, share_rows, _ = shares.shape
    rows = 3 * BLOCK // size_l
    copies = []
    for rel in range(HALVES):
        for k in range(2):
            for l in range(size_l):
                copies.append(
                    pltpu.make_async_copy(
                        shares.at[info[17] ^ rel, l, pl.ds(k * rows, rows)],
                        weight.at[pl.ds((rel * 2 + k) * 3 * BLOCK + l * rows, rows)],
                        sem_in.at[(rel * 2 + k) * size_l + l],
                    )
                )
    for copy in copies:
        copy.start()
    weight[pl.ds(12 * BLOCK, BLOCK)] = lag_ref[...]

    def spec_copy(r, tokens):
        slot = lax.rem(r, 2)
        return pltpu.make_async_copy(
            spec_in.at[r, pl.ds(0, tokens)], spec.at[slot, pl.ds(0, tokens)], sem_spec.at[slot]
        )

    by_length(info[0], lambda tokens: spec_copy(0, tokens).start())
    for copy in copies:
        copy.wait()
    weight_copy = pltpu.make_async_copy(weight, weight_out, sem_in.at[0])
    weight_copy.start()

    def row(r, carry):
        slot = lax.rem(r, 2)

        @pl.when(r + 1 < MEMBERS)
        def _():
            by_length(info[r + 1], lambda tokens: spec_copy(r + 1, tokens).start())

        def run(tokens):
            spec_copy(r, tokens).wait()
            parts[r, pl.ds(0, tokens)] = dot(
                spec[slot, pl.ds(0, tokens)], weight[...]
            ).astype(BF)
            if tokens < parts.shape[1]:
                rest = parts.shape[1] - tokens
                parts[r, pl.ds(tokens, rest)] = jnp.zeros((rest, model), BF)

        by_length(info[r], run)
        return carry

    lax.fori_loop(0, MEMBERS, row, 0)
    stored = store_rows(parts, parts_out, sem_out)
    weight_copy.wait()
    for copy in stored:
        copy.wait()


def mix_call(info, lag_weight, spec, shares):
    _, seq_len, features = spec.shape
    model = shares.shape[-1]
    outs = pl.pallas_call(
        mix_kernel,
        out_shape=row_shapes(seq_len, model) + (jax.ShapeDtypeStruct((features, model), BF),),
        in_specs=[SM, VM, ANY, ANY],
        out_specs=(ANY,) * 11,
        scratch_shapes=[
            pltpu.VMEM((features, model), BF),
            pltpu.VMEM((2, seq_len, features), BF),
            pltpu.VMEM((MEMBERS, seq_len, model), BF),
            pltpu.SemaphoreType.DMA((4 * shares.shape[1],)),
            pltpu.SemaphoreType.DMA((10,)),
            pltpu.SemaphoreType.DMA((2,)),
        ],
        **params(8_000_000_000, 30_000_000),
    )(info, lag_weight, spec, shares)
    return outs[:10], outs[10]


def back_conv_kernel(info, table_ref, pick_ref, weight_ref, *refs):
    rows_in = refs[:10]
    stack_in = refs[10]
    parts_out = refs[11:21]
    gain_out = refs[21]
    stack, d_mix, d_spec, parts, sem_in, sem_out, sem_stack = refs[22:]
    loads = load_rows(rows_in, d_mix, sem_in)
    stack_copy = pltpu.make_async_copy(stack_in, stack, sem_stack)
    stack_copy.start()
    model = stack.shape[2]
    features = d_spec.shape[1]
    odd = info[8] == 1
    gain_out[...] = jnp.zeros_like(gain_out)
    for copy in loads:
        copy.wait()
    stack_copy.wait()

    def row(r, carry):
        def run(tokens):
            here = pl.ds(0, tokens)
            dm = d_mix[r, here]
            for block in range(features // BLOCK):
                cols = pl.ds(block * BLOCK, BLOCK)
                d_spec[here, cols] = dot_nt(dm, weight_ref[cols]).astype(BF)
            first = min(tokens, BLOCK)
            sides = [[None, None], [None, None]]
            for block, table, side in combos(info):
                cols = pl.ds(block * BLOCK, BLOCK)
                term = dot(table_ref[table, pl.ds(0, first), here], d_spec[here, cols])
                sides[side][0] = term if sides[side][0] is None else sides[side][0] + term
                if tokens > BLOCK:
                    term = dot(
                        table_ref[table, :, pl.ds(0, BLOCK)], d_spec[pl.ds(BLOCK, BLOCK), cols]
                    )
                    sides[side][1] = term if sides[side][1] is None else sides[side][1] + term
            d_lag = d_spec[here, pl.ds(12 * BLOCK, BLOCK)]
            back = None
            for lag in range(LAGS):
                moved = dot_nt(d_lag, pick_ref[lag])
                if lag:
                    moved = jnp.concatenate(
                        [moved[lag:], jnp.zeros((lag, model), F32)], axis=0
                    )
                back = moved if back is None else back + moved
            for start in range(0, tokens, BLOCK):
                size = min(BLOCK, tokens)
                k = start // BLOCK
                at = pl.ds(start, size)
                d_a = sides[0][k] + back[start : start + size, :BLOCK]
                d_b = sides[1][k] + back[start : start + size, BLOCK:]
                left, right = jnp.where(odd, d_b, d_a), jnp.where(odd, d_a, d_b)
                x = stack[r, at].astype(F32)
                gain_out[0:1, :BLOCK] += jnp.sum(left * x[:, :BLOCK], axis=0, keepdims=True)
                gain_out[0:1, BLOCK:] += jnp.sum(right * x[:, BLOCK:], axis=0, keepdims=True)
                parts[r, at, :BLOCK] = left.astype(BF)
                parts[r, at, BLOCK:] = right.astype(BF)
            if tokens < parts.shape[1]:
                rest = parts.shape[1] - tokens
                parts[r, pl.ds(tokens, rest)] = jnp.zeros((rest, model), BF)

        by_length(info[r], run)
        return carry

    lax.fori_loop(0, MEMBERS, row, 0)
    for copy in store_rows(parts, parts_out, sem_out):
        copy.wait()


def back_conv_call(info, table, pick, weight, rows, stack):
    seq_len, model = rows[0].shape
    features = weight.shape[0]
    outs = pl.pallas_call(
        back_conv_kernel,
        out_shape=row_shapes(seq_len, model) + (jax.ShapeDtypeStruct((8, model), F32),),
        in_specs=[SM, VM, VM, VM] + [ANY] * 11,
        out_specs=(ANY,) * 10 + (VM,),
        scratch_shapes=[
            pltpu.VMEM((MEMBERS, seq_len, model), BF),
            pltpu.VMEM((MEMBERS, seq_len, model), BF),
            pltpu.VMEM((seq_len, features), BF),
            pltpu.VMEM((MEMBERS, seq_len, model), BF),
            pltpu.SemaphoreType.DMA((10,)),
            pltpu.SemaphoreType.DMA((10,)),
            pltpu.SemaphoreType.DMA,
        ],
        **params(12_000_000_000, 20_000_000),
    )(info, table, pick, weight, *rows, stack)
    return outs[:10], outs[10]


def grad_kernel(info, spec_in, *refs):
    rows_in = refs[:10]
    grad_out, d_mix, spec, total, sem_in, sem_spec = refs[10:]
    features = total.shape[1]
    size_l = grad_out.shape[0] // HALVES
    own = 3 * BLOCK // size_l
    lags = grad_out.shape[1] - 2 * own
    loads = load_rows(rows_in, d_mix, sem_in)

    def spec_copy(r, tokens):
        slot = lax.rem(r, 2)
        return pltpu.make_async_copy(
            spec_in.at[r, pl.ds(0, tokens)], spec.at[slot, pl.ds(0, tokens)], sem_spec.at[slot]
        )

    by_length(info[0], lambda tokens: spec_copy(0, tokens).start())
    total[...] = jnp.zeros_like(total)
    for copy in loads:
        copy.wait()

    def row(r, carry):
        slot = lax.rem(r, 2)

        @pl.when(r + 1 < MEMBERS)
        def _():
            by_length(info[r + 1], lambda tokens: spec_copy(r + 1, tokens).start())

        def run(tokens):
            spec_copy(r, tokens).wait()
            here = pl.ds(0, tokens)
            dm_t = jnp.transpose(d_mix[r, here].astype(F32)).astype(BF)
            for block in range(features // BLOCK):
                cols = pl.ds(block * BLOCK, BLOCK)
                total[:, cols] += dot(dm_t, spec[slot, here, cols])

        by_length(info[r], run)
        return carry

    lax.fori_loop(0, MEMBERS, row, 0)
    for block in range(features // BLOCK):
        cols = pl.ds(block * BLOCK, BLOCK)
        value = jnp.transpose(total[:, cols]).astype(BF)
        if block < 12:
            rel, k, first = block // 6, block // 3 % 2, block % 3 * BLOCK
            base = (info[17] ^ rel) * size_l
            at = first
            while at < first + BLOCK:
                l, inside = at // own, at % own
                size = min(own - inside, first + BLOCK - at)
                grad_out[base + l, pl.ds(k * own + inside, size)] = value[
                    at - first : at - first + size
                ]
                at += size
        else:
            for rel in range(HALVES):
                base = (info[17] ^ rel) * size_l
                for l in range(size_l):
                    at = (rel * size_l + l) * lags
                    grad_out[base + l, pl.ds(2 * own, lags)] = value[at : at + lags]


def grad_call(info, spec, rows, size_l, share_rows):
    seq_len, model = rows[0].shape
    features = spec.shape[2]
    return pl.pallas_call(
        grad_kernel,
        out_shape=jax.ShapeDtypeStruct((HALVES * size_l, share_rows, model), BF),
        in_specs=[SM] + [ANY] * 11,
        out_specs=VM,
        scratch_shapes=[
            pltpu.VMEM((MEMBERS, seq_len, model), BF),
            pltpu.VMEM((2, seq_len, features), BF),
            pltpu.VMEM((model, features), F32),
            pltpu.SemaphoreType.DMA((10,)),
            pltpu.SemaphoreType.DMA((2,)),
        ],
        **params(8_000_000_000, 30_000_000),
    )(info, spec, *rows)


def mlp_kernel(info, normed_ref, d_out_ref, *refs):
    packs = refs[:10]
    hidden_out, d_gate_out, d_up_out, d_normed_out, mlp_out, gate, up, down, sem = refs[10:]
    model, inner = gate.shape
    per_h = packs[0].shape[0] // 2
    share = per_h // 3
    rows = model // (HALVES * MEMBERS)
    count = inner // model
    copies = []

    def add(source, at, h, j):
        to = info[9 + j] + h * MEMBERS
        for which, target in enumerate((gate, up)):
            for s in range(count):
                copies.append(
                    pltpu.make_async_copy(
                        source.at[pl.ds(at + which * share + s * rows, rows)],
                        target.at[
                            pl.ds(pl.multiple_of(to * rows, rows), rows), pl.ds(s * model, model)
                        ],
                        sem.at[0],
                    )
                )
        copies.append(
            pltpu.make_async_copy(
                source.at[pl.ds(at + 2 * share, share)],
                down.at[pl.ds(pl.multiple_of(to * share, share), share)],
                sem.at[0],
            )
        )

    for h in range(HALVES):
        for j in range(6):
            add(packs[j], h * per_h, h, j)
        for j in (6, 7):
            add(packs[2 * j - 6 + h], 0, h, j)
    for copy in copies:
        copy.start()
    for copy in copies:
        copy.wait()

    root, cubic = 0.7978845608028654, 0.044715
    width = 2 * BLOCK

    def step(k, carry):
        cols = pl.ds(pl.multiple_of(k * width, width), width)
        normed, d_out = normed_ref[...], d_out_ref[...]
        pre = dot(normed, gate[:, cols])
        upward = dot(normed, up[:, cols])
        square = pre * pre
        tanh = jnp.tanh(root * pre * (1.0 + cubic * square))
        half = 0.5 * (1.0 + tanh)
        slope = half + 0.5 * pre * (1.0 - tanh * tanh) * (root * (1.0 + 3.0 * cubic * square))
        active = pre * half
        hidden = (active * upward).astype(BF)
        d_hidden = dot_nt(d_out, down[cols])
        d_gate = (d_hidden * upward * slope).astype(BF)
        d_up = (d_hidden * active).astype(BF)
        hidden_out[:, cols] = hidden
        d_gate_out[:, cols] = d_gate
        d_up_out[:, cols] = d_up
        back = dot_nt(d_gate, gate[:, cols]) + dot_nt(d_up, up[:, cols])
        ahead = dot(hidden, down[cols])

        @pl.when(k == 0)
        def _():
            d_normed_out[...] = back
            mlp_out[...] = ahead

        @pl.when(k > 0)
        def _():
            d_normed_out[...] += back
            mlp_out[...] += ahead

        return carry

    lax.fori_loop(0, inner // width, step, 0)


def mlp_call(info, normed, d_out, packs, inner):
    seq_len, model = normed.shape
    wide = jax.ShapeDtypeStruct((seq_len, inner), BF)
    whole = jax.ShapeDtypeStruct((seq_len, model), F32)
    return pl.pallas_call(
        mlp_kernel,
        out_shape=(wide, wide, wide, whole, whole),
        in_specs=[SM, VM, VM] + [ANY] * 10,
        out_specs=(VM,) * 5,
        scratch_shapes=[
            pltpu.VMEM((model, inner), BF),
            pltpu.VMEM((model, inner), BF),
            pltpu.VMEM((inner, model), BF),
            pltpu.SemaphoreType.DMA((1,)),
        ],
        **params(6_500_000_000, 16_000_000),
    )(info, normed, d_out, *packs)


def body(
    inputs,
    cotangent,
    lengths,
    filters,
    gain_first,
    mix_plus,
    mix_minus,
    auto_weight,
    gain_second,
    w_gate,
    w_upward,
    w_down,
):
    _, seq_len, model = inputs.shape
    size_l = lax.axis_size("l")
    n = HALVES * MEMBERS * size_l
    h, m, l = lax.axis_index("h"), lax.axis_index("m"), lax.axis_index("l")
    me = (h * MEMBERS + m) * size_l + l
    own = gain_first.shape[0]
    inner = w_gate.shape[1]
    count = inner // model

    line = jnp.concatenate(
        [
            gain_first.astype(BF).astype(F32),
            gain_second.astype(BF).astype(F32),
            lengths.astype(F32),
            jnp.zeros((128 - 2 * own - 1,), F32),
        ]
    )
    mine = lax.broadcasted_iota(jnp.int32, (n, 1), 0) == me
    small = jnp.where(mine, line[None, :], 0.0)

    x = inputs[0]
    scale_one = rms_scale(x)
    pre_one = x * scale_one
    row = Gather(pre_one.astype(BF))
    lag_rows = auto_weight.shape[0]
    share = jnp.concatenate([mix_plus, mix_minus, auto_weight], axis=0).astype(BF)
    shares = lax.all_gather(share, ("h", "l"), axis=0)
    shares = shares.reshape((HALVES, size_l) + share.shape)

    def blocks(w):
        return jnp.transpose(w.astype(BF).reshape(own, count, model), (1, 0, 2))

    wide = jnp.concatenate([blocks(w_gate), blocks(w_upward)], axis=0).reshape(-1, model)
    wide_rows = wide.shape[0]
    pack = jnp.concatenate([wide, w_down.astype(BF)], axis=0)

    row.first()
    small = sum_peers(small)
    far_pack = flip(pack, "h", 1)
    fwd_table, bwd_table = build_tables(filters, h, m)

    small, far_pack, row, fwd_table = sync_all(small, far_pack, row, fwd_table)
    small = sum_direct(small, ("m",), 3)
    row.second()

    small, row = sync_all(small, row)
    small = sum_direct(small, ("m",), 4)
    row.third()
    pack = jnp.stack([pack, far_pack])
    pack = jnp.where(h == 0, pack, pack[::-1])
    pack = gather_l(pack[None])
    gain_one = small[:, :own].reshape(1, model)
    gain_two = small[:, own : 2 * own].reshape(1, model)
    all_lengths = small[:, 2 * own].astype(jnp.int32)
    members = m ^ lax.iota(jnp.int32, MEMBERS)
    info = jnp.concatenate(
        [
            jnp.take(all_lengths, (h * MEMBERS + members) * size_l + l),
            jnp.stack([m % 2]),
            members,
            jnp.stack([h]),
        ]
    )
    wide = pack[:, :, :wide_rows].reshape(size_l, HALVES, 2 * count, own, model)
    wide = jnp.transpose(wide, (1, 2, 0, 3, 4)).reshape(HALVES, -1, model)
    tall = jnp.transpose(pack[:, :, wide_rows:], (1, 0, 2, 3)).reshape(HALVES, -1, model)
    pack = Gather(jnp.concatenate([wide, tall], axis=1).reshape(-1, model))
    pack.first()
    col = lax.broadcasted_iota(jnp.int32, (LAGS, model, BLOCK), 2)
    feature = lax.broadcasted_iota(jnp.int32, (LAGS, model, BLOCK), 1)
    feature = (feature + (m % 2) * BLOCK) % model
    lag = lax.broadcasted_iota(jnp.int32, (LAGS, model, BLOCK), 0)
    lag_span = lag_rows * size_l
    rel = col // lag_span
    source = lag_span * (MEMBERS * (h ^ rel) + m) + col % lag_span
    pick = ((rel < 2) & (source == lag * model + feature)).astype(BF)

    stack, spec = conv_call(info, gain_one, fwd_table, pick, row.result())

    spec, stack, pack = sync_all(spec, stack, pack)
    pack.second()
    lag_weight = [
        lax.dynamic_index_in_dim(shares, h ^ rel, 0, keepdims=False)[:, -lag_rows:]
        for rel in range(HALVES)
    ]
    lag_weight = jnp.stack(lag_weight).reshape(HALVES * lag_span, model)
    lag_weight = jnp.pad(lag_weight, ((0, BLOCK - HALVES * lag_span), (0, 0)))
    parts, weight = mix_call(info, lag_weight, spec, shares)
    mixed = Reduce(parts)

    mixed, pack = sync_all(mixed, pack)
    mixed.first()
    pack.third()
    mixed, pack = sync_all(mixed, pack)
    mixed.second()
    mixed, pack = sync_all(mixed, pack)
    mixed = mixed.third()

    keep = lax.broadcasted_iota(jnp.int32, (seq_len, 1), 0) < lengths[0]
    middle = x + mixed
    scale_two = rms_scale(middle)
    pre_two = middle * scale_two
    normed_two = (pre_two * gain_two).astype(BF)
    d_out = jnp.where(keep, cotangent[0], 0.0)
    d_out_b = d_out.astype(BF)
    hidden, d_gate, d_up, d_normed_two, mlp_out = mlp_call(
        info, normed_two, d_out_b, pack.result(), inner
    )
    d_middle = d_out + rms_back(middle, scale_two, d_normed_two * gain_two)

    row = Gather(d_middle.astype(BF))
    row.first()

    row, hidden, d_gate, d_up = sync_all(row, hidden, d_gate, d_up)
    row.second()
    output = jnp.where(keep, middle + mlp_out, 0.0)
    grad_down = jnp.einsum("na,nb->ab", hidden, d_out_b, preferred_element_type=F32).astype(BF)
    grad_gate = jnp.einsum("na,nb->ab", normed_two, d_gate, preferred_element_type=F32).astype(BF)
    grad_up = jnp.einsum("na,nb->ab", normed_two, d_up, preferred_element_type=F32).astype(BF)
    grad_gain_two = jnp.sum(d_normed_two * pre_two, axis=0, keepdims=True)

    row, grad_gate, grad_up, grad_down, grad_gain_two = sync_all(
        row, grad_gate, grad_up, grad_down, grad_gain_two
    )
    row.third()
    grads = [
        Scatter(grad_gate, "cyzlh"),
        Scatter(grad_up, "czlyh"),
        Scatter(grad_down, "clyzh"),
    ]
    for grad in grads:
        grad.step()

    row, grads = sync_all(row, grads)
    d_rows = row.result()
    grad_mix = grad_call(info, spec, d_rows, size_l, share.shape[0])
    for grad in grads:
        grad.step()

    grad_mix, grads, d_rows = sync_all(grad_mix, grads, d_rows)
    grad_mix = lax.psum_scatter(grad_mix, ("h", "l"), scatter_dimension=0).astype(F32)
    for grad in grads:
        grad.step()
    d_parts, grad_gain_one = back_conv_call(info, bwd_table, pick, weight, d_rows, stack)
    d_normed = Reduce(d_parts)

    d_normed, grad_gain_one, grads = sync_all(d_normed, grad_gain_one, grads)
    gains = jnp.concatenate([grad_gain_one[0:1], grad_gain_two], axis=0)
    gains = sum_direct(gains, ("m",), 3)
    d_normed.first()
    for grad in grads:
        grad.step()

    d_normed, gains, grads = sync_all(d_normed, gains, grads)
    d_normed.second()
    gains = sum_direct(gains, ("m",), 4)
    for grad in grads:
        grad.step()

    d_normed, gains, grads = sync_all(d_normed, gains, grads)
    gains = sum_peers(gains)
    gains = lax.dynamic_slice_in_dim(gains, me * own, own, 1)
    d_normed = d_normed.third()
    input_grad = d_middle + rms_back(x, scale_one, d_normed * gain_one)
    grad_gate, grad_up, grad_down = [grad.result() for grad in grads]
    mix_rows = mix_plus.shape[0]

    return (
        output[None],
        input_grad[None],
        gains[0],
        grad_mix[:mix_rows],
        grad_mix[mix_rows : 2 * mix_rows],
        grad_mix[2 * mix_rows :],
        gains[1],
        grad_gate,
        grad_up,
        grad_down,
    )


def solution(mesh):
    shape = (HALVES, MEMBERS, mesh.size // (HALVES * MEMBERS))
    inner = Mesh(mesh.devices.reshape(shape), ALL)
    row, vec, mat = P(ALL, None, None), P(ALL), P(ALL, None)
    in_specs = (row, row, vec, P(), vec, mat, mat, mat, vec, mat, mat, mat)
    out_specs = (row, row, vec, mat, mat, mat, vec, mat, mat, mat)
    return jax.shard_map(body, mesh=inner, in_specs=in_specs, out_specs=out_specs, check_vma=False)
```

```python
import functools

import jax
import jax.numpy as jnp
from jax import lax
from jax.experimental import pallas as pl
from jax.experimental.pallas import tpu as pltpu
from jax.sharding import Mesh, PartitionSpec as P

EPSILON = 1e-05
MEMBERS = 8
HALVES = 2
BLOCK = 256
LAGS = 3
VMEM_LIMIT = 60 * 1024 * 1024
BF = jnp.bfloat16
F32 = jnp.float32
GROUP = ("z", "y", "c")
ALL = ("h",) + GROUP + ("l",)
ANY = pl.BlockSpec(memory_space=pl.ANY)
VM = pl.BlockSpec(memory_space=pltpu.VMEM)
SM = pl.BlockSpec(memory_space=pltpu.SMEM)


def rms_scale(values):
    return lax.rsqrt(jnp.mean(values * values, axis=-1, keepdims=True) + EPSILON)


def rms_back(values, scale, d_pre):
    return scale * d_pre - values * (scale * scale * scale) * jnp.mean(
        d_pre * values, axis=-1, keepdims=True
    )


def flip(x, axis, bit):
    if axis == "m":
        axis, bit = {1: "c", 2: "y", 4: "z"}[bit], 1
    size = lax.axis_size(axis)
    return lax.ppermute(x, axis, [(i, i ^ bit) for i in range(size)])


def after(x, *earlier):
    return lax.optimization_barrier((x, earlier))[0]


def dot(a, b):
    return jnp.dot(a, b, preferred_element_type=F32)


def dot_nt(a, b):
    return lax.dot_general(a, b, (((1,), (1,)), ((), ())), preferred_element_type=F32)


def arrays_of(value):
    if hasattr(value, "__dict__"):
        return {k: v for k, v in vars(value).items() if not isinstance(v, (int, str))}
    if isinstance(value, (list, tuple)):
        return [arrays_of(v) for v in value]
    return value


def with_arrays(value, arrays):
    if hasattr(value, "__dict__"):
        fresh = object.__new__(type(value))
        fresh.__dict__.update(vars(value))
        fresh.__dict__.update(arrays)
        return fresh
    if isinstance(value, (list, tuple)):
        return type(value)(with_arrays(v, a) for v, a in zip(value, arrays))
    return arrays


def sync(*values):
    return lax.optimization_barrier(values)


def sync_all(*values):
    leaves, tree = jax.tree.flatten([arrays_of(v) for v in values])
    kept = [k for k, leaf in enumerate(leaves) if isinstance(leaf, jax.Array)]
    for k, new in zip(kept, lax.optimization_barrier([leaves[k] for k in kept])):
        leaves[k] = new
    fresh = jax.tree.unflatten(tree, leaves)
    return tuple(with_arrays(v, a) for v, a in zip(values, fresh))


class Gather:
    def __init__(self, row):
        self.row = row
        self.half = row.shape[0] // 2

    def first(self):
        self.near1, self.near2 = flip(self.row, "m", 2), flip(self.row, "m", 4)
        self.core0 = flip(self.row, "m", 1)

    def second(self, core=True):
        self.top = flip(self.near2[: self.half], "m", 2)
        self.low = flip(self.near1[self.half :], "m", 4)
        if core:
            self.core1, self.core2 = flip(self.near1, "m", 1), flip(self.near2, "m", 1)

    def third(self):
        self.core_top, self.core_low = flip(self.top, "m", 1), flip(self.low, "m", 1)

    def result(self):
        return (
            self.row,
            self.core0,
            self.near1,
            self.core1,
            self.near2,
            self.core2,
            self.top,
            self.low,
            self.core_top,
            self.core_low,
        )


class Reduce:
    def __init__(self, parts):
        self.parts = parts
        self.half = parts[0].shape[0] // 2

    def first(self):
        own, core0, near1, core1, near2, core2, top, low, core_top, core_low = self.parts
        self.own = own.astype(F32) + flip(core0, "m", 1).astype(F32)
        self.near1 = near1.astype(F32) + flip(core1, "m", 1).astype(F32)
        self.near2 = near2.astype(F32) + flip(core2, "m", 1).astype(F32)
        self.top = (top.astype(F32) + flip(core_top, "m", 1).astype(F32)).astype(BF)
        self.low = (low.astype(F32) + flip(core_low, "m", 1).astype(F32)).astype(BF)

    def second(self):
        half = self.half
        got_top = flip(self.top, "m", 2).astype(F32)
        got_low = flip(self.low, "m", 4).astype(F32)
        near1, near2 = self.near1, self.near2
        self.near1 = jnp.concatenate([near1[:half], near1[half:] + got_low], axis=0).astype(BF)
        self.near2 = jnp.concatenate([near2[:half] + got_top, near2[half:]], axis=0).astype(BF)

    def third(self):
        got1, got2 = flip(self.near1, "m", 2), flip(self.near2, "m", 4)
        return self.own + got1.astype(F32) + got2.astype(F32)


def gather_l(x):
    size = lax.axis_size("l")
    if size != 2:
        return lax.all_gather(x, "l", axis=0, tiled=True)
    peer = flip(x, "l", 1)
    first = lax.axis_index("l") == 0
    return jnp.concatenate([jnp.where(first, x, peer), jnp.where(first, peer, x)], axis=0)


def scatter_l(x, axis):
    size = lax.axis_size("l")
    if size != 2:
        return lax.psum_scatter(x.astype(F32), "l", scatter_dimension=axis, tiled=True)
    part = x.shape[axis] // 2
    mine = lax.axis_index("l")
    kept = lax.dynamic_slice_in_dim(x, mine * part, part, axis)
    sent = lax.dynamic_slice_in_dim(x, (1 - mine) * part, part, axis)
    return kept.astype(F32) + flip(sent.astype(BF), "l", 1).astype(F32)


def sum_direct(x, axes, bits):
    total = x
    size = 1
    for axis in axes:
        size *= lax.axis_size(axis)
    for mask in range(1, size):
        if mask & ~bits == 0:
            total = total + lax.ppermute(x, axes, [(i, i ^ mask) for i in range(size)])
    return total


def sum_peers(x):
    size = HALVES * lax.axis_size("l")
    if size == 4:
        return sum_direct(x, ("h", "l"), 3)
    step = 1
    while step < size:
        x = x + lax.ppermute(x, ("h", "l"), [(i, i ^ step) for i in range(size)])
        step *= 2
    return x


def two_parts(values, rows):
    high = values.astype(BF)
    low = (values - high.astype(F32)).astype(BF)
    return jnp.pad(jnp.concatenate([high, low], axis=0), ((0, rows - 4), (0, 0)))[None]


def whole_of(block):
    return block[0:2].astype(F32) + block[2:4].astype(F32)


def tables_kernel(base_ref, fwd_ref, bwd_ref):
    rows, width = fwd_ref.shape[1], fwd_ref.shape[2]
    span = base_ref.shape[1]
    odd = (
        lax.broadcasted_iota(jnp.int32, (rows, width), 0)
        + lax.broadcasted_iota(jnp.int32, (rows, width), 1)
    ) % 2
    sign = (1 - 2 * odd).astype(F32)
    for index in range(4):
        for which, out in ((0, fwd_ref), (1, bwd_ref)):
            line = jnp.broadcast_to(base_ref[pl.ds(which * 4 + index, 1), :], (rows, span))
            rolled = pltpu.roll(line, 0, 1, stride=1, stride_axis=0)[:, :width]
            out[2 * index] = rolled.astype(BF)
            out[2 * index + 1] = (rolled * sign).astype(BF)


def build_tables(filters, h, m):
    seq_len, count = filters.shape
    phi = jnp.transpose(filters.astype(BF).astype(F32))
    zeros = jnp.zeros((count, BLOCK), F32)
    bwd = jnp.concatenate([phi, zeros], axis=1)
    back = jnp.flip(phi, axis=1)
    fwd = jnp.concatenate(
        [
            back[:, seq_len - 1 - BLOCK :],
            jnp.zeros((count, BLOCK), F32),
            back[:, : seq_len - 1 - BLOCK],
        ],
        axis=1,
    )
    rows = []
    for table in (fwd, bwd):
        for rel in range(HALVES):
            first = 12 * (h ^ rel) + (3 * m) // 2
            rows.append(lax.dynamic_slice_in_dim(table, first, 2, 0))
    base = jnp.concatenate(rows, axis=0)
    shape = jax.ShapeDtypeStruct((8, BLOCK, seq_len), BF)
    return pl.pallas_call(
        tables_kernel,
        out_shape=(shape, shape),
        in_specs=[VM],
        out_specs=(VM, VM),
        compiler_params=pltpu.CompilerParams(vmem_limit_bytes=VMEM_LIMIT),
        cost_estimate=pl.CostEstimate(flops=20_000_000, bytes_accessed=5_000_000, transcendentals=0),
    )(base)


def load_rows(refs, scratch, sem):
    started = []
    for j in range(MEMBERS):
        for ref, first, size in used_parts(refs, j, scratch.shape[1]):
            into = scratch.at[j, pl.ds(first, size)]
            started.append(pltpu.make_async_copy(ref, into, sem.at[len(started)]))
            started[-1].start()
    return started


def store_rows(scratch, refs, sem):
    half = scratch.shape[1] // 2
    copies = []
    for j in range(6):
        copies.append((scratch.at[j], refs[j]))
    for j in (6, 7):
        copies.append((scratch.at[j, pl.ds(0, half)], refs[2 * j - 6]))
        copies.append((scratch.at[j, pl.ds(half, half)], refs[2 * j - 5]))
    started = [pltpu.make_async_copy(a, b, sem.at[k]) for k, (a, b) in enumerate(copies)]
    for copy in started:
        copy.start()
    return started


def halves_of(refs, j):
    if j < 6:
        return [(refs[j], 0)]
    return [(refs[2 * j - 6], 0), (refs[2 * j - 5], refs[2 * j - 6].shape[0])]


def used_parts(refs, j, tokens):
    found = []
    for ref, first in halves_of(refs, j):
        size = min(ref.shape[0], tokens - first)
        if size > 0:
            found.append((ref.at[pl.ds(0, size)], first, size))
    return found


def unused_parts(refs, j, tokens):
    found = []
    for ref, first in halves_of(refs, j):
        start = max(tokens - first, 0)
        if start < ref.shape[0]:
            found.append((ref.at[pl.ds(start, ref.shape[0] - start)], ref.shape[0] - start))
    return found


def place(info, r):
    return pl.multiple_of(info[19 + r], 128)


def packed_copies(info, refs, packed, sem, act):
    for j in range(MEMBERS):

        def run(tokens, j=j):
            for k, (ref, first, size) in enumerate(used_parts(refs, j, tokens)):
                into = packed.at[pl.ds(place(info, j) + first, size)]
                act(pltpu.make_async_copy(ref, into, sem.at[j, k]))

        by_length(info[j], run)


def unpacked_copies(info, packed, zeros, refs, sem, act):
    for j in range(MEMBERS):

        def run(tokens, j=j):
            k = 0
            for ref, first, size in used_parts(refs, j, tokens):
                source = packed.at[pl.ds(place(info, j) + first, size)]
                act(pltpu.make_async_copy(source, ref, sem.at[j, k]))
                k += 1
            for ref, size in unused_parts(refs, j, tokens):
                act(pltpu.make_async_copy(zeros.at[pl.ds(0, size)], ref, sem.at[j, k]))
                k += 1

        by_length(info[j], run)


def chunk_copies(info, spec_in, spec, sem, act):
    count, rows = spec.shape[0], spec.shape[1]
    for c in range(count):

        @pl.when(c * rows < info[27])
        def _(c=c):
            act(pltpu.make_async_copy(spec_in.at[pl.ds(c * rows, rows)], spec.at[c], sem.at[c]))


def chunks_of(info, rows):
    return lax.div(info[27] + (rows - 1), rows)


def weight_copies(info, plan, pieces, weight, sem):
    copies = []
    for piece, (rel, l, begin, size, own, source) in zip(pieces, plan):
        l = info[18] if l == "mine" else 1 - info[18] if l == "other" else l
        end = begin + size
        areas = [(0, own, rel * 6 * BLOCK), (own, 2 * own, (rel * 2 + 1) * 3 * BLOCK)]
        if end > 2 * own:
            lags = end - 2 * own
            areas.append((2 * own, end, 12 * BLOCK + rel * 2 * lags))
        for first, last, target in areas:
            low, high = max(first, begin), min(last, end)
            if low < high:
                to = target + l * (last - first) + (low - first)
                if not isinstance(to, int):
                    to = pl.multiple_of(to, 16)
                copies.append(
                    pltpu.make_async_copy(
                        piece.at[pl.ds(source + low - begin, high - low)],
                        weight.at[pl.ds(to, high - low)],
                        sem.at[len(copies)],
                    )
                )
    return copies


def start(copy):
    copy.start()


def finish(copy):
    copy.wait()


def by_length(length, run):
    pl.when(length <= 128)(functools.partial(run, 128))
    pl.when((length > 128) & (length <= 256))(functools.partial(run, 256))
    pl.when(length > 256)(functools.partial(run, 512))


def combos(info):
    middle = info[8]
    for rel in range(HALVES):
        for sign in range(2):
            for pos, which in enumerate((0, middle, 1)):
                block = (rel * 2 + sign) * 3 + pos
                yield block, rel * 4 + which * 2 + sign, pos % 2


def gain_columns(table_ref, feature, own):
    devices = table_ref.shape[0]
    shift = own.bit_length() - 1
    rows = feature.shape[0]
    device = lax.broadcasted_iota(jnp.int32, (rows, devices), 1)
    chosen = (device == (feature >> shift)).astype(BF)
    found = dot(chosen, table_ref[...].astype(BF))
    lane = lax.broadcasted_iota(jnp.int32, found.shape, 1)
    return jnp.sum(jnp.where(lane == (feature & (own - 1)), found, 0.0), axis=1, keepdims=True)


def feature_places(info, model, lag_span):
    line = lax.broadcasted_iota(jnp.int32, (BLOCK, 1), 0)
    rel = (line >= lag_span).astype(jnp.int32)
    source = lag_span * (MEMBERS * (info[17] ^ rel) + info[9]) + line - rel * lag_span
    return [line + info[8] * BLOCK, line + (1 - info[8]) * BLOCK, source & (model - 1)]


def feature_gains(info, table_ref, model, own, lag_span):
    return [
        gain_columns(table_ref, feature, own) for feature in feature_places(info, model, lag_span)
    ]


def conv_kernel(own, place_ref, table_ref, pick_ref, *refs):
    rows_in = refs[:10]
    spec_out, info, gains = refs[10:13]
    stack, lines, normed, spec, sem_in, sem_line, sem_spec = refs[13:]
    seq_len = stack.shape[1]
    loads = load_rows(rows_in, stack, sem_in)
    line_copies = []
    for j in range(MEMBERS):
        ref, first = halves_of(rows_in, j)[-1]
        line_copies.append(
            pltpu.make_async_copy(
                ref.at[pl.ds(seq_len - first, lines.shape[1])], lines.at[j], sem_line.at[j]
            )
        )
        line_copies[-1].start()
    gains[...] = jnp.zeros_like(gains)
    for k in range(11):
        info[8 + k] = place_ref[k]
    for copy in line_copies:
        copy.wait()
    lane = lax.broadcasted_iota(jnp.int32, (1, 128), 1)
    weights = jnp.where(lane == 2 * own, 16.0, jnp.where(lane == 2 * own + 1, 1.0, 0.0))
    total = jnp.int32(0)
    size_l = gains.shape[0] // (HALVES * MEMBERS)
    for j in range(MEMBERS):
        line = lines[j, :, :128].astype(F32)[0:1]
        length = jnp.sum(line * weights).astype(jnp.int32)
        info[j] = length
        info[19 + j] = total
        total = total + jnp.where(length <= 128, 128, jnp.where(length <= 256, 256, seq_len))
        device = (info[17] * MEMBERS + info[9 + j]) * size_l + info[18]
        gains[pl.ds(device, 1), :] = line
    info[27] = total
    for copy in loads:
        copy.wait()
    odd = info[8] == 1

    def spec_copy(r, tokens):
        slot = lax.rem(r, 2)
        return pltpu.make_async_copy(
            spec.at[slot, pl.ds(0, tokens)],
            spec_out.at[pl.ds(place(info, r), tokens)],
            sem_spec.at[slot],
        )

    def row(r, carry):
        slot = lax.rem(r, 2)

        @pl.when(r >= 2)
        def _():
            by_length(info[r - 2], lambda tokens: spec_copy(r - 2, tokens).wait())

        def run(tokens):
            left = stack[r, pl.ds(0, tokens), :BLOCK]
            right = stack[r, pl.ds(0, tokens), BLOCK:]
            normed[pl.ds(0, tokens), :BLOCK] = jnp.where(odd, right, left)
            normed[pl.ds(0, tokens), BLOCK:] = jnp.where(odd, left, right)
            first = min(tokens, BLOCK)
            for block, table, side in combos(info):
                cols = pl.ds(side * BLOCK, BLOCK)
                into = pl.ds(block * BLOCK, BLOCK)
                spec[slot, pl.ds(0, first), into] = dot(
                    table_ref[table, pl.ds(0, first), pl.ds(BLOCK, first)],
                    normed[pl.ds(0, first), cols],
                ).astype(BF)
                if tokens > BLOCK:
                    spec[slot, pl.ds(BLOCK, BLOCK), into] = dot(
                        table_ref[table], normed[:, cols]
                    ).astype(BF)
            lagged = None
            for lag in range(LAGS):
                moved = dot(normed[pl.ds(0, tokens)], pick_ref[lag])
                if lag:
                    moved = jnp.concatenate(
                        [jnp.zeros((lag, BLOCK), F32), moved[: tokens - lag]], axis=0
                    )
                lagged = moved if lagged is None else lagged + moved
            spec[slot, pl.ds(0, tokens), pl.ds(12 * BLOCK, BLOCK)] = lagged.astype(BF)
            spec_copy(r, tokens).start()

        by_length(info[r], run)
        return carry

    lax.fori_loop(0, MEMBERS, row, 0)
    for r in (MEMBERS - 2, MEMBERS - 1):
        by_length(info[r], lambda tokens, r=r: spec_copy(r, tokens).wait())


def row_shapes(seq_len, model):
    whole = jax.ShapeDtypeStruct((seq_len, model), BF)
    half = jax.ShapeDtypeStruct((seq_len // 2, model), BF)
    return (whole,) * 6 + (half,) * 4


def params(flops, data):
    return dict(
        compiler_params=pltpu.CompilerParams(vmem_limit_bytes=VMEM_LIMIT),
        cost_estimate=pl.CostEstimate(flops=flops, bytes_accessed=data, transcendentals=0),
    )


def conv_call(own, devices, place, table, pick, rows, seq_len):
    model = rows[0].shape[1]
    features = 13 * BLOCK
    return pl.pallas_call(
        functools.partial(conv_kernel, own),
        out_shape=(
            jax.ShapeDtypeStruct((MEMBERS * seq_len, features), BF),
            jax.ShapeDtypeStruct((32,), jnp.int32),
            jax.ShapeDtypeStruct((devices, 128), F32),
        ),
        in_specs=[SM, VM, VM] + [ANY] * 10,
        out_specs=(ANY, SM, VM),
        scratch_shapes=[
            pltpu.VMEM((MEMBERS, seq_len, model), BF),
            pltpu.VMEM((MEMBERS, 16, model), BF),
            pltpu.VMEM((seq_len, model), BF),
            pltpu.VMEM((2, seq_len, features), BF),
            pltpu.SemaphoreType.DMA((10,)),
            pltpu.SemaphoreType.DMA((MEMBERS,)),
            pltpu.SemaphoreType.DMA((2,)),
        ],
        **params(5_000_000_000, 20_000_000),
    )(place, table, pick, *rows)


def mix_kernel(plan, own, lag_span, info, gain_ref, lag_ref, spec_in, *refs):
    pieces, refs = refs[: len(plan)], refs[len(plan) :]
    parts_out = refs[:10]
    weight, spec, parts, zeros, sem_in, sem_out, sem_spec = refs[10:]
    weight[pl.ds(12 * BLOCK, BLOCK)] = lag_ref[...]
    copies = weight_copies(info, plan, pieces, weight, sem_in)
    for copy in copies:
        copy.start()
    chunk_copies(info, spec_in, spec, sem_spec, start)
    zeros[...] = jnp.zeros_like(zeros)
    rows = spec.shape[1]
    for copy in copies:
        copy.wait()
    columns = feature_gains(info, gain_ref, weight.shape[1], own, lag_span)
    for block in range(weight.shape[0] // BLOCK):
        at = pl.ds(block * BLOCK, BLOCK)
        column = columns[2 if block == 12 else block % 3 % 2]
        weight[at] = (weight[at].astype(F32) * column).astype(BF)

    def chunk(c, carry):
        here = pl.ds(pl.multiple_of(c * rows, rows), rows)
        pltpu.make_async_copy(spec_in.at[here], spec.at[c], sem_spec.at[c]).wait()
        parts[here] = dot(spec[c], weight[...]).astype(BF)
        return carry

    lax.fori_loop(0, chunks_of(info, rows), chunk, 0)
    unpacked_copies(info, parts, zeros, parts_out, sem_out, start)
    unpacked_copies(info, parts, zeros, parts_out, sem_out, finish)


def mix_call(info, plan, own, lag_span, gain, lag_weight, spec, pieces):
    tokens, features = spec.shape
    model = pieces[0].shape[-1]
    seq_len = tokens // MEMBERS
    return pl.pallas_call(
        functools.partial(mix_kernel, plan, own, lag_span),
        out_shape=row_shapes(seq_len, model),
        in_specs=[SM, VM, VM, ANY] + [ANY] * len(plan),
        out_specs=(ANY,) * 10,
        scratch_shapes=[
            pltpu.VMEM((features, model), BF),
            pltpu.VMEM((MEMBERS, seq_len, features), BF),
            pltpu.VMEM((tokens, model), BF),
            pltpu.VMEM((seq_len, model), BF),
            pltpu.SemaphoreType.DMA((3 * len(plan),)),
            pltpu.SemaphoreType.DMA((MEMBERS, 3)),
            pltpu.SemaphoreType.DMA((MEMBERS,)),
        ],
        **params(8_000_000_000, 30_000_000),
    )(info, gain, lag_weight, spec, *pieces)


def back_conv_kernel(plan, info, table_ref, pick_ref, lag_ref, *refs):
    pieces, refs = refs[: len(plan)], refs[len(plan) :]
    rows_in, parts_out = refs[:10], refs[10:20]
    d_mix, d_spec, parts, weight, sem_in, sem_out, sem_w = refs[20:]
    packed_copies(info, rows_in, d_mix, sem_in, start)
    weight[pl.ds(12 * BLOCK, BLOCK)] = lag_ref[...]
    copies = weight_copies(info, plan, pieces, weight, sem_w)
    for copy in copies:
        copy.start()
    _, seq_len, model = parts.shape
    features = d_spec.shape[1]
    odd = info[8] == 1
    packed_copies(info, rows_in, d_mix, sem_in, finish)
    for copy in copies:
        copy.wait()

    def chunk(c, carry):
        here = pl.ds(pl.multiple_of(c * seq_len, seq_len), seq_len)
        dm = d_mix[here]
        for block in range(features // BLOCK):
            cols = pl.ds(block * BLOCK, BLOCK)
            d_spec[here, cols] = dot_nt(dm, weight[cols]).astype(BF)
        return carry

    lax.fori_loop(0, chunks_of(info, seq_len), chunk, 0)

    def row(r, carry):
        at_row = place(info, r)

        def run(tokens):
            here = pl.ds(at_row, tokens)
            first = min(tokens, BLOCK)
            sides = [[None, None], [None, None]]
            for block, table, side in combos(info):
                cols = pl.ds(block * BLOCK, BLOCK)
                term = dot(table_ref[table, pl.ds(0, first), pl.ds(0, tokens)], d_spec[here, cols])
                sides[side][0] = term if sides[side][0] is None else sides[side][0] + term
                if tokens > BLOCK:
                    term = dot(
                        table_ref[table, :, pl.ds(0, BLOCK)],
                        d_spec[pl.ds(at_row + BLOCK, BLOCK), cols],
                    )
                    sides[side][1] = term if sides[side][1] is None else sides[side][1] + term
            d_lag = d_spec[here, pl.ds(12 * BLOCK, BLOCK)]
            back = None
            for lag in range(LAGS):
                moved = dot_nt(d_lag, pick_ref[lag])
                if lag:
                    moved = jnp.concatenate(
                        [moved[lag:], jnp.zeros((lag, model), F32)], axis=0
                    )
                back = moved if back is None else back + moved
            for begin in range(0, tokens, BLOCK):
                size = min(BLOCK, tokens)
                k = begin // BLOCK
                at = pl.ds(begin, size)
                d_a = sides[0][k] + back[begin : begin + size, :BLOCK]
                d_b = sides[1][k] + back[begin : begin + size, BLOCK:]
                left, right = jnp.where(odd, d_b, d_a), jnp.where(odd, d_a, d_b)
                parts[r, at, :BLOCK] = left.astype(BF)
                parts[r, at, BLOCK:] = right.astype(BF)
            if tokens < parts.shape[1]:
                rest = parts.shape[1] - tokens
                parts[r, pl.ds(tokens, rest)] = jnp.zeros((rest, model), BF)

        by_length(info[r], run)
        return carry

    lax.fori_loop(0, MEMBERS, row, 0)
    for copy in store_rows(parts, parts_out, sem_out):
        copy.wait()


def back_conv_call(info, plan, table, pick, lag_weight, pieces, rows):
    seq_len, model = rows[0].shape
    features = 13 * BLOCK
    return pl.pallas_call(
        functools.partial(back_conv_kernel, plan),
        out_shape=row_shapes(seq_len, model),
        in_specs=[SM, VM, VM, VM] + [ANY] * (10 + len(plan)),
        out_specs=(ANY,) * 10,
        scratch_shapes=[
            pltpu.VMEM((MEMBERS * seq_len, model), BF),
            pltpu.VMEM((MEMBERS * seq_len, features), BF),
            pltpu.VMEM((MEMBERS, seq_len, model), BF),
            pltpu.VMEM((features, model), BF),
            pltpu.SemaphoreType.DMA((MEMBERS, 2)),
            pltpu.SemaphoreType.DMA((10,)),
            pltpu.SemaphoreType.DMA((3 * len(plan),)),
        ],
        **params(12_000_000_000, 20_000_000),
    )(info, table, pick, lag_weight, *pieces, *rows)


def spread(value, feature, model):
    lane = lax.broadcasted_iota(jnp.int32, (value.shape[0], model), 1)
    return jnp.sum(jnp.where(lane == feature, value, 0.0), axis=0, keepdims=True)


def grad_kernel(plan, first_block, size_l, gain_own, cuts, info, gain_ref, lag_ref, spec_in, *refs):
    pieces, refs = refs[: len(plan)], refs[len(plan) :]
    rows_in, refs = refs[:10], refs[10:]
    count = len(cuts)
    outs, gain_out, refs = refs[:count], refs[count], refs[count + 1 :]
    shares, lag_shares, d_mix, spec, total, weight, sem_in, sem_spec, sem_w, sem_out = refs
    features = total.shape[1]
    model = total.shape[0]
    rows = spec.shape[1]
    own = 3 * BLOCK // size_l
    lags = lag_shares.shape[1]
    cols_in = pl.ds(first_block * BLOCK, features)

    def share_of(l):
        return info[18] ^ l if size_l == 2 else l

    def chunk_copy(c):
        source = spec_in.at[pl.ds(pl.multiple_of(c * rows, rows), rows), cols_in]
        return pltpu.make_async_copy(source, spec.at[c], sem_spec.at[c])

    packed_copies(info, rows_in, d_mix, sem_in, start)
    for c in range(spec.shape[0]):

        @pl.when(c * rows < info[27])
        def _(c=c):
            chunk_copy(c).start()

    weight[pl.ds(12 * BLOCK, BLOCK)] = lag_ref[...]
    weights = weight_copies(info, plan, pieces, weight, sem_w)
    for copy in weights:
        copy.start()
    total[...] = jnp.zeros_like(total)
    packed_copies(info, rows_in, d_mix, sem_in, finish)

    def chunk(c, carry):
        base = pl.multiple_of(c * rows, rows)
        here = pl.ds(base, rows)
        chunk_copy(c).wait()
        for tile in range(0, rows, 128):

            @pl.when(base + tile >= info[27])
            def _(tile=tile):
                spec[c, pl.ds(tile, 128)] = jnp.zeros((128, features), BF)
                d_mix[pl.ds(base + tile, 128)] = jnp.zeros((128, d_mix.shape[1]), BF)

        dm_t = jnp.transpose(d_mix[here].astype(F32)).astype(BF)
        for block in range(features // BLOCK):
            cols = pl.ds(block * BLOCK, BLOCK)
            total[:, cols] += dot(dm_t, spec[c, :, cols])
        return carry

    lax.fori_loop(0, chunks_of(info, rows), chunk, 0)
    for copy in weights:
        copy.wait()
    lag_span = lags * size_l
    columns = feature_gains(info, gain_ref, model, gain_own, lag_span)
    places = feature_places(info, model, lag_span)
    sums = [None, None, None]
    for k in range(features // BLOCK):
        block = first_block + k
        kind = 2 if block == 12 else block % 3 % 2
        value = jnp.transpose(total[:, pl.ds(k * BLOCK, BLOCK)])
        part = jnp.sum(
            value * weight[pl.ds(block * BLOCK, BLOCK)].astype(F32), axis=1, keepdims=True
        )
        sums[kind] = part if sums[kind] is None else sums[kind] + part
        value = (value * columns[kind]).astype(BF)
        if block < 12:
            branch, first = block // 3 % 2, block % 3 * BLOCK
            at = first
            while at < first + BLOCK:
                l, inside = at // own, at % own
                size = min(own - inside, first + BLOCK - at)
                shares[share_of(l), pl.ds(branch * own + inside, size)] = value[
                    at - first : at - first + size
                ]
                at += size
        else:
            for l in range(size_l):
                lag_shares[share_of(l)] = value[l * lags : (l + 1) * lags]
                at = (size_l + l) * lags
                shares[share_of(l), pl.ds(2 * own, lags)] = value[at : at + lags]
    copies = []
    for n, (k, a, b) in enumerate(cuts):
        source = lag_shares.at[b] if k is None else shares.at[k, pl.ds(a, b - a)]
        copies.append(pltpu.make_async_copy(source, outs[n], sem_out.at[n]))
        copies[-1].start()
    gain_out[...] = jnp.zeros_like(gain_out)
    for kind in range(3):
        if sums[kind] is not None:
            gain_out[0:1] += spread(sums[kind], places[kind], model)
    for copy in copies:
        copy.wait()


def grad_call(info, plan, gain_own, gain, lag_weight, spec, pieces, rows, size_l, lags, cuts):
    seq_len, model = rows[0].shape
    tokens, features = spec.shape
    far = cuts[-1][0] is None
    features = features - 6 * BLOCK if far else 6 * BLOCK
    share_rows = 6 * BLOCK // size_l + (lags if far else 0)
    shapes = tuple(
        jax.ShapeDtypeStruct((lags if k is None else b - a, model), BF) for k, a, b in cuts
    )
    return pl.pallas_call(
        functools.partial(grad_kernel, plan, 6 if far else 0, size_l, gain_own, cuts),
        out_shape=shapes + (jax.ShapeDtypeStruct((8, model), F32),),
        in_specs=[SM, VM, VM] + [ANY] * (11 + len(plan)),
        out_specs=(ANY,) * len(shapes) + (VM,),
        scratch_shapes=[
            pltpu.VMEM((size_l, share_rows, model), BF),
            pltpu.VMEM((size_l, lags, model), BF),
            pltpu.VMEM((tokens, model), BF),
            pltpu.VMEM((MEMBERS, seq_len, features), BF),
            pltpu.VMEM((model, features), F32),
            pltpu.VMEM((13 * BLOCK, model), BF),
            pltpu.SemaphoreType.DMA((MEMBERS, 2)),
            pltpu.SemaphoreType.DMA((MEMBERS,)),
            pltpu.SemaphoreType.DMA((3 * len(plan),)),
            pltpu.SemaphoreType.DMA((len(cuts),)),
        ],
        **params(4_000_000_000, 15_000_000),
    )(info, gain, lag_weight, spec, *pieces, *rows)


def mlp_kernel(info, normed_ref, d_out_ref, *refs):
    packs = refs[:10]
    wide_out, d_normed_out, mlp_out = refs[10:13], refs[13], refs[14]
    held, wide, sem, sem_out = refs[15:]
    model = normed_ref.shape[1]
    devices, blocks, _, _ = held.shape
    count = blocks // 3
    size_l = devices // (HALVES * MEMBERS)
    half = HALVES * size_l // 2
    copies = []
    for j in range(MEMBERS):
        for ref, first in halves_of(packs, j):
            first = first // blocks
            for k in range(ref.shape[0] // blocks):
                rel, l = (first + k) // size_l, (first + k) % size_l
                l = info[18] ^ l if size_l == 2 else l
                device = ((info[17] ^ rel) * MEMBERS + info[9 + j]) * size_l + l
                source = ref.at[pl.ds(k * blocks, blocks)]
                copies.append(pltpu.make_async_copy(source, held.at[device], sem.at[len(copies)]))
    for copy in copies:
        copy.start()
    for copy in copies:
        copy.wait()
    root, cubic = 0.7978845608028654, 0.044715
    out_copies = []
    for s in range(count):
        cols = pl.ds(s * model, model)
        normed, d_out = normed_ref[...], d_out_ref[...]
        gate_s = held[:, s].reshape(model, model)
        up_s = held[:, count + s].reshape(model, model)
        pre = dot(normed, gate_s)
        upward = dot(normed, up_s)
        share = devices // count
        down_s = held[pl.ds(s * share, share), 2 * count :].reshape(model, model)
        d_hidden = dot_nt(d_out, down_s)
        square = pre * pre
        tanh = jnp.tanh(root * pre * (1.0 + cubic * square))
        half = 0.5 * (1.0 + tanh)
        slope = half + 0.5 * pre * (1.0 - tanh * tanh) * (root * (1.0 + 3.0 * cubic * square))
        active = pre * half
        hidden = (active * upward).astype(BF)
        d_gate = (d_hidden * upward * slope).astype(BF)
        d_up = (d_hidden * active).astype(BF)
        for k, value in enumerate((hidden, d_gate, d_up)):
            wide[k, :, cols] = value
            copy = pltpu.make_async_copy(
                wide.at[k, :, cols], wide_out[k].at[:, cols], sem_out.at[k, s]
            )
            copy.start()
            out_copies.append(copy)
        back = dot_nt(d_gate, gate_s) + dot_nt(d_up, up_s)
        ahead = dot(hidden, down_s)
        if s == 0:
            d_normed_out[...] = back
            mlp_out[...] = ahead
        else:
            d_normed_out[...] += back
            mlp_out[...] += ahead
    for copy in out_copies:
        copy.wait()


def mlp_call(info, normed, d_out, packs, devices):
    seq_len, model = normed.shape
    blocks = packs[0].shape[0] * MEMBERS // devices
    own = packs[0].shape[1]
    inner = blocks // 3 * model
    wide = jax.ShapeDtypeStruct((seq_len, inner), BF)
    whole = jax.ShapeDtypeStruct((seq_len, model), F32)
    count = inner // model
    return pl.pallas_call(
        mlp_kernel,
        out_shape=(wide, wide, wide, whole, whole),
        in_specs=[SM, VM, VM] + [ANY] * 10,
        out_specs=(ANY, ANY, ANY, VM, VM),
        scratch_shapes=[
            pltpu.VMEM((devices, blocks, own, model), BF),
            pltpu.VMEM((3, seq_len, inner), BF),
            pltpu.SemaphoreType.DMA((devices,)),
            pltpu.SemaphoreType.DMA((3, count)),
        ],
        **params(6_500_000_000, 16_000_000),
    )(info, normed, d_out, *packs)


def mlp_grad_kernel(normed_ref, d_out_ref, hidden, d_gate, d_up, out, wide, total, sem, sem_out):
    model = normed_ref.shape[1]
    inner = wide.shape[2]
    count = inner // model
    groups, size_l, _, blocks, own, _ = total.shape
    copies = [
        pltpu.make_async_copy(source, wide.at[k], sem.at[k])
        for k, source in enumerate((d_gate, d_up, hidden))
    ]
    for copy in copies:
        copy.start()

    def turned(value):
        return jnp.transpose(value.astype(F32)).astype(BF)

    normed_t = turned(normed_ref[...])
    for k in range(2):
        copies[k].wait()
        for s in range(count):
            value = dot(normed_t, wide[k, :, pl.ds(s * model, model)]).astype(BF)
            value = value.reshape(HALVES, groups, size_l, own, model)
            for h in range(HALVES):
                total[:, :, h, k * count + s] = value[h]
    copies[2].wait()
    share = HALVES * groups // count
    for s in range(count):
        value = dot(turned(wide[2, :, pl.ds(s * model, model)]), d_out_ref[...]).astype(BF)
        h, at = s * share // groups, s * share % groups
        total[pl.ds(at, share), :, h, 2 * count :] = value.reshape(
            share, size_l, count, own, model
        )
    copy = pltpu.make_async_copy(total, out, sem_out)
    copy.start()
    copy.wait()


def mlp_grad_call(normed, d_out, hidden, d_gate, d_up, size_l):
    seq_len, inner = hidden.shape
    model = normed.shape[1]
    count = inner // model
    own = model // (HALVES * MEMBERS * size_l)
    shape = (MEMBERS, size_l, HALVES, 3 * count, own, model)
    return pl.pallas_call(
        mlp_grad_kernel,
        out_shape=jax.ShapeDtypeStruct(shape, BF),
        in_specs=[VM, VM, ANY, ANY, ANY],
        out_specs=ANY,
        scratch_shapes=[
            pltpu.VMEM((3, seq_len, inner), BF),
            pltpu.VMEM(shape, BF),
            pltpu.SemaphoreType.DMA((3,)),
            pltpu.SemaphoreType.DMA,
        ],
        **params(3_200_000_000, 14_000_000),
    )(normed, d_out, hidden, d_gate, d_up)


def body(
    inputs,
    cotangent,
    lengths,
    filters,
    gain_first,
    mix_plus,
    mix_minus,
    auto_weight,
    gain_second,
    w_gate,
    w_upward,
    w_down,
):
    _, seq_len, model = inputs.shape
    size_l = lax.axis_size("l")
    n = HALVES * MEMBERS * size_l
    h, m, l = lax.axis_index("h"), lax.axis_index(GROUP), lax.axis_index("l")
    me = (h * MEMBERS + m) * size_l + l
    own = gain_first.shape[0]
    inner = w_gate.shape[1]
    count = inner // model

    def blocks(w):
        return jnp.transpose(w.astype(BF).reshape(own, count, model), (1, 0, 2))

    pack = jnp.concatenate(
        [blocks(w_gate), blocks(w_upward), w_down.astype(BF).reshape(count, own, model)], axis=0
    )
    pack_rows = 3 * count * own
    plus, minus, auto = mix_plus.astype(BF), mix_minus.astype(BF), auto_weight.astype(BF)
    own_rows, lag_rows = plus.shape[0], auto.shape[0]
    share_rows = 2 * own_rows + lag_rows
    sizes, cuts = [], [0]
    if size_l == 2:
        a, b = own_rows * 3 // 8, own_rows // 12
        chunks = [
            pack.reshape(pack_rows, model),
            plus[:a],
            jnp.concatenate([plus[a:], minus[:b]], axis=0),
            jnp.concatenate([minus[b:], auto], axis=0),
        ]
        cuts = [0, 0, a, own_rows + b, share_rows]
        sizes = [part.shape[0] for part in chunks]
    far, pairs = [None] * 4, [None] * 5

    def cross(k):
        if size_l == 2:
            far[k] = flip(chunks[k], "h", 1)

    def cross_l(k):
        if size_l == 2:
            both = ([chunks[k]] if k < 4 else []) + ([far[k - 1]] if k else [])
            pairs[k] = flip(jnp.concatenate(both, axis=0) if len(both) > 1 else both[0], "l", 1)

    x = inputs[0]
    scale_one = rms_scale(x)
    pre_one = x * scale_one
    line = jnp.concatenate(
        [
            gain_first.astype(BF),
            gain_second.astype(BF),
            (lengths // 16).astype(BF),
            (lengths % 16).astype(BF),
            jnp.zeros((model - 2 * own - 2,), BF),
        ]
    )
    below = lax.broadcasted_iota(jnp.int32, (32, 1), 0) == 0
    below = jnp.where(below, line[None, :], 0.0).astype(BF)
    row = Gather(jnp.concatenate([pre_one.astype(BF), below], axis=0))

    cross(0)
    cross_l(0)
    if size_l == 2:
        row.row, far[0], pairs[0], *chunks[1:] = sync_all(row.row, far[0], pairs[0], *chunks[1:])
    cross(1)
    cross_l(1)
    row.first()
    fwd_table, bwd_table = build_tables(filters, h, m)

    far, pairs, row, fwd_table = sync_all(far, pairs, row, fwd_table)
    if size_l == 2:
        *chunks[2:], far[1] = sync_all(*chunks[2:], far[1])
    cross(2)
    cross_l(2)
    row.second(core=False)
    row.core1 = flip(row.near1, "m", 1)

    far, pairs, row = sync_all(far, pairs, row)
    if size_l == 2:
        chunks[3], far[2] = sync_all(chunks[3], far[2])
    cross(3)
    cross_l(3)
    row.third()
    row.core2 = flip(row.near2, "m", 1)
    members = m ^ lax.iota(jnp.int32, MEMBERS)
    place = jnp.concatenate([jnp.stack([m % 2]), members, jnp.stack([h, l])])

    col = lax.broadcasted_iota(jnp.int32, (LAGS, model, BLOCK), 2)
    feature = lax.broadcasted_iota(jnp.int32, (LAGS, model, BLOCK), 1)
    feature = (feature + (m % 2) * BLOCK) % model
    lag = lax.broadcasted_iota(jnp.int32, (LAGS, model, BLOCK), 0)
    lag_span = lag_rows * size_l
    rel = col // lag_span
    source = lag_span * (MEMBERS * (h ^ rel) + m) + col % lag_span
    pick = ((rel < 2) & (source == lag * model + feature)).astype(BF)

    if size_l == 2:
        held = [chunks[0], pairs[0], far[0], pairs[1][sizes[1] :]]
        pack = jnp.concatenate([part[:pack_rows] for part in held], axis=0)
        pack = Gather(pack.reshape(-1, own, model))
    else:
        pack = lax.all_gather(jnp.stack([pack, flip(pack, "h", 1)]), "l", axis=1)
        pack = Gather(pack.reshape(-1, own, model))
    x_rows = row.result()
    spec, info, gains = conv_call(own, n, place, fwd_table, pick, x_rows, seq_len)

    far, pairs, pack, gains, spec = sync_all(far, pairs, pack, gains, spec)
    cross_l(4)
    gains = sum_peers(gains)
    pack.first()

    pairs, gains, spec = sync_all(pairs, gains, spec)
    gain_one = gains[:, :own].reshape(1, model)
    gain_two = gains[:, own : 2 * own].reshape(1, model)
    plan, pieces = [], []
    if size_l == 2:
        for k in (1, 2, 3):
            at, size = cuts[k], sizes[k]
            plan.append((0, "mine", at, size, own_rows, 0))
            plan.append((1, "mine", at, size, own_rows, 0))
            plan.append((0, "other", at, size, own_rows, 0))
            plan.append((1, "other", at, size, own_rows, sizes[k + 1] if k < 3 else 0))
            pieces += [chunks[k], far[k], pairs[k], pairs[k + 1]]
        lag_weight = jnp.zeros((BLOCK, model), BF)
    else:
        share = jnp.concatenate([plus, minus, auto], axis=0)
        shares = lax.all_gather(share, ("h", "l"), axis=0)
        shares = shares.reshape((HALVES, size_l) + share.shape)
        lag_weight = []
        for rel in range(HALVES):
            half = lax.dynamic_index_in_dim(shares, h ^ rel, 0, keepdims=False)
            lag_weight.append(half[:, 2 * own_rows :])
            for k in range(size_l):
                plan.append((rel, k, 0, 2 * own_rows, own_rows, 0))
                pieces.append(half[k, : 2 * own_rows])
        lag_weight = jnp.stack(lag_weight).reshape(HALVES * lag_span, model)
        lag_weight = jnp.pad(lag_weight, ((0, BLOCK - HALVES * lag_span), (0, 0)))
    plan = tuple(plan)
    mixed = Reduce(mix_call(info, plan, own, lag_span, gains, lag_weight, spec, pieces))

    mixed, pack = sync_all(mixed, pack)
    mixed.first()
    pack.second()
    mixed = sync_all(mixed)[0]
    mixed.second()
    mixed, pack = sync_all(mixed, pack)
    mixed = mixed.third()
    pack.third()

    keep = lax.broadcasted_iota(jnp.int32, (seq_len, 1), 0) < lengths[0]
    middle = x + mixed
    scale_two = rms_scale(middle)
    pre_two = middle * scale_two
    normed_two = (pre_two * gain_two).astype(BF)
    d_out = jnp.where(keep, cotangent[0], 0.0)
    d_out_b = d_out.astype(BF)
    hidden, d_gate, d_up, d_normed_two, mlp_out = mlp_call(
        info, normed_two, d_out_b, pack.result(), n
    )
    d_middle = d_out + rms_back(middle, scale_two, d_normed_two * gain_two)

    row = Gather(d_middle.astype(BF))
    row.first()

    row, hidden, d_gate, d_up = sync_all(row, hidden, d_gate, d_up)
    row.second()
    mlp = mlp_grad_call(normed_two, d_out_b, hidden, d_gate, d_up, size_l)
    output = jnp.where(keep, middle + mlp_out, 0.0)
    grad_gain_two = jnp.sum(d_normed_two * pre_two, axis=0, keepdims=True)

    row, mlp, grad_gain_two = sync_all(row, mlp, grad_gain_two)
    mlp = lax.psum_scatter(mlp, GROUP, scatter_dimension=0)
    row.third()
    d_rows = row.result()
    if size_l == 2:
        cut = share_rows // 2 - 8
        cuts_far = ((1, 0, cut), (1, cut, share_rows), (0, 0, cut), (0, cut, share_rows))
        cut_near = ((0, own_rows), (own_rows, 2 * own_rows))
        cuts_near = tuple((k, a, b) for k in range(2) for a, b in cut_near)
    else:
        cuts_far = tuple((k, 0, share_rows) for k in range(size_l))
        cuts_near = tuple((k, 0, 2 * own_rows) for k in range(size_l))
    cuts_far += tuple((None, 0, k) for k in range(size_l))
    with_spec = (info, plan, own, gains, lag_weight, spec, pieces)
    *grad_far, gain_far = grad_call(*with_spec, d_rows, size_l, lag_rows, cuts_far)
    grad_lag = grad_far[-size_l:]

    grad_far, grad_lag, d_rows = sync_all(grad_far, grad_lag, d_rows)
    if size_l == 2:
        got_far = [flip(part, "l", 1) for part in grad_far[:2]]
    *grad_near, gain_near = grad_call(*with_spec, d_rows, size_l, lag_rows, cuts_near)

    if size_l == 2:
        grad_near, d_rows, got_far[0] = sync_all(grad_near, d_rows, got_far[0])
        back = [flip((grad_far[2].astype(F32) + got_far[0].astype(F32)).astype(BF), "h", 1)]
        got_near = [flip(grad_near[2], "l", 1)]
    else:
        grad_near, d_rows = sync_all(grad_near, d_rows)
    grad_gains = jnp.concatenate([(gain_far + gain_near)[0:1], grad_gain_two], axis=0)
    grad_gains = sum_direct(grad_gains, GROUP, 3)
    d_normed = Reduce(back_conv_call(info, plan, bwd_table, pick, lag_weight, pieces, d_rows))

    if size_l == 2:
        d_normed, back, got_far, got_near, grad_gains = sync_all(
            d_normed, back, got_far, got_near, grad_gains
        )
        part = (grad_far[3].astype(F32) + got_far[1].astype(F32)).astype(BF)
        back.append(flip(part, "h", 1))
    else:
        d_normed, grad_gains = sync_all(d_normed, grad_gains)
    d_normed.first()
    grad_gains = sum_direct(grad_gains, GROUP, 4)

    d_normed, grad_gains, mlp = sync_all(d_normed, grad_gains, mlp)
    d_normed.second()
    if size_l == 2:
        other = lax.dynamic_index_in_dim(mlp, 1 - l, 0, keepdims=False)
        mlp = lax.dynamic_index_in_dim(mlp, l, 0, keepdims=False).astype(F32)
        blocks_left = other.shape[0] * other.shape[1]
        other = jnp.concatenate(
            [other.reshape((blocks_left,) + other.shape[2:]), two_parts(grad_gains, own)], axis=0
        )
        other = flip(other, "l", 1)
        grad_gains = grad_gains + whole_of(other[blocks_left])
        mlp = mlp + other[:blocks_left].reshape(mlp.shape).astype(F32)
    else:
        grad_gains = lax.psum(grad_gains, "l")
        mlp = lax.psum_scatter(mlp.astype(F32), "l", scatter_dimension=0)

    if size_l == 2:
        d_normed, grad_gains, mlp, back, grad_near, grad_lag = sync_all(
            d_normed, grad_gains, mlp, back, grad_near, grad_lag
        )
    else:
        d_normed, grad_gains, mlp = sync_all(d_normed, grad_gains, mlp)
    d_normed = d_normed.third()
    if size_l == 2:
        other = lax.dynamic_index_in_dim(mlp, 1 - h, 0, keepdims=False).astype(BF)
        other = flip(jnp.concatenate([other, two_parts(grad_gains, own)], axis=0), "h", 1)
        mlp = lax.dynamic_index_in_dim(mlp, h, 0, keepdims=False) + other[:-1].astype(F32)
        grad_gains = grad_gains + whole_of(other[-1])
        got_near.append(flip(jnp.concatenate([grad_near[3], grad_lag[1]], axis=0), "l", 1))
    else:
        mlp_far = lax.dynamic_index_in_dim(mlp, 1 - h, 0, keepdims=False).astype(BF)
        mlp_near = lax.dynamic_index_in_dim(mlp, h, 0, keepdims=False)
        mlp = mlp_near + flip(mlp_far, "h", 1).astype(F32)
        grad_gains = grad_gains + flip(grad_gains, "h", 1)
    grad_gains = lax.dynamic_slice_in_dim(grad_gains, me * own, own, 1)
    input_grad = d_middle + rms_back(x, scale_one, d_normed * gain_one)
    if size_l == 2:
        near = jnp.concatenate([grad_near[0], grad_near[1], grad_lag[0]], axis=0).astype(F32)
        got = jnp.concatenate(got_near, axis=0).astype(F32)
        grad_mix = near + got + jnp.concatenate(back, axis=0).astype(F32)
    else:
        near = jnp.concatenate([jnp.stack(grad_near), jnp.stack(grad_lag)], axis=1)
        both = jnp.stack([near, jnp.stack(grad_far[:size_l])])
        grad_mix = jnp.where(h == 0, both, both[::-1]).reshape((-1,) + near.shape[1:])
        grad_mix = lax.psum_scatter(grad_mix, ("h", "l"), scatter_dimension=0).astype(F32)
    mlp = mlp.reshape(3, count, own, model)
    grad_gate, grad_up = [
        jnp.transpose(mlp[k], (1, 0, 2)).reshape(own, inner) for k in range(2)
    ]
    grad_down = mlp[2].reshape(count * own, model)

    return (
        output[None],
        input_grad[None],
        grad_gains[0],
        grad_mix[:own_rows],
        grad_mix[own_rows : 2 * own_rows],
        grad_mix[2 * own_rows :],
        grad_gains[1],
        grad_gate,
        grad_up,
        grad_down,
    )


def solution(mesh):
    shape = (HALVES, 2, 2, 2, mesh.size // (HALVES * MEMBERS))
    inner = Mesh(mesh.devices.reshape(shape), ALL)
    row, vec, mat = P(ALL, None, None), P(ALL), P(ALL, None)
    in_specs = (row, row, vec, P(), vec, mat, mat, mat, vec, mat, mat, mat)
    out_specs = (row, row, vec, mat, mat, mat, vec, mat, mat, mat)
    return jax.shard_map(body, mesh=inner, in_specs=in_specs, out_specs=out_specs, check_vma=False)
```

```python
import functools

import jax
import jax.numpy as jnp
from jax import lax
from jax.experimental import pallas as pl
from jax.experimental.pallas import tpu as pltpu
from jax.sharding import Mesh, PartitionSpec as P

EPSILON = 1e-05
MEMBERS = 8
HALVES = 2
BLOCK = 256
LAGS = 3
VMEM_LIMIT = 60 * 1024 * 1024
BF = jnp.bfloat16
F32 = jnp.float32
GROUP = ("z", "y", "c")
ALL = ("h",) + GROUP + ("l",)
ANY = pl.BlockSpec(memory_space=pl.ANY)
VM = pl.BlockSpec(memory_space=pltpu.VMEM)
SM = pl.BlockSpec(memory_space=pltpu.SMEM)


def rms_scale(values):
    return lax.rsqrt(jnp.mean(values * values, axis=-1, keepdims=True) + EPSILON)


def rms_back(values, scale, d_pre):
    return scale * d_pre - values * (scale * scale * scale) * jnp.mean(
        d_pre * values, axis=-1, keepdims=True
    )


def flip(x, axis, bit):
    if axis == "m":
        axis, bit = {1: "c", 2: "y", 4: "z"}[bit], 1
    size = lax.axis_size(axis)
    return lax.ppermute(x, axis, [(i, i ^ bit) for i in range(size)])


def after(x, *earlier):
    return lax.optimization_barrier((x, earlier))[0]


def dot(a, b):
    return jnp.dot(a, b, preferred_element_type=F32)


def dot_nt(a, b):
    return lax.dot_general(a, b, (((1,), (1,)), ((), ())), preferred_element_type=F32)


def arrays_of(value):
    if hasattr(value, "__dict__"):
        return {k: v for k, v in vars(value).items() if not isinstance(v, (int, str))}
    if isinstance(value, (list, tuple)):
        return [arrays_of(v) for v in value]
    return value


def with_arrays(value, arrays):
    if hasattr(value, "__dict__"):
        fresh = object.__new__(type(value))
        fresh.__dict__.update(vars(value))
        fresh.__dict__.update(arrays)
        return fresh
    if isinstance(value, (list, tuple)):
        return type(value)(with_arrays(v, a) for v, a in zip(value, arrays))
    return arrays


def sync(*values):
    return lax.optimization_barrier(values)


def sync_all(*values):
    leaves, tree = jax.tree.flatten([arrays_of(v) for v in values])
    kept = [k for k, leaf in enumerate(leaves) if isinstance(leaf, jax.Array)]
    for k, new in zip(kept, lax.optimization_barrier([leaves[k] for k in kept])):
        leaves[k] = new
    fresh = jax.tree.unflatten(tree, leaves)
    return tuple(with_arrays(v, a) for v, a in zip(values, fresh))


class Gather:
    def __init__(self, row):
        self.row = row
        self.half = row.shape[0] // 2

    def first(self):
        self.near1, self.near2 = flip(self.row, "m", 2), flip(self.row, "m", 4)
        self.core0 = flip(self.row, "m", 1)

    def second(self, core=True):
        self.top = flip(self.near2[: self.half], "m", 2)
        self.low = flip(self.near1[self.half :], "m", 4)
        if core:
            self.core1, self.core2 = flip(self.near1, "m", 1), flip(self.near2, "m", 1)

    def third(self):
        self.core_top, self.core_low = flip(self.top, "m", 1), flip(self.low, "m", 1)

    def result(self):
        return (
            self.row,
            self.core0,
            self.near1,
            self.core1,
            self.near2,
            self.core2,
            self.top,
            self.low,
            self.core_top,
            self.core_low,
        )


class Reduce:
    def __init__(self, parts):
        self.parts = parts
        self.half = parts[0].shape[0] // 2

    def first(self):
        own, core0, near1, core1, near2, core2, top, low, core_top, core_low = self.parts
        self.own = own.astype(F32) + flip(core0, "m", 1).astype(F32)
        self.near1 = near1.astype(F32) + flip(core1, "m", 1).astype(F32)
        self.near2 = near2.astype(F32) + flip(core2, "m", 1).astype(F32)
        self.top = (top.astype(F32) + flip(core_top, "m", 1).astype(F32)).astype(BF)
        self.low = (low.astype(F32) + flip(core_low, "m", 1).astype(F32)).astype(BF)

    def second(self):
        half = self.half
        got_top = flip(self.top, "m", 2).astype(F32)
        got_low = flip(self.low, "m", 4).astype(F32)
        near1, near2 = self.near1, self.near2
        self.near1 = jnp.concatenate([near1[:half], near1[half:] + got_low], axis=0).astype(BF)
        self.near2 = jnp.concatenate([near2[:half] + got_top, near2[half:]], axis=0).astype(BF)

    def third(self):
        got1, got2 = flip(self.near1, "m", 2), flip(self.near2, "m", 4)
        return self.own + got1.astype(F32) + got2.astype(F32)


def gather_l(x):
    size = lax.axis_size("l")
    if size != 2:
        return lax.all_gather(x, "l", axis=0, tiled=True)
    peer = flip(x, "l", 1)
    first = lax.axis_index("l") == 0
    return jnp.concatenate([jnp.where(first, x, peer), jnp.where(first, peer, x)], axis=0)


def scatter_l(x, axis):
    size = lax.axis_size("l")
    if size != 2:
        return lax.psum_scatter(x.astype(F32), "l", scatter_dimension=axis, tiled=True)
    part = x.shape[axis] // 2
    mine = lax.axis_index("l")
    kept = lax.dynamic_slice_in_dim(x, mine * part, part, axis)
    sent = lax.dynamic_slice_in_dim(x, (1 - mine) * part, part, axis)
    return kept.astype(F32) + flip(sent.astype(BF), "l", 1).astype(F32)


def sum_direct(x, axes, bits):
    total = x
    size = 1
    for axis in axes:
        size *= lax.axis_size(axis)
    for mask in range(1, size):
        if mask & ~bits == 0:
            total = total + lax.ppermute(x, axes, [(i, i ^ mask) for i in range(size)])
    return total


def sum_peers(x):
    size = HALVES * lax.axis_size("l")
    if size == 4:
        return sum_direct(x, ("h", "l"), 3)
    step = 1
    while step < size:
        x = x + lax.ppermute(x, ("h", "l"), [(i, i ^ step) for i in range(size)])
        step *= 2
    return x


def two_parts(values, rows):
    high = values.astype(BF)
    low = (values - high.astype(F32)).astype(BF)
    return jnp.pad(jnp.concatenate([high, low], axis=0), ((0, rows - 4), (0, 0)))[None]


def whole_of(block):
    return block[0:2].astype(F32) + block[2:4].astype(F32)


def tables_kernel(base_ref, fwd_ref, bwd_ref):
    rows, width = fwd_ref.shape[1], fwd_ref.shape[2]
    span = base_ref.shape[1]
    odd = (
        lax.broadcasted_iota(jnp.int32, (rows, width), 0)
        + lax.broadcasted_iota(jnp.int32, (rows, width), 1)
    ) % 2
    sign = (1 - 2 * odd).astype(F32)
    for index in range(4):
        for which, out in ((0, fwd_ref), (1, bwd_ref)):
            line = jnp.broadcast_to(base_ref[pl.ds(which * 4 + index, 1), :], (rows, span))
            rolled = pltpu.roll(line, 0, 1, stride=1, stride_axis=0)[:, :width]
            out[2 * index] = rolled.astype(BF)
            out[2 * index + 1] = (rolled * sign).astype(BF)


def build_tables(filters, h, m):
    seq_len, count = filters.shape
    phi = jnp.transpose(filters.astype(BF).astype(F32))
    zeros = jnp.zeros((count, BLOCK), F32)
    bwd = jnp.concatenate([phi, zeros], axis=1)
    back = jnp.flip(phi, axis=1)
    fwd = jnp.concatenate(
        [
            back[:, seq_len - 1 - BLOCK :],
            jnp.zeros((count, BLOCK), F32),
            back[:, : seq_len - 1 - BLOCK],
        ],
        axis=1,
    )
    rows = []
    for table in (fwd, bwd):
        for rel in range(HALVES):
            first = 12 * (h ^ rel) + (3 * m) // 2
            rows.append(lax.dynamic_slice_in_dim(table, first, 2, 0))
    base = jnp.concatenate(rows, axis=0)
    shape = jax.ShapeDtypeStruct((8, BLOCK, seq_len), BF)
    return pl.pallas_call(
        tables_kernel,
        out_shape=(shape, shape),
        in_specs=[VM],
        out_specs=(VM, VM),
        compiler_params=pltpu.CompilerParams(vmem_limit_bytes=VMEM_LIMIT),
        cost_estimate=pl.CostEstimate(flops=20_000_000, bytes_accessed=5_000_000, transcendentals=0),
    )(base)


def load_rows(refs, scratch, sem):
    started = []
    for j in range(MEMBERS):
        for ref, first, size in used_parts(refs, j, scratch.shape[1]):
            into = scratch.at[j, pl.ds(first, size)]
            started.append(pltpu.make_async_copy(ref, into, sem.at[len(started)]))
            started[-1].start()
    return started


def store_rows(scratch, refs, sem):
    half = scratch.shape[1] // 2
    copies = []
    for j in range(6):
        copies.append((scratch.at[j], refs[j]))
    for j in (6, 7):
        copies.append((scratch.at[j, pl.ds(0, half)], refs[2 * j - 6]))
        copies.append((scratch.at[j, pl.ds(half, half)], refs[2 * j - 5]))
    started = [pltpu.make_async_copy(a, b, sem.at[k]) for k, (a, b) in enumerate(copies)]
    for copy in started:
        copy.start()
    return started


def halves_of(refs, j):
    if j < 6:
        return [(refs[j], 0)]
    return [(refs[2 * j - 6], 0), (refs[2 * j - 5], refs[2 * j - 6].shape[0])]


def used_parts(refs, j, tokens):
    found = []
    for ref, first in halves_of(refs, j):
        size = min(ref.shape[0], tokens - first)
        if size > 0:
            found.append((ref.at[pl.ds(0, size)], first, size))
    return found


def unused_parts(refs, j, tokens):
    found = []
    for ref, first in halves_of(refs, j):
        start = max(tokens - first, 0)
        if start < ref.shape[0]:
            found.append((ref.at[pl.ds(start, ref.shape[0] - start)], ref.shape[0] - start))
    return found


def place(info, r):
    return pl.multiple_of(info[19 + r], 128)


def packed_copies(info, refs, packed, sem, act):
    for j in range(MEMBERS):

        def run(tokens, j=j):
            for k, (ref, first, size) in enumerate(used_parts(refs, j, tokens)):
                into = packed.at[pl.ds(place(info, j) + first, size)]
                act(pltpu.make_async_copy(ref, into, sem.at[j, k]))

        by_length(info[j], run)


def unpacked_copies(info, packed, zeros, refs, sem, act):
    for j in range(MEMBERS):

        def run(tokens, j=j):
            k = 0
            for ref, first, size in used_parts(refs, j, tokens):
                source = packed.at[pl.ds(place(info, j) + first, size)]
                act(pltpu.make_async_copy(source, ref, sem.at[j, k]))
                k += 1
            for ref, size in unused_parts(refs, j, tokens):
                act(pltpu.make_async_copy(zeros.at[pl.ds(0, size)], ref, sem.at[j, k]))
                k += 1

        by_length(info[j], run)


def chunk_copies(info, spec_in, spec, sem, act):
    count, rows = spec.shape[0], spec.shape[1]
    for c in range(count):

        @pl.when(c * rows < info[27])
        def _(c=c):
            act(pltpu.make_async_copy(spec_in.at[pl.ds(c * rows, rows)], spec.at[c], sem.at[c]))


def chunks_of(info, rows):
    return lax.div(info[27] + (rows - 1), rows)


def weight_copies(info, plan, pieces, weight, sem):
    copies = []
    for piece, (rel, l, begin, size, own, source) in zip(pieces, plan):
        l = info[18] if l == "mine" else 1 - info[18] if l == "other" else l
        end = begin + size
        areas = [(0, own, rel * 6 * BLOCK), (own, 2 * own, (rel * 2 + 1) * 3 * BLOCK)]
        if end > 2 * own:
            lags = end - 2 * own
            areas.append((2 * own, end, 12 * BLOCK + rel * 2 * lags))
        for first, last, target in areas:
            low, high = max(first, begin), min(last, end)
            if low < high:
                to = target + l * (last - first) + (low - first)
                if not isinstance(to, int):
                    to = pl.multiple_of(to, 16)
                copies.append(
                    pltpu.make_async_copy(
                        piece.at[pl.ds(source + low - begin, high - low)],
                        weight.at[pl.ds(to, high - low)],
                        sem.at[len(copies)],
                    )
                )
    return copies


def start(copy):
    copy.start()


def finish(copy):
    copy.wait()


def by_length(length, run):
    for tokens in range(128, 513, 128):
        pl.when((length > tokens - 128) & (length <= tokens))(functools.partial(run, tokens))


def combos(info):
    middle = info[8]
    for rel in range(HALVES):
        for sign in range(2):
            for pos, which in enumerate((0, middle, 1)):
                block = (rel * 2 + sign) * 3 + pos
                yield block, rel * 4 + which * 2 + sign, pos % 2


def gain_columns(table_ref, feature, own):
    devices = table_ref.shape[0]
    shift = own.bit_length() - 1
    rows = feature.shape[0]
    device = lax.broadcasted_iota(jnp.int32, (rows, devices), 1)
    chosen = (device == (feature >> shift)).astype(BF)
    found = dot(chosen, table_ref[...].astype(BF))
    lane = lax.broadcasted_iota(jnp.int32, found.shape, 1)
    return jnp.sum(jnp.where(lane == (feature & (own - 1)), found, 0.0), axis=1, keepdims=True)


def feature_places(info, model, lag_span):
    line = lax.broadcasted_iota(jnp.int32, (BLOCK, 1), 0)
    rel = (line >= lag_span).astype(jnp.int32)
    source = lag_span * (MEMBERS * (info[17] ^ rel) + info[9]) + line - rel * lag_span
    return [line + info[8] * BLOCK, line + (1 - info[8]) * BLOCK, source & (model - 1)]


def feature_gains(info, table_ref, model, own, lag_span):
    return [
        gain_columns(table_ref, feature, own) for feature in feature_places(info, model, lag_span)
    ]


def read_lines(own, place_ref, lines, info, gains, seq_len):
    lane = lax.broadcasted_iota(jnp.int32, (1, 128), 1)
    weights = jnp.where(lane == 0, 16.0, jnp.where(lane == 1, 1.0, 0.0))
    total = jnp.int32(0)
    size_l = gains.shape[0] // (HALVES * MEMBERS)
    for k in range(11):
        info[8 + k] = place_ref[k]
    for j in range(MEMBERS):
        line = lines[j, :, :256].astype(F32)[0:1]
        length = jnp.sum(line[:, 128:] * weights).astype(jnp.int32)
        info[j] = length
        info[19 + j] = total
        total = total + ((length + 127) >> 7 << 7)
        for peer in range(HALVES * size_l):
            device = (peer // size_l * MEMBERS + info[9 + j]) * size_l + peer % size_l
            gains[pl.ds(device, 1), pl.ds(0, 2 * own)] = line[
                :, 2 * own * peer : 2 * own * (peer + 1)
            ]
    info[27] = total


def conv_kernel(own, place_ref, table_ref, pick_ref, *refs):
    rows_in = refs[:10]
    spec_out, info, gains = refs[10:13]
    stack, lines, normed, spec, sem_in, sem_line, sem_spec = refs[13:]
    seq_len = stack.shape[1]
    line_copies = []
    for j in range(MEMBERS):
        ref, first = halves_of(rows_in, j)[-1]
        source = ref.at[pl.ds(seq_len - first, lines.shape[1])]
        line_copies.append(pltpu.make_async_copy(source, lines.at[j], sem_line.at[j]))
        line_copies[-1].start()
    loads = load_rows(rows_in, stack, sem_in)
    gains[...] = jnp.zeros_like(gains)
    for copy in line_copies:
        copy.wait()
    read_lines(own, place_ref, lines, info, gains, seq_len)
    for copy in loads:
        copy.wait()
    odd = info[8] == 1

    def spec_copy(r, tokens):
        slot = lax.rem(r, 2)
        return pltpu.make_async_copy(
            spec.at[slot, pl.ds(0, tokens)],
            spec_out.at[pl.ds(place(info, r), tokens)],
            sem_spec.at[slot],
        )

    def row(r, carry):
        slot = lax.rem(r, 2)

        @pl.when(r >= 2)
        def _():
            by_length(info[r - 2], lambda tokens: spec_copy(r - 2, tokens).wait())

        def run(tokens):
            left = stack[r, pl.ds(0, tokens), :BLOCK]
            right = stack[r, pl.ds(0, tokens), BLOCK:]
            normed[pl.ds(0, tokens), :BLOCK] = jnp.where(odd, right, left)
            normed[pl.ds(0, tokens), BLOCK:] = jnp.where(odd, left, right)
            first = min(tokens, BLOCK)
            for block, table, side in combos(info):
                cols = pl.ds(side * BLOCK, BLOCK)
                into = pl.ds(block * BLOCK, BLOCK)
                spec[slot, pl.ds(0, first), into] = dot(
                    table_ref[table, pl.ds(0, first), pl.ds(BLOCK, first)],
                    normed[pl.ds(0, first), cols],
                ).astype(BF)
                if tokens > BLOCK:
                    rest = pl.ds(0, tokens - BLOCK)
                    spec[slot, pl.ds(BLOCK, tokens - BLOCK), into] = dot(
                        table_ref[table, rest, pl.ds(0, tokens)], normed[pl.ds(0, tokens), cols]
                    ).astype(BF)
            lagged = None
            for lag in range(LAGS):
                moved = dot(normed[pl.ds(0, tokens)], pick_ref[lag])
                if lag:
                    moved = jnp.concatenate(
                        [jnp.zeros((lag, BLOCK), F32), moved[: tokens - lag]], axis=0
                    )
                lagged = moved if lagged is None else lagged + moved
            spec[slot, pl.ds(0, tokens), pl.ds(12 * BLOCK, BLOCK)] = lagged.astype(BF)
            spec_copy(r, tokens).start()

        by_length(info[r], run)
        return carry

    lax.fori_loop(0, MEMBERS, row, 0)
    for r in (MEMBERS - 2, MEMBERS - 1):
        by_length(info[r], lambda tokens, r=r: spec_copy(r, tokens).wait())


def row_shapes(seq_len, model):
    whole = jax.ShapeDtypeStruct((seq_len, model), BF)
    half = jax.ShapeDtypeStruct((seq_len // 2, model), BF)
    return (whole,) * 6 + (half,) * 4


def params(flops, data):
    return dict(
        compiler_params=pltpu.CompilerParams(vmem_limit_bytes=VMEM_LIMIT),
        cost_estimate=pl.CostEstimate(flops=flops, bytes_accessed=data, transcendentals=0),
    )


def conv_call(own, devices, place, table, pick, rows, seq_len):
    model = rows[0].shape[1]
    features = 13 * BLOCK
    return pl.pallas_call(
        functools.partial(conv_kernel, own),
        out_shape=(
            jax.ShapeDtypeStruct((MEMBERS * seq_len, features), BF),
            jax.ShapeDtypeStruct((32,), jnp.int32),
            jax.ShapeDtypeStruct((devices, 128), F32),
        ),
        in_specs=[SM, VM, VM] + [ANY] * 10,
        out_specs=(ANY, SM, VM),
        scratch_shapes=[
            pltpu.VMEM((MEMBERS, seq_len, model), BF),
            pltpu.VMEM((MEMBERS, 16, model), BF),
            pltpu.VMEM((seq_len, model), BF),
            pltpu.VMEM((2, seq_len, features), BF),
            pltpu.SemaphoreType.DMA((10,)),
            pltpu.SemaphoreType.DMA((MEMBERS,)),
            pltpu.SemaphoreType.DMA((2,)),
        ],
        **params(5_000_000_000, 20_000_000),
    )(place, table, pick, *rows)


def mix_kernel(plan, own, lag_span, info, gain_ref, lag_ref, spec_in, *refs):
    pieces, refs = refs[: len(plan)], refs[len(plan) :]
    parts_out = refs[:10]
    weight, spec, parts, zeros, sem_in, sem_out, sem_spec = refs[10:]
    weight[pl.ds(12 * BLOCK, BLOCK)] = lag_ref[...]
    copies = weight_copies(info, plan, pieces, weight, sem_in)
    for copy in copies:
        copy.start()
    chunk_copies(info, spec_in, spec, sem_spec, start)
    zeros[...] = jnp.zeros_like(zeros)
    rows = spec.shape[1]
    for copy in copies:
        copy.wait()
    columns = feature_gains(info, gain_ref, weight.shape[1], own, lag_span)
    for block in range(weight.shape[0] // BLOCK):
        at = pl.ds(block * BLOCK, BLOCK)
        column = columns[2 if block == 12 else block % 3 % 2]
        weight[at] = (weight[at].astype(F32) * column).astype(BF)

    def chunk(c, carry):
        here = pl.ds(pl.multiple_of(c * rows, rows), rows)
        pltpu.make_async_copy(spec_in.at[here], spec.at[c], sem_spec.at[c]).wait()
        parts[here] = dot(spec[c], weight[...]).astype(BF)
        return carry

    lax.fori_loop(0, chunks_of(info, rows), chunk, 0)
    unpacked_copies(info, parts, zeros, parts_out, sem_out, start)
    unpacked_copies(info, parts, zeros, parts_out, sem_out, finish)


def mix_call(info, plan, own, lag_span, gain, lag_weight, spec, pieces):
    tokens, features = spec.shape
    model = pieces[0].shape[-1]
    seq_len = tokens // MEMBERS
    return pl.pallas_call(
        functools.partial(mix_kernel, plan, own, lag_span),
        out_shape=row_shapes(seq_len, model),
        in_specs=[SM, VM, VM, ANY] + [ANY] * len(plan),
        out_specs=(ANY,) * 10,
        scratch_shapes=[
            pltpu.VMEM((features, model), BF),
            pltpu.VMEM((MEMBERS, seq_len, features), BF),
            pltpu.VMEM((tokens, model), BF),
            pltpu.VMEM((seq_len, model), BF),
            pltpu.SemaphoreType.DMA((3 * len(plan),)),
            pltpu.SemaphoreType.DMA((MEMBERS, 3)),
            pltpu.SemaphoreType.DMA((MEMBERS,)),
        ],
        **params(8_000_000_000, 30_000_000),
    )(info, gain, lag_weight, spec, *pieces)


def back_conv_kernel(plan, info, table_ref, pick_ref, lag_ref, *refs):
    pieces, refs = refs[: len(plan)], refs[len(plan) :]
    rows_in, parts_out = refs[:10], refs[10:20]
    d_mix, d_spec, parts, weight, sem_in, sem_out, sem_w = refs[20:]
    packed_copies(info, rows_in, d_mix, sem_in, start)
    weight[pl.ds(12 * BLOCK, BLOCK)] = lag_ref[...]
    copies = weight_copies(info, plan, pieces, weight, sem_w)
    for copy in copies:
        copy.start()
    _, seq_len, model = parts.shape
    features = d_spec.shape[1]
    odd = info[8] == 1
    packed_copies(info, rows_in, d_mix, sem_in, finish)
    for copy in copies:
        copy.wait()

    def chunk(c, carry):
        here = pl.ds(pl.multiple_of(c * seq_len, seq_len), seq_len)
        dm = d_mix[here]
        for block in range(features // BLOCK):
            cols = pl.ds(block * BLOCK, BLOCK)
            d_spec[here, cols] = dot_nt(dm, weight[cols]).astype(BF)
        return carry

    lax.fori_loop(0, chunks_of(info, seq_len), chunk, 0)

    def row(r, carry):
        at_row = place(info, r)

        def run(tokens):
            here = pl.ds(at_row, tokens)
            first = min(tokens, BLOCK)
            sides = [[None, None], [None, None]]
            for block, table, side in combos(info):
                cols = pl.ds(block * BLOCK, BLOCK)
                term = dot(table_ref[table, pl.ds(0, first), pl.ds(0, tokens)], d_spec[here, cols])
                sides[side][0] = term if sides[side][0] is None else sides[side][0] + term
                if tokens > BLOCK:
                    rest = pl.ds(0, tokens - BLOCK)
                    term = dot(
                        table_ref[table, rest, rest],
                        d_spec[pl.ds(at_row + BLOCK, tokens - BLOCK), cols],
                    )
                    sides[side][1] = term if sides[side][1] is None else sides[side][1] + term
            d_lag = d_spec[here, pl.ds(12 * BLOCK, BLOCK)]
            back = None
            for lag in range(LAGS):
                moved = dot_nt(d_lag, pick_ref[lag])
                if lag:
                    moved = jnp.concatenate(
                        [moved[lag:], jnp.zeros((lag, model), F32)], axis=0
                    )
                back = moved if back is None else back + moved
            for begin in range(0, tokens, BLOCK):
                size = min(BLOCK, tokens - begin)
                k = begin // BLOCK
                at = pl.ds(begin, size)
                d_a = sides[0][k] + back[begin : begin + size, :BLOCK]
                d_b = sides[1][k] + back[begin : begin + size, BLOCK:]
                left, right = jnp.where(odd, d_b, d_a), jnp.where(odd, d_a, d_b)
                parts[r, at, :BLOCK] = left.astype(BF)
                parts[r, at, BLOCK:] = right.astype(BF)
            if tokens < parts.shape[1]:
                rest = parts.shape[1] - tokens
                parts[r, pl.ds(tokens, rest)] = jnp.zeros((rest, model), BF)

        by_length(info[r], run)
        return carry

    lax.fori_loop(0, MEMBERS, row, 0)
    for copy in store_rows(parts, parts_out, sem_out):
        copy.wait()


def back_conv_call(info, plan, table, pick, lag_weight, pieces, rows):
    seq_len, model = rows[0].shape
    features = 13 * BLOCK
    return pl.pallas_call(
        functools.partial(back_conv_kernel, plan),
        out_shape=row_shapes(seq_len, model),
        in_specs=[SM, VM, VM, VM] + [ANY] * (10 + len(plan)),
        out_specs=(ANY,) * 10,
        scratch_shapes=[
            pltpu.VMEM((MEMBERS * seq_len, model), BF),
            pltpu.VMEM((MEMBERS * seq_len, features), BF),
            pltpu.VMEM((MEMBERS, seq_len, model), BF),
            pltpu.VMEM((features, model), BF),
            pltpu.SemaphoreType.DMA((MEMBERS, 2)),
            pltpu.SemaphoreType.DMA((10,)),
            pltpu.SemaphoreType.DMA((3 * len(plan),)),
        ],
        **params(12_000_000_000, 20_000_000),
    )(info, table, pick, lag_weight, *pieces, *rows)


def spread(value, feature, model):
    lane = lax.broadcasted_iota(jnp.int32, (value.shape[0], model), 1)
    return jnp.sum(jnp.where(lane == feature, value, 0.0), axis=0, keepdims=True)


def grad_kernel(plan, size_l, gain_own, lags, cuts, info, gain_ref, lag_ref, spec_in, *refs):
    pieces, refs = refs[: len(plan)], refs[len(plan) :]
    rows_in, refs = refs[:10], refs[10:]
    count = len(cuts)
    outs, gain_out, refs = refs[:count], refs[count], refs[count + 1 :]
    shares, d_mix, spec, total, weight, sem_in, sem_spec, sem_w, sem_out = refs
    features = total.shape[1]
    model = total.shape[0]
    rows = spec.shape[1]
    own = 3 * BLOCK // size_l

    def share_of(rel, l):
        return rel * size_l + (info[18] ^ l if size_l == 2 else l)

    packed_copies(info, rows_in, d_mix, sem_in, start)
    chunk_copies(info, spec_in, spec, sem_spec, start)
    weight[pl.ds(12 * BLOCK, BLOCK)] = lag_ref[...]
    weights = weight_copies(info, plan, pieces, weight, sem_w)
    for copy in weights:
        copy.start()
    total[...] = jnp.zeros_like(total)
    packed_copies(info, rows_in, d_mix, sem_in, finish)

    def chunk(c, carry):
        base = pl.multiple_of(c * rows, rows)
        here = pl.ds(base, rows)
        pltpu.make_async_copy(spec_in.at[here], spec.at[c], sem_spec.at[c]).wait()
        for tile in range(0, rows, 128):

            @pl.when(base + tile >= info[27])
            def _(tile=tile):
                spec[c, pl.ds(tile, 128)] = jnp.zeros((128, features), BF)
                d_mix[pl.ds(base + tile, 128)] = jnp.zeros((128, d_mix.shape[1]), BF)

        dm_t = jnp.transpose(d_mix[here].astype(F32)).astype(BF)
        for block in range(features // BLOCK):
            cols = pl.ds(block * BLOCK, BLOCK)
            total[:, cols] += dot(dm_t, spec[c, :, cols])
        return carry

    lax.fori_loop(0, chunks_of(info, rows), chunk, 0)
    for copy in weights:
        copy.wait()
    lag_span = lags * size_l
    columns = feature_gains(info, gain_ref, model, gain_own, lag_span)
    places = feature_places(info, model, lag_span)
    sums = [None, None, None]
    for block in range(features // BLOCK):
        kind = 2 if block == 12 else block % 3 % 2
        value = jnp.transpose(total[:, pl.ds(block * BLOCK, BLOCK)])
        part = jnp.sum(
            value * weight[pl.ds(block * BLOCK, BLOCK)].astype(F32), axis=1, keepdims=True
        )
        sums[kind] = part if sums[kind] is None else sums[kind] + part
        value = (value * columns[kind]).astype(BF)
        if block < 12:
            rel, branch, first = block // 6, block // 3 % 2, block % 3 * BLOCK
            at = first
            while at < first + BLOCK:
                l, inside = at // own, at % own
                size = min(own - inside, first + BLOCK - at)
                shares[share_of(rel, l), pl.ds(branch * own + inside, size)] = value[
                    at - first : at - first + size
                ]
                at += size
        else:
            for rel in range(HALVES):
                for l in range(size_l):
                    at = (rel * size_l + l) * lags
                    shares[share_of(rel, l), pl.ds(2 * own, lags)] = value[at : at + lags]
    copies = []
    for out, parts in zip(outs, cuts):
        at = 0
        for k, a, b in parts:
            source, into = shares.at[k, pl.ds(a, b - a)], out.at[pl.ds(at, b - a)]
            if len(parts) == 1:
                into = out
            copies.append(pltpu.make_async_copy(source, into, sem_out.at[len(copies)]))
            copies[-1].start()
            at += b - a
    gain_out[...] = jnp.zeros_like(gain_out)
    for kind in range(3):
        gain_out[0:1] += spread(sums[kind], places[kind], model)
    for copy in copies:
        copy.wait()


def grad_call(info, plan, gain_own, gain, lag_weight, spec, pieces, rows, size_l, lags, cuts):
    seq_len, model = rows[0].shape
    tokens, features = spec.shape
    share_rows = 6 * BLOCK // size_l + lags
    shapes = tuple(
        jax.ShapeDtypeStruct((sum(b - a for _, a, b in parts), model), BF) for parts in cuts
    )
    return pl.pallas_call(
        functools.partial(grad_kernel, plan, size_l, gain_own, lags, cuts),
        out_shape=shapes + (jax.ShapeDtypeStruct((8, model), F32),),
        in_specs=[SM, VM, VM] + [ANY] * (11 + len(plan)),
        out_specs=(ANY,) * len(shapes) + (VM,),
        scratch_shapes=[
            pltpu.VMEM((HALVES * size_l, share_rows, model), BF),
            pltpu.VMEM((tokens, model), BF),
            pltpu.VMEM((MEMBERS, seq_len, features), BF),
            pltpu.VMEM((model, features), F32),
            pltpu.VMEM((features, model), BF),
            pltpu.SemaphoreType.DMA((MEMBERS, 2)),
            pltpu.SemaphoreType.DMA((MEMBERS,)),
            pltpu.SemaphoreType.DMA((3 * len(plan),)),
            pltpu.SemaphoreType.DMA((sum(len(parts) for parts in cuts),)),
        ],
        **params(8_000_000_000, 30_000_000),
    )(info, gain, lag_weight, spec, *pieces, *rows)


def mlp_kernel(info, normed_ref, d_out_ref, *refs):
    packs = refs[:10]
    wide_out, d_normed_out, mlp_out = refs[10:13], refs[13], refs[14]
    held, wide, sem, sem_out = refs[15:]
    model = normed_ref.shape[1]
    devices, blocks, _, _ = held.shape
    count = blocks // 3
    size_l = devices // (HALVES * MEMBERS)
    half = HALVES * size_l // 2
    copies = []
    for j in range(MEMBERS):
        for ref, first in halves_of(packs, j):
            first = first // blocks
            for k in range(ref.shape[0] // blocks):
                rel, l = (first + k) // size_l, (first + k) % size_l
                l = info[18] ^ l if size_l == 2 else l
                device = ((info[17] ^ rel) * MEMBERS + info[9 + j]) * size_l + l
                source = ref.at[pl.ds(k * blocks, blocks)]
                copies.append(pltpu.make_async_copy(source, held.at[device], sem.at[len(copies)]))
    for copy in copies:
        copy.start()
    for copy in copies:
        copy.wait()
    root, cubic = 0.7978845608028654, 0.044715
    out_copies = []
    for s in range(count):
        cols = pl.ds(s * model, model)
        normed, d_out = normed_ref[...], d_out_ref[...]
        gate_s = held[:, s].reshape(model, model)
        up_s = held[:, count + s].reshape(model, model)
        pre = dot(normed, gate_s)
        upward = dot(normed, up_s)
        share = devices // count
        down_s = held[pl.ds(s * share, share), 2 * count :].reshape(model, model)
        d_hidden = dot_nt(d_out, down_s)
        square = pre * pre
        tanh = jnp.tanh(root * pre * (1.0 + cubic * square))
        half = 0.5 * (1.0 + tanh)
        slope = half + 0.5 * pre * (1.0 - tanh * tanh) * (root * (1.0 + 3.0 * cubic * square))
        active = pre * half
        hidden = (active * upward).astype(BF)
        d_gate = (d_hidden * upward * slope).astype(BF)
        d_up = (d_hidden * active).astype(BF)
        for k, value in enumerate((hidden, d_gate, d_up)):
            wide[k, :, cols] = value
            copy = pltpu.make_async_copy(
                wide.at[k, :, cols], wide_out[k].at[:, cols], sem_out.at[k, s]
            )
            copy.start()
            out_copies.append(copy)
        back = dot_nt(d_gate, gate_s) + dot_nt(d_up, up_s)
        ahead = dot(hidden, down_s)
        if s == 0:
            d_normed_out[...] = back
            mlp_out[...] = ahead
        else:
            d_normed_out[...] += back
            mlp_out[...] += ahead
    for copy in out_copies:
        copy.wait()


def mlp_call(info, normed, d_out, packs, devices):
    seq_len, model = normed.shape
    blocks = packs[0].shape[0] * MEMBERS // devices
    own = packs[0].shape[1]
    inner = blocks // 3 * model
    wide = jax.ShapeDtypeStruct((seq_len, inner), BF)
    whole = jax.ShapeDtypeStruct((seq_len, model), F32)
    count = inner // model
    return pl.pallas_call(
        mlp_kernel,
        out_shape=(wide, wide, wide, whole, whole),
        in_specs=[SM, VM, VM] + [ANY] * 10,
        out_specs=(ANY, ANY, ANY, VM, VM),
        scratch_shapes=[
            pltpu.VMEM((devices, blocks, own, model), BF),
            pltpu.VMEM((3, seq_len, inner), BF),
            pltpu.SemaphoreType.DMA((devices,)),
            pltpu.SemaphoreType.DMA((3, count)),
        ],
        **params(6_500_000_000, 16_000_000),
    )(info, normed, d_out, *packs)


def mlp_grad_kernel(normed_ref, d_out_ref, hidden, d_gate, d_up, out, wide, total, sem, sem_out):
    model = normed_ref.shape[1]
    inner = wide.shape[2]
    count = inner // model
    groups, size_l, _, blocks, own, _ = total.shape
    copies = [
        pltpu.make_async_copy(source, wide.at[k], sem.at[k])
        for k, source in enumerate((d_gate, d_up, hidden))
    ]
    for copy in copies:
        copy.start()

    def turned(value):
        return jnp.transpose(value.astype(F32)).astype(BF)

    normed_t = turned(normed_ref[...])
    for k in range(2):
        copies[k].wait()
        for s in range(count):
            value = dot(normed_t, wide[k, :, pl.ds(s * model, model)]).astype(BF)
            value = value.reshape(HALVES, groups, size_l, own, model)
            for h in range(HALVES):
                total[:, :, h, k * count + s] = value[h]
    copies[2].wait()
    share = HALVES * groups // count
    for s in range(count):
        value = dot(turned(wide[2, :, pl.ds(s * model, model)]), d_out_ref[...]).astype(BF)
        h, at = s * share // groups, s * share % groups
        total[pl.ds(at, share), :, h, 2 * count :] = value.reshape(
            share, size_l, count, own, model
        )
    copy = pltpu.make_async_copy(total, out, sem_out)
    copy.start()
    copy.wait()


def mlp_grad_call(normed, d_out, hidden, d_gate, d_up, size_l):
    seq_len, inner = hidden.shape
    model = normed.shape[1]
    count = inner // model
    own = model // (HALVES * MEMBERS * size_l)
    shape = (MEMBERS, size_l, HALVES, 3 * count, own, model)
    return pl.pallas_call(
        mlp_grad_kernel,
        out_shape=jax.ShapeDtypeStruct(shape, BF),
        in_specs=[VM, VM, ANY, ANY, ANY],
        out_specs=ANY,
        scratch_shapes=[
            pltpu.VMEM((3, seq_len, inner), BF),
            pltpu.VMEM(shape, BF),
            pltpu.SemaphoreType.DMA((3,)),
            pltpu.SemaphoreType.DMA,
        ],
        **params(3_200_000_000, 14_000_000),
    )(normed, d_out, hidden, d_gate, d_up)


def body(
    inputs,
    cotangent,
    lengths,
    filters,
    gain_first,
    mix_plus,
    mix_minus,
    auto_weight,
    gain_second,
    w_gate,
    w_upward,
    w_down,
):
    _, seq_len, model = inputs.shape
    size_l = lax.axis_size("l")
    n = HALVES * MEMBERS * size_l
    h, m, l = lax.axis_index("h"), lax.axis_index(GROUP), lax.axis_index("l")
    me = (h * MEMBERS + m) * size_l + l
    own = gain_first.shape[0]
    inner = w_gate.shape[1]
    count = inner // model

    def blocks(w):
        return jnp.transpose(w.astype(BF).reshape(own, count, model), (1, 0, 2))

    pack = jnp.concatenate(
        [blocks(w_gate), blocks(w_upward), w_down.astype(BF).reshape(count, own, model)], axis=0
    )
    pack_rows = 3 * count * own
    plus, minus, auto = mix_plus.astype(BF), mix_minus.astype(BF), auto_weight.astype(BF)
    own_rows, lag_rows = plus.shape[0], auto.shape[0]
    share_rows = 2 * own_rows + lag_rows
    sizes, cuts = [], [0]
    if size_l == 2:
        a, b = own_rows * 13 // 24, own_rows // 3
        chunks = [
            pack.reshape(pack_rows, model),
            plus[:a],
            jnp.concatenate([plus[a:], minus[:b]], axis=0),
            jnp.concatenate([minus[b:], auto], axis=0),
        ]
        cuts = [0, 0, a, own_rows + b, share_rows]
        sizes = [part.shape[0] for part in chunks]
    far, pairs = [None] * 4, [None] * 5

    def cross(k):
        if size_l == 2:
            far[k] = flip(chunks[k], "h", 1)

    def cross_l(k):
        if size_l == 2:
            both = ([chunks[k]] if k < 4 else []) + ([far[k - 1]] if k else [])
            pairs[k] = flip(jnp.concatenate(both, axis=0) if len(both) > 1 else both[0], "l", 1)

    x = inputs[0]
    scale_one = rms_scale(x)
    pre_one = x * scale_one
    gains = jnp.concatenate([gain_first.astype(BF), gain_second.astype(BF)]).astype(F32)
    peers = HALVES * size_l
    here = lax.broadcasted_iota(jnp.int32, (peers, 1), 0) == h * size_l + l
    gains = sum_peers(jnp.where(here, gains[None], 0.0).reshape(1, -1))[0]
    line = jnp.concatenate(
        [
            gains.astype(BF),
            (lengths // 16).astype(BF),
            (lengths % 16).astype(BF),
            jnp.zeros((model - 2 * own * peers - 2,), BF),
        ]
    )
    below = lax.broadcasted_iota(jnp.int32, (32, 1), 0) == 0
    below = jnp.where(below, line[None, :], 0.0).astype(BF)
    row = Gather(jnp.concatenate([pre_one.astype(BF), below], axis=0))

    col = lax.broadcasted_iota(jnp.int32, (LAGS, model, BLOCK), 2)
    feature = lax.broadcasted_iota(jnp.int32, (LAGS, model, BLOCK), 1)
    feature = (feature + (m % 2) * BLOCK) % model
    lag = lax.broadcasted_iota(jnp.int32, (LAGS, model, BLOCK), 0)
    lag_span = lag_rows * size_l
    rel = col // lag_span
    source = lag_span * (MEMBERS * (h ^ rel) + m) + col % lag_span
    pick = ((rel < 2) & (source == lag * model + feature)).astype(BF)

    members = m ^ lax.iota(jnp.int32, MEMBERS)
    place = jnp.concatenate([jnp.stack([m % 2]), members, jnp.stack([h, l])])
    cross(0)
    cross_l(0)
    if size_l == 2:
        row.row, far[0], pairs[0], *chunks[1:] = sync_all(row.row, far[0], pairs[0], *chunks[1:])
    cross(1)
    cross_l(1)
    row.first()
    fwd_table, bwd_table = build_tables(filters, h, m)

    far, pairs, row, fwd_table, pick, place = sync_all(far, pairs, row, fwd_table, pick, place)
    if size_l == 2:
        *chunks[2:], far[1] = sync_all(*chunks[2:], far[1])
    cross(2)
    cross_l(2)
    row.second(core=False)
    row.core1 = flip(row.near1, "m", 1)

    far, pairs, row = sync_all(far, pairs, row)
    if size_l == 2:
        chunks[3], far[2] = sync_all(chunks[3], far[2])
    cross(3)
    cross_l(3)
    row.third()
    row.core2 = flip(row.near2, "m", 1)
    x_rows = row.result()
    spec, info, gains = conv_call(own, n, place, fwd_table, pick, x_rows, seq_len)

    far, pairs, gains, spec = sync_all(far, pairs, gains, spec)
    cross_l(4)
    if size_l == 2:
        held = [chunks[0], pairs[0], far[0], pairs[1][sizes[1] :]]
    else:
        held = [lax.all_gather(part, "l", axis=0) for part in (pack, flip(pack, "h", 1))]
    pack = Gather(jnp.concatenate(held, axis=0).reshape(-1, own, model))
    pack.first()

    pairs, gains, spec = sync_all(pairs, gains, spec)
    gain_one = gains[:, :own].reshape(1, model)
    gain_two = gains[:, own : 2 * own].reshape(1, model)
    plan, pieces = [], []
    if size_l == 2:
        for k in (1, 2, 3):
            at, size = cuts[k], sizes[k]
            plan.append((0, "mine", at, size, own_rows, 0))
            plan.append((1, "mine", at, size, own_rows, 0))
            plan.append((0, "other", at, size, own_rows, 0))
            plan.append((1, "other", at, size, own_rows, sizes[k + 1] if k < 3 else 0))
            pieces += [chunks[k], far[k], pairs[k], pairs[k + 1]]
        lag_weight = jnp.zeros((BLOCK, model), BF)
    else:
        share = jnp.concatenate([plus, minus, auto], axis=0)
        shares = lax.all_gather(share, ("h", "l"), axis=0)
        shares = shares.reshape((HALVES, size_l) + share.shape)
        lag_weight = []
        for rel in range(HALVES):
            half = lax.dynamic_index_in_dim(shares, h ^ rel, 0, keepdims=False)
            lag_weight.append(half[:, 2 * own_rows :])
            for k in range(size_l):
                plan.append((rel, k, 0, 2 * own_rows, own_rows, 0))
                pieces.append(half[k, : 2 * own_rows])
        lag_weight = jnp.stack(lag_weight).reshape(HALVES * lag_span, model)
        lag_weight = jnp.pad(lag_weight, ((0, BLOCK - HALVES * lag_span), (0, 0)))
    plan = tuple(plan)
    mixed = Reduce(mix_call(info, plan, own, lag_span, gains, lag_weight, spec, pieces))

    mixed, pack = sync_all(mixed, pack)
    mixed.first()
    mixed = sync_all(mixed)[0]
    mixed.second()
    mixed, pack = sync_all(mixed, pack)
    mixed = mixed.third()
    pack.second()
    mixed, pack = sync_all(mixed, pack)
    pack.third()

    keep = lax.broadcasted_iota(jnp.int32, (seq_len, 1), 0) < lengths[0]
    middle = x + mixed
    scale_two = rms_scale(middle)
    pre_two = middle * scale_two
    normed_two = (pre_two * gain_two).astype(BF)
    d_out = jnp.where(keep, cotangent[0], 0.0)
    d_out_b = d_out.astype(BF)
    hidden, d_gate, d_up, d_normed_two, mlp_out = mlp_call(
        info, normed_two, d_out_b, pack.result(), n
    )
    d_middle = d_out + rms_back(middle, scale_two, d_normed_two * gain_two)

    row = Gather(d_middle.astype(BF))
    row.first()

    mlp = mlp_grad_call(normed_two, d_out_b, hidden, d_gate, d_up, size_l)

    row, mlp = sync_all(row, mlp)
    row.second()
    output = jnp.where(keep, middle + mlp_out, 0.0)
    grad_gain_two = jnp.sum(d_normed_two * pre_two, axis=0, keepdims=True)

    row, grad_gain_two, mlp = sync_all(row, grad_gain_two, mlp)
    mlp = lax.psum_scatter(mlp, GROUP, scatter_dimension=0)
    row.third()
    d_rows = row.result()
    if size_l == 2:
        cut = share_rows * 5 // 8 - 14
        cuts = (
            ((3, 0, cut),),
            ((3, cut, share_rows), (1, 0, share_rows)),
            ((2, 0, cut),),
            ((2, cut, share_rows),),
            ((0, 0, share_rows),),
        )
    else:
        cuts = tuple(((k, 0, share_rows),) for k in range(HALVES * size_l))
    *grad_mix, gain_mix = grad_call(
        info, plan, own, gains, lag_weight, spec, pieces, d_rows, size_l, lag_rows, cuts
    )

    grad_mix, d_rows = sync_all(grad_mix, d_rows)
    grad_gains = jnp.concatenate([gain_mix[0:1], grad_gain_two], axis=0)
    grad_gains = sum_direct(grad_gains, GROUP, 3)
    grad_gains = sum_direct(grad_gains, GROUP, 4)
    if size_l == 2:
        got_far, got_rest = flip(grad_mix[0], "l", 1), flip(grad_mix[1], "l", 1)
        d_rows, got_far, grad_gains = sync_all(d_rows, got_far, grad_gains)
        back = [flip((grad_mix[2].astype(F32) + got_far.astype(F32)).astype(BF), "h", 1)]
    d_normed = Reduce(back_conv_call(info, plan, bwd_table, pick, lag_weight, pieces, d_rows))

    if size_l == 2:
        d_normed, back, got_rest = sync_all(d_normed, back, got_rest)
    d_normed.first()

    d_normed, grad_gains, mlp = sync_all(d_normed, grad_gains, mlp)
    d_normed.second()
    if size_l == 2:
        got_rest = sync_all(got_rest, d_normed.own)[0]
        left = share_rows - cut
        part = (grad_mix[3].astype(F32) + got_rest[:left].astype(F32)).astype(BF)
        back.append(flip(part, "h", 1))
        other = lax.dynamic_index_in_dim(mlp, 1 - l, 0, keepdims=False)
        mlp = lax.dynamic_index_in_dim(mlp, l, 0, keepdims=False).astype(F32)
        blocks_left = other.shape[0] * other.shape[1]
        other = jnp.concatenate(
            [other.reshape((blocks_left,) + other.shape[2:]), two_parts(grad_gains, own)], axis=0
        )
        other = flip(other, "l", 1)
        grad_gains = grad_gains + whole_of(other[blocks_left])
        mlp = mlp + other[:blocks_left].reshape(mlp.shape).astype(F32)
    else:
        grad_gains = lax.psum(grad_gains, "l")
        mlp = lax.psum_scatter(mlp.astype(F32), "l", scatter_dimension=0)

    if size_l == 2:
        d_normed, grad_gains, mlp, back, got_rest = sync_all(
            d_normed, grad_gains, mlp, back, got_rest
        )
    else:
        d_normed, grad_gains, mlp = sync_all(d_normed, grad_gains, mlp)
    d_normed = d_normed.third()
    if size_l == 2:
        other = lax.dynamic_index_in_dim(mlp, 1 - h, 0, keepdims=False).astype(BF)
        other = flip(jnp.concatenate([other, two_parts(grad_gains, own)], axis=0), "h", 1)
        mlp = lax.dynamic_index_in_dim(mlp, h, 0, keepdims=False) + other[:-1].astype(F32)
        grad_gains = grad_gains + whole_of(other[-1])
    else:
        mlp_far = lax.dynamic_index_in_dim(mlp, 1 - h, 0, keepdims=False).astype(BF)
        mlp_near = lax.dynamic_index_in_dim(mlp, h, 0, keepdims=False)
        mlp = mlp_near + flip(mlp_far, "h", 1).astype(F32)
        grad_gains = grad_gains + flip(grad_gains, "h", 1)
    grad_gains = lax.dynamic_slice_in_dim(grad_gains, me * own, own, 1)
    input_grad = d_middle + rms_back(x, scale_one, d_normed * gain_one)
    if size_l == 2:
        near = grad_mix[4].astype(F32) + got_rest[left:].astype(F32)
        grad_mix = near + jnp.concatenate(back, axis=0).astype(F32)
    else:
        both = jnp.stack(grad_mix).reshape((HALVES, size_l) + grad_mix[0].shape)
        grad_mix = jnp.where(h == 0, both, both[::-1]).reshape((-1,) + both.shape[2:])
        grad_mix = lax.psum_scatter(grad_mix, ("h", "l"), scatter_dimension=0).astype(F32)
    mlp = mlp.reshape(3, count, own, model)
    grad_gate, grad_up = [
        jnp.transpose(mlp[k], (1, 0, 2)).reshape(own, inner) for k in range(2)
    ]
    grad_down = mlp[2].reshape(count * own, model)

    return (
        output[None],
        input_grad[None],
        grad_gains[0],
        grad_mix[:own_rows],
        grad_mix[own_rows : 2 * own_rows],
        grad_mix[2 * own_rows :],
        grad_gains[1],
        grad_gate,
        grad_up,
        grad_down,
    )


def solution(mesh):
    shape = (HALVES, 2, 2, 2, mesh.size // (HALVES * MEMBERS))
    inner = Mesh(mesh.devices.reshape(shape), ALL)
    row, vec, mat = P(ALL, None, None), P(ALL), P(ALL, None)
    in_specs = (row, row, vec, P(), vec, mat, mat, mat, vec, mat, mat, mat)
    out_specs = (row, row, vec, mat, mat, mat, vec, mat, mat, mat)
    return jax.shard_map(body, mesh=inner, in_specs=in_specs, out_specs=out_specs, check_vma=False)
```

```python
import functools

import jax
import jax.numpy as jnp
from jax import lax
from jax.experimental import pallas as pl
from jax.experimental.pallas import tpu as pltpu
from jax.sharding import Mesh, PartitionSpec as P

EPSILON = 1e-05
MEMBERS = 8
HALVES = 2
BLOCK = 256
LAGS = 3
VMEM_LIMIT = 60 * 1024 * 1024
BF = jnp.bfloat16
F32 = jnp.float32
GROUP = ("z", "y", "c")
ALL = ("h",) + GROUP + ("l",)
ANY = pl.BlockSpec(memory_space=pl.ANY)
VM = pl.BlockSpec(memory_space=pltpu.VMEM)
SM = pl.BlockSpec(memory_space=pltpu.SMEM)


def rms_scale(values):
    return lax.rsqrt(jnp.mean(values * values, axis=-1, keepdims=True) + EPSILON)


def rms_back(values, scale, d_pre):
    return scale * d_pre - values * (scale * scale * scale) * jnp.mean(
        d_pre * values, axis=-1, keepdims=True
    )


def flip(x, axis, bit):
    if axis == "m":
        axis, bit = {1: "c", 2: "y", 4: "z"}[bit], 1
    size = lax.axis_size(axis)
    return lax.ppermute(x, axis, [(i, i ^ bit) for i in range(size)])


def after(x, *earlier):
    return lax.optimization_barrier((x, earlier))[0]


def dot(a, b):
    return jnp.dot(a, b, preferred_element_type=F32)


def dot_nt(a, b):
    return lax.dot_general(a, b, (((1,), (1,)), ((), ())), preferred_element_type=F32)


def arrays_of(value):
    if hasattr(value, "__dict__"):
        return {k: v for k, v in vars(value).items() if not isinstance(v, (int, str))}
    if isinstance(value, (list, tuple)):
        return [arrays_of(v) for v in value]
    return value


def with_arrays(value, arrays):
    if hasattr(value, "__dict__"):
        fresh = object.__new__(type(value))
        fresh.__dict__.update(vars(value))
        fresh.__dict__.update(arrays)
        return fresh
    if isinstance(value, (list, tuple)):
        return type(value)(with_arrays(v, a) for v, a in zip(value, arrays))
    return arrays


def sync(*values):
    return lax.optimization_barrier(values)


def sync_all(*values):
    leaves, tree = jax.tree.flatten([arrays_of(v) for v in values])
    kept = [k for k, leaf in enumerate(leaves) if isinstance(leaf, jax.Array)]
    for k, new in zip(kept, lax.optimization_barrier([leaves[k] for k in kept])):
        leaves[k] = new
    fresh = jax.tree.unflatten(tree, leaves)
    return tuple(with_arrays(v, a) for v, a in zip(values, fresh))


class Gather:
    def __init__(self, row):
        self.row = row
        self.half = row.shape[0] // 2

    def first(self):
        self.near1, self.near2 = flip(self.row, "m", 2), flip(self.row, "m", 4)
        self.core0 = flip(self.row, "m", 1)

    def second(self, core=True):
        self.top = flip(self.near2[: self.half], "m", 2)
        self.low = flip(self.near1[self.half :], "m", 4)
        if core:
            self.core1, self.core2 = flip(self.near1, "m", 1), flip(self.near2, "m", 1)

    def third(self):
        self.core_top, self.core_low = flip(self.top, "m", 1), flip(self.low, "m", 1)

    def result(self):
        return (
            self.row,
            self.core0,
            self.near1,
            self.core1,
            self.near2,
            self.core2,
            self.top,
            self.low,
            self.core_top,
            self.core_low,
        )


class Reduce:
    def __init__(self, parts):
        self.parts = parts
        self.half = parts[0].shape[0] // 2

    def first(self):
        own, core0, near1, core1, near2, core2, top, low, core_top, core_low = self.parts
        self.own = own.astype(F32) + flip(core0, "m", 1).astype(F32)
        self.near1 = near1.astype(F32) + flip(core1, "m", 1).astype(F32)
        self.near2 = near2.astype(F32) + flip(core2, "m", 1).astype(F32)
        self.top = (top.astype(F32) + flip(core_top, "m", 1).astype(F32)).astype(BF)
        self.low = (low.astype(F32) + flip(core_low, "m", 1).astype(F32)).astype(BF)

    def second(self):
        half = self.half
        got_top = flip(self.top, "m", 2).astype(F32)
        got_low = flip(self.low, "m", 4).astype(F32)
        near1, near2 = self.near1, self.near2
        self.near1 = jnp.concatenate([near1[:half], near1[half:] + got_low], axis=0).astype(BF)
        self.near2 = jnp.concatenate([near2[:half] + got_top, near2[half:]], axis=0).astype(BF)

    def third(self):
        return self.own, flip(self.near1, "m", 2), flip(self.near2, "m", 4)


def gather_l(x):
    size = lax.axis_size("l")
    if size != 2:
        return lax.all_gather(x, "l", axis=0, tiled=True)
    peer = flip(x, "l", 1)
    first = lax.axis_index("l") == 0
    return jnp.concatenate([jnp.where(first, x, peer), jnp.where(first, peer, x)], axis=0)


def scatter_l(x, axis):
    size = lax.axis_size("l")
    if size != 2:
        return lax.psum_scatter(x.astype(F32), "l", scatter_dimension=axis, tiled=True)
    part = x.shape[axis] // 2
    mine = lax.axis_index("l")
    kept = lax.dynamic_slice_in_dim(x, mine * part, part, axis)
    sent = lax.dynamic_slice_in_dim(x, (1 - mine) * part, part, axis)
    return kept.astype(F32) + flip(sent.astype(BF), "l", 1).astype(F32)


def sum_direct(x, axes, bits):
    total = x
    size = 1
    for axis in axes:
        size *= lax.axis_size(axis)
    for mask in range(1, size):
        if mask & ~bits == 0:
            total = total + lax.ppermute(x, axes, [(i, i ^ mask) for i in range(size)])
    return total


def sum_peers(x):
    size = HALVES * lax.axis_size("l")
    if size == 4:
        return sum_direct(x, ("h", "l"), 3)
    step = 1
    while step < size:
        x = x + lax.ppermute(x, ("h", "l"), [(i, i ^ step) for i in range(size)])
        step *= 2
    return x


def two_parts(values, rows):
    high = values.astype(BF)
    low = (values - high.astype(F32)).astype(BF)
    return jnp.pad(jnp.concatenate([high, low], axis=0), ((0, rows - 4), (0, 0)))[None]


def whole_of(block):
    return block[0:2].astype(F32) + block[2:4].astype(F32)


def tables_kernel(base_ref, fwd_ref, bwd_ref):
    rows, width = fwd_ref.shape[1], fwd_ref.shape[2]
    span = base_ref.shape[1]
    odd = (
        lax.broadcasted_iota(jnp.int32, (rows, width), 0)
        + lax.broadcasted_iota(jnp.int32, (rows, width), 1)
    ) % 2
    sign = (1 - 2 * odd).astype(F32)
    for index in range(4):
        for which, out in ((0, fwd_ref), (1, bwd_ref)):
            line = jnp.broadcast_to(base_ref[pl.ds(which * 4 + index, 1), :], (rows, span))
            rolled = pltpu.roll(line, 0, 1, stride=1, stride_axis=0)[:, :width]
            out[2 * index] = rolled.astype(BF)
            out[2 * index + 1] = (rolled * sign).astype(BF)


def build_tables(filters, h, m):
    seq_len, count = filters.shape
    phi = jnp.transpose(filters.astype(BF).astype(F32))
    zeros = jnp.zeros((count, BLOCK), F32)
    bwd = jnp.concatenate([phi, zeros], axis=1)
    back = jnp.flip(phi, axis=1)
    fwd = jnp.concatenate(
        [
            back[:, seq_len - 1 - BLOCK :],
            jnp.zeros((count, BLOCK), F32),
            back[:, : seq_len - 1 - BLOCK],
        ],
        axis=1,
    )
    rows = []
    for table in (fwd, bwd):
        for rel in range(HALVES):
            first = 12 * (h ^ rel) + (3 * m) // 2
            rows.append(lax.dynamic_slice_in_dim(table, first, 2, 0))
    base = jnp.concatenate(rows, axis=0)
    shape = jax.ShapeDtypeStruct((8, BLOCK, seq_len), BF)
    return pl.pallas_call(
        tables_kernel,
        out_shape=(shape, shape),
        in_specs=[VM],
        out_specs=(VM, VM),
        compiler_params=pltpu.CompilerParams(vmem_limit_bytes=VMEM_LIMIT),
        cost_estimate=pl.CostEstimate(flops=20_000_000, bytes_accessed=5_000_000, transcendentals=0),
    )(base)


def load_rows(refs, scratch, sem):
    started = []
    for j in range(MEMBERS):
        for ref, first, size in used_parts(refs, j, scratch.shape[1]):
            into = scratch.at[j, pl.ds(first, size)]
            started.append(pltpu.make_async_copy(ref, into, sem.at[len(started)]))
            started[-1].start()
    return started


def row_stores(scratch, refs, j, sem):
    copies = []
    for k, (ref, first) in enumerate(halves_of(refs, j)):
        source = scratch.at[j, pl.ds(first, ref.shape[0])]
        copies.append(pltpu.make_async_copy(source, ref, sem.at[j, k]))
    return copies


def halves_of(refs, j):
    if j < 6:
        return [(refs[j], 0)]
    return [(refs[2 * j - 6], 0), (refs[2 * j - 5], refs[2 * j - 6].shape[0])]


def used_parts(refs, j, tokens):
    found = []
    for ref, first in halves_of(refs, j):
        size = min(ref.shape[0], tokens - first)
        if size > 0:
            found.append((ref.at[pl.ds(0, size)], first, size))
    return found


def unused_parts(refs, j, tokens):
    found = []
    for ref, first in halves_of(refs, j):
        start = max(tokens - first, 0)
        if start < ref.shape[0]:
            found.append((ref.at[pl.ds(start, ref.shape[0] - start)], ref.shape[0] - start))
    return found


def place(info, r):
    return pl.multiple_of(info[19 + r], 128)


def packed_copies(info, refs, packed, sem, act):
    for j in range(MEMBERS):

        def run(tokens, j=j):
            for k, (ref, first, size) in enumerate(used_parts(refs, j, tokens)):
                into = packed.at[pl.ds(place(info, j) + first, size)]
                act(pltpu.make_async_copy(ref, into, sem.at[j, k]))

        by_length(info[j], run)


def unpacked_copies(info, packed, zeros, refs, sem, act, low=None, high=None):
    for j in range(MEMBERS):

        def run(tokens, j=j):
            k = 0
            for ref, first, size in used_parts(refs, j, tokens):
                source = packed.at[pl.ds(place(info, j) + first, size)]
                act(pltpu.make_async_copy(source, ref, sem.at[j, k]))
                k += 1
            for ref, size in unused_parts(refs, j, tokens):
                act(pltpu.make_async_copy(zeros.at[pl.ds(0, size)], ref, sem.at[j, k]))
                k += 1

        if low is None:
            by_length(info[j], run)
        else:
            end = info[20 + j]
            pl.when((end > low) & (end <= high))(functools.partial(by_length, info[j], run))


def chunk_copies(info, spec_in, spec, sem, act):
    count, rows = spec.shape[0], spec.shape[1]
    for c in range(count):

        @pl.when(c * rows < info[27])
        def _(c=c):
            act(pltpu.make_async_copy(spec_in.at[pl.ds(c * rows, rows)], spec.at[c], sem.at[c]))


def chunks_of(info, rows):
    return lax.div(info[27] + (rows - 1), rows)


def weight_copies(info, plan, pieces, weight, sem):
    copies = []
    for piece, (rel, l, begin, size, own, source) in zip(pieces, plan):
        l = info[18] if l == "mine" else 1 - info[18] if l == "other" else l
        end = begin + size
        areas = [(0, own, rel * 6 * BLOCK), (own, 2 * own, (rel * 2 + 1) * 3 * BLOCK)]
        if end > 2 * own:
            lags = end - 2 * own
            areas.append((2 * own, end, 12 * BLOCK + rel * 2 * lags))
        for first, last, target in areas:
            low, high = max(first, begin), min(last, end)
            if low < high:
                to = target + l * (last - first) + (low - first)
                if not isinstance(to, int):
                    to = pl.multiple_of(to, 16)
                copies.append(
                    pltpu.make_async_copy(
                        piece.at[pl.ds(source + low - begin, high - low)],
                        weight.at[pl.ds(to, high - low)],
                        sem.at[len(copies)],
                    )
                )
    return copies


def start(copy):
    copy.start()


def finish(copy):
    copy.wait()


def by_length(length, run):
    for tokens in range(128, 513, 128):
        pl.when((length > tokens - 128) & (length <= tokens))(functools.partial(run, tokens))


def combos(info):
    middle = info[8]
    for rel in range(HALVES):
        for sign in range(2):
            for pos, which in enumerate((0, middle, 1)):
                block = (rel * 2 + sign) * 3 + pos
                yield block, rel * 4 + which * 2 + sign, pos % 2


def gain_columns(table_ref, feature, own):
    devices = table_ref.shape[0]
    shift = own.bit_length() - 1
    rows = feature.shape[0]
    device = lax.broadcasted_iota(jnp.int32, (rows, devices), 1)
    chosen = (device == (feature >> shift)).astype(BF)
    found = dot(chosen, table_ref[...].astype(BF))
    lane = lax.broadcasted_iota(jnp.int32, found.shape, 1)
    return jnp.sum(jnp.where(lane == (feature & (own - 1)), found, 0.0), axis=1, keepdims=True)


def feature_places(info, model, lag_span):
    line = lax.broadcasted_iota(jnp.int32, (BLOCK, 1), 0)
    rel = (line >= lag_span).astype(jnp.int32)
    source = lag_span * (MEMBERS * (info[17] ^ rel) + info[9]) + line - rel * lag_span
    return [line + info[8] * BLOCK, line + (1 - info[8]) * BLOCK, source & (model - 1)]


def feature_gains(info, table_ref, model, own, lag_span):
    return [
        gain_columns(table_ref, feature, own) for feature in feature_places(info, model, lag_span)
    ]


def read_lines(own, place_ref, lines, info, gains, seq_len):
    lane = lax.broadcasted_iota(jnp.int32, (1, 128), 1)
    weights = jnp.where(lane == 0, 16.0, jnp.where(lane == 1, 1.0, 0.0))
    total = jnp.int32(0)
    size_l = gains.shape[0] // (HALVES * MEMBERS)
    for k in range(11):
        info[8 + k] = place_ref[k]
    for j in range(MEMBERS):
        line = lines[j, :, :256].astype(F32)[0:1]
        length = jnp.sum(line[:, 128:] * weights).astype(jnp.int32)
        info[j] = length
        info[19 + j] = total
        total = total + ((length + 127) >> 7 << 7)
        for peer in range(HALVES * size_l):
            device = (peer // size_l * MEMBERS + info[9 + j]) * size_l + peer % size_l
            gains[pl.ds(device, 1), pl.ds(0, 2 * own)] = line[
                :, 2 * own * peer : 2 * own * (peer + 1)
            ]
    info[27] = total


def conv_kernel(own, place_ref, table_ref, pick_ref, *refs):
    rows_in = refs[:10]
    spec_out, info, gains = refs[10:13]
    stack, lines, normed, spec, sem_in, sem_line, sem_spec = refs[13:]
    seq_len = stack.shape[1]
    line_copies = []
    for j in range(MEMBERS):
        ref, first = halves_of(rows_in, j)[-1]
        source = ref.at[pl.ds(seq_len - first, lines.shape[1])]
        line_copies.append(pltpu.make_async_copy(source, lines.at[j], sem_line.at[j]))
        line_copies[-1].start()
    loads = load_rows(rows_in, stack, sem_in)
    gains[...] = jnp.zeros_like(gains)
    for copy in line_copies:
        copy.wait()
    read_lines(own, place_ref, lines, info, gains, seq_len)
    for copy in loads:
        copy.wait()
    odd = info[8] == 1

    def spec_copy(r, tokens):
        slot = lax.rem(r, 2)
        return pltpu.make_async_copy(
            spec.at[slot, pl.ds(0, tokens)],
            spec_out.at[pl.ds(place(info, r), tokens)],
            sem_spec.at[slot],
        )

    def row(r, carry):
        slot = lax.rem(r, 2)

        @pl.when(r >= 2)
        def _():
            by_length(info[r - 2], lambda tokens: spec_copy(r - 2, tokens).wait())

        def run(tokens):
            left = stack[r, pl.ds(0, tokens), :BLOCK]
            right = stack[r, pl.ds(0, tokens), BLOCK:]
            normed[pl.ds(0, tokens), :BLOCK] = jnp.where(odd, right, left)
            normed[pl.ds(0, tokens), BLOCK:] = jnp.where(odd, left, right)
            first = min(tokens, BLOCK)
            for block, table, side in combos(info):
                cols = pl.ds(side * BLOCK, BLOCK)
                into = pl.ds(block * BLOCK, BLOCK)
                spec[slot, pl.ds(0, first), into] = dot(
                    table_ref[table, pl.ds(0, first), pl.ds(BLOCK, first)],
                    normed[pl.ds(0, first), cols],
                ).astype(BF)
                if tokens > BLOCK:
                    rest = pl.ds(0, tokens - BLOCK)
                    spec[slot, pl.ds(BLOCK, tokens - BLOCK), into] = dot(
                        table_ref[table, rest, pl.ds(0, tokens)], normed[pl.ds(0, tokens), cols]
                    ).astype(BF)
            lagged = None
            for lag in range(LAGS):
                moved = dot(normed[pl.ds(0, tokens)], pick_ref[lag])
                if lag:
                    moved = jnp.concatenate(
                        [jnp.zeros((lag, BLOCK), F32), moved[: tokens - lag]], axis=0
                    )
                lagged = moved if lagged is None else lagged + moved
            spec[slot, pl.ds(0, tokens), pl.ds(12 * BLOCK, BLOCK)] = lagged.astype(BF)
            spec_copy(r, tokens).start()

        by_length(info[r], run)
        return carry

    lax.fori_loop(0, MEMBERS, row, 0)
    for r in (MEMBERS - 2, MEMBERS - 1):
        by_length(info[r], lambda tokens, r=r: spec_copy(r, tokens).wait())


def row_shapes(seq_len, model):
    whole = jax.ShapeDtypeStruct((seq_len, model), BF)
    half = jax.ShapeDtypeStruct((seq_len // 2, model), BF)
    return (whole,) * 6 + (half,) * 4


def params(flops, data):
    return dict(
        compiler_params=pltpu.CompilerParams(vmem_limit_bytes=VMEM_LIMIT),
        cost_estimate=pl.CostEstimate(flops=flops, bytes_accessed=data, transcendentals=0),
    )


def conv_call(own, devices, place, table, pick, rows, seq_len):
    model = rows[0].shape[1]
    features = 13 * BLOCK
    return pl.pallas_call(
        functools.partial(conv_kernel, own),
        out_shape=(
            jax.ShapeDtypeStruct((MEMBERS * seq_len, features), BF),
            jax.ShapeDtypeStruct((32,), jnp.int32),
            jax.ShapeDtypeStruct((devices, 128), F32),
        ),
        in_specs=[SM, VM, VM] + [ANY] * 10,
        out_specs=(ANY, SM, VM),
        scratch_shapes=[
            pltpu.VMEM((MEMBERS, seq_len, model), BF),
            pltpu.VMEM((MEMBERS, 16, model), BF),
            pltpu.VMEM((seq_len, model), BF),
            pltpu.VMEM((2, seq_len, features), BF),
            pltpu.SemaphoreType.DMA((10,)),
            pltpu.SemaphoreType.DMA((MEMBERS,)),
            pltpu.SemaphoreType.DMA((2,)),
        ],
        **params(5_000_000_000, 20_000_000),
    )(place, table, pick, *rows)


def mix_kernel(plan, own, lag_span, info, gain_ref, lag_ref, spec_in, *refs):
    pieces, refs = refs[: len(plan)], refs[len(plan) :]
    parts_out = refs[:10]
    weight, spec, parts, zeros, sem_in, sem_out, sem_spec = refs[10:]
    weight[pl.ds(12 * BLOCK, BLOCK)] = lag_ref[...]
    copies = weight_copies(info, plan, pieces, weight, sem_in)
    for copy in copies:
        copy.start()
    chunk_copies(info, spec_in, spec, sem_spec, start)
    zeros[...] = jnp.zeros_like(zeros)
    rows = spec.shape[1]
    for copy in copies:
        copy.wait()
    columns = feature_gains(info, gain_ref, weight.shape[1], own, lag_span)
    for block in range(weight.shape[0] // BLOCK):
        at = pl.ds(block * BLOCK, BLOCK)
        column = columns[2 if block == 12 else block % 3 % 2]
        weight[at] = (weight[at].astype(F32) * column).astype(BF)

    def chunk(c, carry):
        here = pl.ds(pl.multiple_of(c * rows, rows), rows)
        pltpu.make_async_copy(spec_in.at[here], spec.at[c], sem_spec.at[c]).wait()
        parts[here] = dot(spec[c], weight[...]).astype(BF)
        unpacked_copies(
            info, parts, zeros, parts_out, sem_out, start, c * rows, c * rows + rows
        )
        return carry

    lax.fori_loop(0, chunks_of(info, rows), chunk, 0)
    unpacked_copies(info, parts, zeros, parts_out, sem_out, finish)


def mix_call(info, plan, own, lag_span, gain, lag_weight, spec, pieces):
    tokens, features = spec.shape
    model = pieces[0].shape[-1]
    seq_len = tokens // MEMBERS
    return pl.pallas_call(
        functools.partial(mix_kernel, plan, own, lag_span),
        out_shape=row_shapes(seq_len, model),
        in_specs=[SM, VM, VM, ANY] + [ANY] * len(plan),
        out_specs=(ANY,) * 10,
        scratch_shapes=[
            pltpu.VMEM((features, model), BF),
            pltpu.VMEM((MEMBERS, seq_len, features), BF),
            pltpu.VMEM((tokens, model), BF),
            pltpu.VMEM((seq_len, model), BF),
            pltpu.SemaphoreType.DMA((3 * len(plan),)),
            pltpu.SemaphoreType.DMA((MEMBERS, 3)),
            pltpu.SemaphoreType.DMA((MEMBERS,)),
        ],
        **params(8_000_000_000, 30_000_000),
    )(info, gain, lag_weight, spec, *pieces)


def back_conv_kernel(plan, info, table_ref, pick_ref, lag_ref, *refs):
    pieces, refs = refs[: len(plan)], refs[len(plan) :]
    rows_in, parts_out = refs[:10], refs[10:20]
    d_mix, d_spec, parts, weight, sem_in, sem_out, sem_w = refs[20:]
    packed_copies(info, rows_in, d_mix, sem_in, start)
    weight[pl.ds(12 * BLOCK, BLOCK)] = lag_ref[...]
    copies = weight_copies(info, plan, pieces, weight, sem_w)
    for copy in copies:
        copy.start()
    _, seq_len, model = parts.shape
    features = d_spec.shape[1]
    odd = info[8] == 1
    packed_copies(info, rows_in, d_mix, sem_in, finish)
    for copy in copies:
        copy.wait()

    def chunk(c, carry):
        here = pl.ds(pl.multiple_of(c * seq_len, seq_len), seq_len)
        dm = d_mix[here]
        for block in range(features // BLOCK):
            cols = pl.ds(block * BLOCK, BLOCK)
            d_spec[here, cols] = dot_nt(dm, weight[cols]).astype(BF)
        return carry

    lax.fori_loop(0, chunks_of(info, seq_len), chunk, 0)

    def row(r, carry):
        at_row = place(info, r)

        def run(tokens):
            here = pl.ds(at_row, tokens)
            first = min(tokens, BLOCK)
            sides = [[None, None], [None, None]]
            for block, table, side in combos(info):
                cols = pl.ds(block * BLOCK, BLOCK)
                term = dot(table_ref[table, pl.ds(0, first), pl.ds(0, tokens)], d_spec[here, cols])
                sides[side][0] = term if sides[side][0] is None else sides[side][0] + term
                if tokens > BLOCK:
                    rest = pl.ds(0, tokens - BLOCK)
                    term = dot(
                        table_ref[table, rest, rest],
                        d_spec[pl.ds(at_row + BLOCK, tokens - BLOCK), cols],
                    )
                    sides[side][1] = term if sides[side][1] is None else sides[side][1] + term
            d_lag = d_spec[here, pl.ds(12 * BLOCK, BLOCK)]
            back = None
            for lag in range(LAGS):
                moved = dot_nt(d_lag, pick_ref[lag])
                if lag:
                    moved = jnp.concatenate(
                        [moved[lag:], jnp.zeros((lag, model), F32)], axis=0
                    )
                back = moved if back is None else back + moved
            for begin in range(0, tokens, BLOCK):
                size = min(BLOCK, tokens - begin)
                k = begin // BLOCK
                at = pl.ds(begin, size)
                d_a = sides[0][k] + back[begin : begin + size, :BLOCK]
                d_b = sides[1][k] + back[begin : begin + size, BLOCK:]
                left, right = jnp.where(odd, d_b, d_a), jnp.where(odd, d_a, d_b)
                parts[r, at, :BLOCK] = left.astype(BF)
                parts[r, at, BLOCK:] = right.astype(BF)
            if tokens < parts.shape[1]:
                rest = parts.shape[1] - tokens
                parts[r, pl.ds(tokens, rest)] = jnp.zeros((rest, model), BF)

        by_length(info[r], run)
        for j in range(MEMBERS):

            @pl.when(r == j)
            def _(j=j):
                for copy in row_stores(parts, parts_out, j, sem_out):
                    copy.start()

        return carry

    lax.fori_loop(0, MEMBERS, row, 0)
    for j in range(MEMBERS):
        for copy in row_stores(parts, parts_out, j, sem_out):
            copy.wait()


def back_conv_call(info, plan, table, pick, lag_weight, pieces, rows):
    seq_len, model = rows[0].shape
    features = 13 * BLOCK
    return pl.pallas_call(
        functools.partial(back_conv_kernel, plan),
        out_shape=row_shapes(seq_len, model),
        in_specs=[SM, VM, VM, VM] + [ANY] * (10 + len(plan)),
        out_specs=(ANY,) * 10,
        scratch_shapes=[
            pltpu.VMEM((MEMBERS * seq_len, model), BF),
            pltpu.VMEM((MEMBERS * seq_len, features), BF),
            pltpu.VMEM((MEMBERS, seq_len, model), BF),
            pltpu.VMEM((features, model), BF),
            pltpu.SemaphoreType.DMA((MEMBERS, 2)),
            pltpu.SemaphoreType.DMA((MEMBERS, 2)),
            pltpu.SemaphoreType.DMA((3 * len(plan),)),
        ],
        **params(12_000_000_000, 20_000_000),
    )(info, table, pick, lag_weight, *pieces, *rows)


def spread(value, feature, model):
    lane = lax.broadcasted_iota(jnp.int32, (value.shape[0], model), 1)
    return jnp.sum(jnp.where(lane == feature, value, 0.0), axis=0, keepdims=True)


def grad_kernel(plan, size_l, gain_own, lags, cuts, info, gain_ref, lag_ref, spec_in, *refs):
    pieces, refs = refs[: len(plan)], refs[len(plan) :]
    rows_in, refs = refs[:10], refs[10:]
    count = len(cuts)
    outs, gain_out, refs = refs[:count], refs[count], refs[count + 1 :]
    shares, d_mix, spec, total, weight, sem_in, sem_spec, sem_w, sem_out = refs
    features = total.shape[1]
    model = total.shape[0]
    rows = spec.shape[1]
    own = 3 * BLOCK // size_l

    def share_of(rel, l):
        return rel * size_l + (info[18] ^ l if size_l == 2 else l)

    packed_copies(info, rows_in, d_mix, sem_in, start)
    chunk_copies(info, spec_in, spec, sem_spec, start)
    weight[pl.ds(12 * BLOCK, BLOCK)] = lag_ref[...]
    weights = weight_copies(info, plan, pieces, weight, sem_w)
    for copy in weights:
        copy.start()
    total[...] = jnp.zeros_like(total)
    packed_copies(info, rows_in, d_mix, sem_in, finish)

    def chunk(c, carry):
        base = pl.multiple_of(c * rows, rows)
        here = pl.ds(base, rows)
        pltpu.make_async_copy(spec_in.at[here], spec.at[c], sem_spec.at[c]).wait()
        for tile in range(0, rows, 128):

            @pl.when(base + tile >= info[27])
            def _(tile=tile):
                spec[c, pl.ds(tile, 128)] = jnp.zeros((128, features), BF)
                d_mix[pl.ds(base + tile, 128)] = jnp.zeros((128, d_mix.shape[1]), BF)

        dm_t = jnp.transpose(d_mix[here].astype(F32)).astype(BF)
        for block in range(features // BLOCK):
            cols = pl.ds(block * BLOCK, BLOCK)
            total[:, cols] += dot(dm_t, spec[c, :, cols])
        return carry

    lax.fori_loop(0, chunks_of(info, rows), chunk, 0)
    for copy in weights:
        copy.wait()
    lag_span = lags * size_l
    columns = feature_gains(info, gain_ref, model, gain_own, lag_span)
    places = feature_places(info, model, lag_span)
    sums = [None, None, None]
    for block in range(features // BLOCK):
        kind = 2 if block == 12 else block % 3 % 2
        value = jnp.transpose(total[:, pl.ds(block * BLOCK, BLOCK)])
        part = jnp.sum(
            value * weight[pl.ds(block * BLOCK, BLOCK)].astype(F32), axis=1, keepdims=True
        )
        sums[kind] = part if sums[kind] is None else sums[kind] + part
        value = (value * columns[kind]).astype(BF)
        if block < 12:
            rel, branch, first = block // 6, block // 3 % 2, block % 3 * BLOCK
            at = first
            while at < first + BLOCK:
                l, inside = at // own, at % own
                size = min(own - inside, first + BLOCK - at)
                shares[share_of(rel, l), pl.ds(branch * own + inside, size)] = value[
                    at - first : at - first + size
                ]
                at += size
        else:
            for rel in range(HALVES):
                for l in range(size_l):
                    at = (rel * size_l + l) * lags
                    shares[share_of(rel, l), pl.ds(2 * own, lags)] = value[at : at + lags]
    copies = []
    for out, parts in zip(outs, cuts):
        at = 0
        for k, a, b in parts:
            source, into = shares.at[k, pl.ds(a, b - a)], out.at[pl.ds(at, b - a)]
            if len(parts) == 1:
                into = out
            copies.append(pltpu.make_async_copy(source, into, sem_out.at[len(copies)]))
            copies[-1].start()
            at += b - a
    gain_out[...] = jnp.zeros_like(gain_out)
    for kind in range(3):
        gain_out[0:1] += spread(sums[kind], places[kind], model)
    for copy in copies:
        copy.wait()


def grad_call(info, plan, gain_own, gain, lag_weight, spec, pieces, rows, size_l, lags, cuts):
    seq_len, model = rows[0].shape
    tokens, features = spec.shape
    share_rows = 6 * BLOCK // size_l + lags
    shapes = tuple(
        jax.ShapeDtypeStruct((sum(b - a for _, a, b in parts), model), BF) for parts in cuts
    )
    return pl.pallas_call(
        functools.partial(grad_kernel, plan, size_l, gain_own, lags, cuts),
        out_shape=shapes + (jax.ShapeDtypeStruct((8, model), F32),),
        in_specs=[SM, VM, VM] + [ANY] * (11 + len(plan)),
        out_specs=(ANY,) * len(shapes) + (VM,),
        scratch_shapes=[
            pltpu.VMEM((HALVES * size_l, share_rows, model), BF),
            pltpu.VMEM((tokens, model), BF),
            pltpu.VMEM((MEMBERS, seq_len, features), BF),
            pltpu.VMEM((model, features), F32),
            pltpu.VMEM((features, model), BF),
            pltpu.SemaphoreType.DMA((MEMBERS, 2)),
            pltpu.SemaphoreType.DMA((MEMBERS,)),
            pltpu.SemaphoreType.DMA((3 * len(plan),)),
            pltpu.SemaphoreType.DMA((sum(len(parts) for parts in cuts),)),
        ],
        **params(8_000_000_000, 30_000_000),
    )(info, gain, lag_weight, spec, *pieces, *rows)


def mlp_kernel(info, gain_ref, x_ref, own_ref, got1_ref, got2_ref, cot_ref, *refs):
    packs, refs = refs[:10], refs[10:]
    wide_out, (normed_ref, d_out_ref, d_middle_out, row_out, output, gain_out) = refs[:3], refs[3:9]
    held, wide, middle_ref, back_ref, ahead_ref, sem, sem_out = refs[9:]
    seq_len, model = x_ref.shape
    devices, blocks, _, _ = held.shape
    count = blocks // 3
    size_l = devices // (HALVES * MEMBERS)
    half = HALVES * size_l // 2
    copies = []
    for j in range(MEMBERS):
        for ref, first in halves_of(packs, j):
            first = first // blocks
            for k in range(ref.shape[0] // blocks):
                rel, l = (first + k) // size_l, (first + k) % size_l
                l = info[18] ^ l if size_l == 2 else l
                device = ((info[17] ^ rel) * MEMBERS + info[9 + j]) * size_l + l
                source = ref.at[pl.ds(k * blocks, blocks)]
                copies.append(pltpu.make_async_copy(source, held.at[device], sem.at[len(copies)]))
    for copy in copies:
        copy.start()
    gain = gain_ref[...]
    middle = x_ref[...] + (
        own_ref[...] + got1_ref[...].astype(F32) + got2_ref[...].astype(F32)
    )
    middle_ref[...] = middle
    scale = rms_scale(middle)
    normed_ref[...] = (middle * scale * gain).astype(BF)
    keep = lax.broadcasted_iota(jnp.int32, (seq_len, 1), 0) < info[0]
    d_out_ref[...] = jnp.where(keep, cot_ref[...], 0.0).astype(BF)
    for copy in copies:
        copy.wait()
    root, cubic = 0.7978845608028654, 0.044715
    out_copies = []
    for s in range(count):
        cols = pl.ds(s * model, model)
        normed, d_out = normed_ref[...], d_out_ref[...]
        gate_s = held[:, s].reshape(model, model)
        up_s = held[:, count + s].reshape(model, model)
        pre = dot(normed, gate_s)
        upward = dot(normed, up_s)
        share = devices // count
        down_s = held[pl.ds(s * share, share), 2 * count :].reshape(model, model)
        d_hidden = dot_nt(d_out, down_s)
        square = pre * pre
        tanh = jnp.tanh(root * pre * (1.0 + cubic * square))
        half = 0.5 * (1.0 + tanh)
        slope = half + 0.5 * pre * (1.0 - tanh * tanh) * (root * (1.0 + 3.0 * cubic * square))
        active = pre * half
        hidden = (active * upward).astype(BF)
        d_gate = (d_hidden * upward * slope).astype(BF)
        d_up = (d_hidden * active).astype(BF)
        for k, value in enumerate((hidden, d_gate, d_up)):
            wide[k, :, cols] = value
            copy = pltpu.make_async_copy(
                wide.at[k, :, cols], wide_out[k].at[:, cols], sem_out.at[k, s]
            )
            copy.start()
            out_copies.append(copy)
        back = dot_nt(d_gate, gate_s) + dot_nt(d_up, up_s)
        ahead = dot(hidden, down_s)
        if s == 0:
            back_ref[...] = back
            ahead_ref[...] = ahead
        else:
            back_ref[...] += back
            ahead_ref[...] += ahead
    middle, back = middle_ref[...], back_ref[...]
    d_middle = jnp.where(keep, cot_ref[...], 0.0) + rms_back(middle, scale, back * gain)
    d_middle_out[...] = d_middle
    row_out[...] = d_middle.astype(BF)
    output[...] = jnp.where(keep, middle + ahead_ref[...], 0.0)
    gain_out[...] = jnp.zeros_like(gain_out)
    gain_out[0:1] = jnp.sum(back * (middle * scale), axis=0, keepdims=True)
    for copy in out_copies:
        copy.wait()


def mlp_call(info, gain, x, sums, cotangent, packs, devices):
    seq_len, model = x.shape
    blocks = packs[0].shape[0] * MEMBERS // devices
    own = packs[0].shape[1]
    inner = blocks // 3 * model
    wide = jax.ShapeDtypeStruct((seq_len, inner), BF)
    whole = jax.ShapeDtypeStruct((seq_len, model), F32)
    short = jax.ShapeDtypeStruct((seq_len, model), BF)
    count = inner // model
    return pl.pallas_call(
        mlp_kernel,
        out_shape=(wide, wide, wide, short, short, whole, short, whole)
        + (jax.ShapeDtypeStruct((8, model), F32),),
        in_specs=[SM] + [VM] * 6 + [ANY] * 10,
        out_specs=(ANY, ANY, ANY) + (VM,) * 6,
        scratch_shapes=[
            pltpu.VMEM((devices, blocks, own, model), BF),
            pltpu.VMEM((3, seq_len, inner), BF),
            pltpu.VMEM((seq_len, model), F32),
            pltpu.VMEM((seq_len, model), F32),
            pltpu.VMEM((seq_len, model), F32),
            pltpu.SemaphoreType.DMA((devices,)),
            pltpu.SemaphoreType.DMA((3, count)),
        ],
        **params(6_500_000_000, 16_000_000),
    )(info, gain, x, *sums, cotangent, *packs)


def mlp_grad_kernel(normed_ref, d_out_ref, hidden, d_gate, d_up, out, wide, total, sem, sem_out):
    model = normed_ref.shape[1]
    inner = wide.shape[2]
    count = inner // model
    groups, size_l, _, blocks, own, _ = total.shape
    copies = [
        pltpu.make_async_copy(source, wide.at[k], sem.at[k])
        for k, source in enumerate((d_gate, d_up, hidden))
    ]
    for copy in copies:
        copy.start()

    def turned(value):
        return jnp.transpose(value.astype(F32)).astype(BF)

    normed_t = turned(normed_ref[...])
    for k in range(2):
        copies[k].wait()
        for s in range(count):
            value = dot(normed_t, wide[k, :, pl.ds(s * model, model)]).astype(BF)
            value = value.reshape(HALVES, groups, size_l, own, model)
            for h in range(HALVES):
                total[:, :, h, k * count + s] = value[h]
    copies[2].wait()
    share = HALVES * groups // count
    for s in range(count):
        value = dot(turned(wide[2, :, pl.ds(s * model, model)]), d_out_ref[...]).astype(BF)
        h, at = s * share // groups, s * share % groups
        total[pl.ds(at, share), :, h, 2 * count :] = value.reshape(
            share, size_l, count, own, model
        )
    copy = pltpu.make_async_copy(total, out, sem_out)
    copy.start()
    copy.wait()


def mlp_grad_call(normed, d_out, hidden, d_gate, d_up, size_l):
    seq_len, inner = hidden.shape
    model = normed.shape[1]
    count = inner // model
    own = model // (HALVES * MEMBERS * size_l)
    shape = (MEMBERS, size_l, HALVES, 3 * count, own, model)
    return pl.pallas_call(
        mlp_grad_kernel,
        out_shape=jax.ShapeDtypeStruct(shape, BF),
        in_specs=[VM, VM, ANY, ANY, ANY],
        out_specs=ANY,
        scratch_shapes=[
            pltpu.VMEM((3, seq_len, inner), BF),
            pltpu.VMEM(shape, BF),
            pltpu.SemaphoreType.DMA((3,)),
            pltpu.SemaphoreType.DMA,
        ],
        **params(3_200_000_000, 14_000_000),
    )(normed, d_out, hidden, d_gate, d_up)


def body(
    inputs,
    cotangent,
    lengths,
    filters,
    gain_first,
    mix_plus,
    mix_minus,
    auto_weight,
    gain_second,
    w_gate,
    w_upward,
    w_down,
):
    _, seq_len, model = inputs.shape
    size_l = lax.axis_size("l")
    n = HALVES * MEMBERS * size_l
    h, m, l = lax.axis_index("h"), lax.axis_index(GROUP), lax.axis_index("l")
    me = (h * MEMBERS + m) * size_l + l
    own = gain_first.shape[0]
    inner = w_gate.shape[1]
    count = inner // model

    def blocks(w):
        return jnp.transpose(w.astype(BF).reshape(own, count, model), (1, 0, 2))

    pack = jnp.concatenate(
        [blocks(w_gate), blocks(w_upward), w_down.astype(BF).reshape(count, own, model)], axis=0
    )
    pack_rows = 3 * count * own
    plus, minus, auto = mix_plus.astype(BF), mix_minus.astype(BF), auto_weight.astype(BF)
    own_rows, lag_rows = plus.shape[0], auto.shape[0]
    share_rows = 2 * own_rows + lag_rows
    sizes, cuts = [], [0]
    if size_l == 2:
        a, b = own_rows * 13 // 24, own_rows // 3
        chunks = [
            pack.reshape(pack_rows, model),
            plus[:a],
            jnp.concatenate([plus[a:], minus[:b]], axis=0),
            jnp.concatenate([minus[b:], auto], axis=0),
        ]
        cuts = [0, 0, a, own_rows + b, share_rows]
        sizes = [part.shape[0] for part in chunks]
    far, pairs = [None] * 4, [None] * 5

    def cross(k):
        if size_l == 2:
            far[k] = flip(chunks[k], "h", 1)

    def cross_l(k):
        if size_l == 2:
            both = ([chunks[k]] if k < 4 else []) + ([far[k - 1]] if k else [])
            pairs[k] = flip(jnp.concatenate(both, axis=0) if len(both) > 1 else both[0], "l", 1)

    x = inputs[0]
    scale_one = rms_scale(x)
    pre_one = x * scale_one
    gains = jnp.concatenate([gain_first.astype(BF), gain_second.astype(BF)]).astype(F32)
    peers = HALVES * size_l
    here = lax.broadcasted_iota(jnp.int32, (peers, 1), 0) == h * size_l + l
    gains = jnp.where(here, gains[None], 0.0).reshape(1, -1)
    gains = sum_peers(gains)[0]
    line = jnp.concatenate(
        [
            gains.astype(BF),
            (lengths // 16).astype(BF),
            (lengths % 16).astype(BF),
            jnp.zeros((model - 2 * own * peers - 2,), BF),
        ]
    )
    below = lax.broadcasted_iota(jnp.int32, (32, 1), 0) == 0
    below = jnp.where(below, line[None, :], 0.0).astype(BF)
    row = Gather(jnp.concatenate([pre_one.astype(BF), below], axis=0))

    cross(0)
    cross_l(0)
    if size_l == 2:
        row.row, filters, far[0], pairs[0], *chunks[1:] = sync_all(
            row.row, filters, far[0], pairs[0], *chunks[1:]
        )
    cross(1)
    cross_l(1)
    row.first()
    fwd_table, bwd_table = build_tables(filters, h, m)

    far, pairs, row, fwd_table = sync_all(far, pairs, row, fwd_table)
    if size_l == 2:
        *chunks[2:], far[1] = sync_all(*chunks[2:], far[1])
    cross(2)
    cross_l(2)
    row.second(core=False)
    row.core1 = flip(row.near1, "m", 1)
    late = sync_all(m, row.near1)[0]
    members = late ^ lax.iota(jnp.int32, MEMBERS)
    place = jnp.concatenate([jnp.stack([late % 2]), members, jnp.stack([h, l])])

    col = lax.broadcasted_iota(jnp.int32, (LAGS, model, BLOCK), 2)
    feature = lax.broadcasted_iota(jnp.int32, (LAGS, model, BLOCK), 1)
    feature = (feature + (late % 2) * BLOCK) % model
    lag = lax.broadcasted_iota(jnp.int32, (LAGS, model, BLOCK), 0)
    lag_span = lag_rows * size_l
    rel = col // lag_span
    source = lag_span * (MEMBERS * (h ^ rel) + late) + col % lag_span
    pick = ((rel < 2) & (source == lag * model + feature)).astype(BF)

    far, pairs, row, pick, place = sync_all(far, pairs, row, pick, place)
    if size_l == 2:
        chunks[3], far[2] = sync_all(chunks[3], far[2])
    cross(3)
    cross_l(3)
    row.third()
    row.core2 = flip(row.near2, "m", 1)
    x_rows = row.result()
    spec, info, gains = conv_call(own, n, place, fwd_table, pick, x_rows, seq_len)

    far, pairs, gains, spec = sync_all(far, pairs, gains, spec)
    cross_l(4)
    if size_l == 2:
        held = [chunks[0], pairs[0], far[0], pairs[1][sizes[1] :]]
    else:
        held = [lax.all_gather(part, "l", axis=0) for part in (pack, flip(pack, "h", 1))]
    pack = Gather(jnp.concatenate(held, axis=0).reshape(-1, own, model))
    pack.first()

    pairs, gains, spec = sync_all(pairs, gains, spec)
    gain_one = gains[:, :own].reshape(1, model)
    gain_two = gains[:, own : 2 * own].reshape(1, model)
    plan, pieces = [], []
    if size_l == 2:
        for k in (1, 2, 3):
            at, size = cuts[k], sizes[k]
            plan.append((0, "mine", at, size, own_rows, 0))
            plan.append((1, "mine", at, size, own_rows, 0))
            plan.append((0, "other", at, size, own_rows, 0))
            plan.append((1, "other", at, size, own_rows, sizes[k + 1] if k < 3 else 0))
            pieces += [chunks[k], far[k], pairs[k], pairs[k + 1]]
        lag_weight = jnp.zeros((BLOCK, model), BF)
    else:
        share = jnp.concatenate([plus, minus, auto], axis=0)
        shares = lax.all_gather(share, ("h", "l"), axis=0)
        shares = shares.reshape((HALVES, size_l) + share.shape)
        lag_weight = []
        for rel in range(HALVES):
            half = lax.dynamic_index_in_dim(shares, h ^ rel, 0, keepdims=False)
            lag_weight.append(half[:, 2 * own_rows :])
            for k in range(size_l):
                plan.append((rel, k, 0, 2 * own_rows, own_rows, 0))
                pieces.append(half[k, : 2 * own_rows])
        lag_weight = jnp.stack(lag_weight).reshape(HALVES * lag_span, model)
        lag_weight = jnp.pad(lag_weight, ((0, BLOCK - HALVES * lag_span), (0, 0)))
    plan = tuple(plan)
    mixed = Reduce(mix_call(info, plan, own, lag_span, gains, lag_weight, spec, pieces))

    mixed, pack = sync_all(mixed, pack)
    mixed.first()
    mixed = sync_all(mixed)[0]
    mixed.second()
    mixed, pack = sync_all(mixed, pack)
    mixed = mixed.third()
    pack.second()
    mixed, pack = sync_all(mixed, pack)
    pack.third()

    hidden, d_gate, d_up, normed_two, d_out_b, d_middle, d_row, output, grad_gain_two = mlp_call(
        info, gain_two, x, mixed, cotangent[0], pack.result(), n
    )
    grad_gain_two = grad_gain_two[0:1]

    row = Gather(d_row)
    row.first()

    mlp = mlp_grad_call(normed_two, d_out_b, hidden, d_gate, d_up, size_l)

    row, mlp = sync_all(row, mlp)
    row.second()

    row, grad_gain_two, mlp = sync_all(row, grad_gain_two, mlp)
    mlp = lax.psum_scatter(mlp, GROUP, scatter_dimension=0)
    row.third()
    d_rows = row.result()
    if size_l == 2:
        cut = share_rows * 5 // 8 - 14
        cuts = (
            ((3, 0, cut),),
            ((3, cut, share_rows), (1, 0, share_rows)),
            ((2, 0, cut),),
            ((2, cut, share_rows),),
            ((0, 0, share_rows),),
        )
    else:
        cuts = tuple(((k, 0, share_rows),) for k in range(HALVES * size_l))
    *grad_mix, gain_mix = grad_call(
        info, plan, own, gains, lag_weight, spec, pieces, d_rows, size_l, lag_rows, cuts
    )

    grad_mix, d_rows = sync_all(grad_mix, d_rows)
    grad_gains = jnp.concatenate([gain_mix[0:1], grad_gain_two], axis=0)
    grad_gains = sum_direct(grad_gains, GROUP, 3)
    grad_gains = sum_direct(grad_gains, GROUP, 4)
    if size_l == 2:
        got_far, got_rest = flip(grad_mix[0], "l", 1), flip(grad_mix[1], "l", 1)
        d_rows, got_far, grad_gains = sync_all(d_rows, got_far, grad_gains)
        back = [flip((grad_mix[2].astype(F32) + got_far.astype(F32)).astype(BF), "h", 1)]
    d_normed = Reduce(back_conv_call(info, plan, bwd_table, pick, lag_weight, pieces, d_rows))

    if size_l == 2:
        d_normed, back, got_rest = sync_all(d_normed, back, got_rest)
    d_normed.first()

    d_normed, grad_gains, mlp = sync_all(d_normed, grad_gains, mlp)
    d_normed.second()
    if size_l == 2:
        got_rest = sync_all(got_rest, d_normed.own)[0]
        left = share_rows - cut
        part = (grad_mix[3].astype(F32) + got_rest[:left].astype(F32)).astype(BF)
        back.append(flip(part, "h", 1))
        other = lax.dynamic_index_in_dim(mlp, 1 - l, 0, keepdims=False)
        mlp = lax.dynamic_index_in_dim(mlp, l, 0, keepdims=False).astype(F32)
        blocks_left = other.shape[0] * other.shape[1]
        other = jnp.concatenate(
            [other.reshape((blocks_left,) + other.shape[2:]), two_parts(grad_gains, own)], axis=0
        )
        other = flip(other, "l", 1)
        grad_gains = grad_gains + whole_of(other[blocks_left])
        mlp = mlp + other[:blocks_left].reshape(mlp.shape).astype(F32)
    else:
        grad_gains = lax.psum(grad_gains, "l")
        mlp = lax.psum_scatter(mlp.astype(F32), "l", scatter_dimension=0)

    d_normed = sync_all(d_normed)[0]
    if size_l == 2:
        grad_gains, mlp = sync_all(grad_gains, mlp, d_normed.near1, d_normed.near2)[:2]
        back, got_rest = sync_all(back, got_rest, d_normed.near1, mlp)[:2]
    else:
        grad_gains, mlp = sync_all(grad_gains, mlp, d_normed.near1)[:2]
    d_normed = d_normed.third()
    if size_l == 2:
        other = lax.dynamic_index_in_dim(mlp, 1 - h, 0, keepdims=False).astype(BF)
        other = flip(jnp.concatenate([other, two_parts(grad_gains, own)], axis=0), "h", 1)
        mlp = lax.dynamic_index_in_dim(mlp, h, 0, keepdims=False) + other[:-1].astype(F32)
        grad_gains = grad_gains + whole_of(other[-1])
    else:
        mlp_far = lax.dynamic_index_in_dim(mlp, 1 - h, 0, keepdims=False).astype(BF)
        mlp_near = lax.dynamic_index_in_dim(mlp, h, 0, keepdims=False)
        mlp = mlp_near + flip(mlp_far, "h", 1).astype(F32)
        grad_gains = grad_gains + flip(grad_gains, "h", 1)
    grad_gains = lax.dynamic_slice_in_dim(grad_gains, me * own, own, 1)
    own_sum, got1, got2 = d_normed
    d_normed = own_sum + got1.astype(F32) + got2.astype(F32)
    input_grad = d_middle + rms_back(x, scale_one, d_normed * gain_one)
    if size_l == 2:
        near = grad_mix[4].astype(F32) + got_rest[left:].astype(F32)
        grad_mix = near + jnp.concatenate(back, axis=0).astype(F32)
    else:
        both = jnp.stack(grad_mix).reshape((HALVES, size_l) + grad_mix[0].shape)
        grad_mix = jnp.where(h == 0, both, both[::-1]).reshape((-1,) + both.shape[2:])
        grad_mix = lax.psum_scatter(grad_mix, ("h", "l"), scatter_dimension=0).astype(F32)
    mlp = mlp.reshape(3, count, own, model)
    grad_gate, grad_up = [
        jnp.transpose(mlp[k], (1, 0, 2)).reshape(own, inner) for k in range(2)
    ]
    grad_down = mlp[2].reshape(count * own, model)

    return (
        output[None],
        input_grad[None],
        grad_gains[0],
        grad_mix[:own_rows],
        grad_mix[own_rows : 2 * own_rows],
        grad_mix[2 * own_rows :],
        grad_gains[1],
        grad_gate,
        grad_up,
        grad_down,
    )


def solution(mesh):
    shape = (HALVES, 2, 2, 2, mesh.size // (HALVES * MEMBERS))
    inner = Mesh(mesh.devices.reshape(shape), ALL)
    row, vec, mat = P(ALL, None, None), P(ALL), P(ALL, None)
    in_specs = (row, row, vec, P(), vec, mat, mat, mat, vec, mat, mat, mat)
    out_specs = (row, row, vec, mat, mat, mat, vec, mat, mat, mat)
    return jax.shard_map(body, mesh=inner, in_specs=in_specs, out_specs=out_specs, check_vma=False)
```

```python
import functools

import jax
import jax.numpy as jnp
from jax import lax
from jax.experimental import pallas as pl
from jax.experimental.pallas import tpu as pltpu
from jax.sharding import Mesh, PartitionSpec as P

EPSILON = 1e-05
MEMBERS = 8
HALVES = 2
BLOCK = 256
LAGS = 3
VMEM_LIMIT = 60 * 1024 * 1024
BF = jnp.bfloat16
F32 = jnp.float32
GROUP = ("z", "y", "c")
ALL = ("h",) + GROUP + ("l",)
ANY = pl.BlockSpec(memory_space=pl.ANY)
VM = pl.BlockSpec(memory_space=pltpu.VMEM)
SM = pl.BlockSpec(memory_space=pltpu.SMEM)


def rms_scale(values):
    return lax.rsqrt(jnp.mean(values * values, axis=-1, keepdims=True) + EPSILON)


def rms_back(values, scale, d_pre):
    return scale * d_pre - values * (scale * scale * scale) * jnp.mean(
        d_pre * values, axis=-1, keepdims=True
    )


def flip(x, axis, bit):
    if axis == "m":
        axis, bit = {1: "c", 2: "y", 4: "z"}[bit], 1
    size = lax.axis_size(axis)
    return lax.ppermute(x, axis, [(i, i ^ bit) for i in range(size)])


def after(x, *earlier):
    return lax.optimization_barrier((x, earlier))[0]


def dot(a, b):
    return jnp.dot(a, b, preferred_element_type=F32)


def dot_nt(a, b):
    return lax.dot_general(a, b, (((1,), (1,)), ((), ())), preferred_element_type=F32)


def arrays_of(value):
    if hasattr(value, "__dict__"):
        return {k: v for k, v in vars(value).items() if not isinstance(v, (int, str))}
    if isinstance(value, (list, tuple)):
        return [arrays_of(v) for v in value]
    return value


def with_arrays(value, arrays):
    if hasattr(value, "__dict__"):
        fresh = object.__new__(type(value))
        fresh.__dict__.update(vars(value))
        fresh.__dict__.update(arrays)
        return fresh
    if isinstance(value, (list, tuple)):
        return type(value)(with_arrays(v, a) for v, a in zip(value, arrays))
    return arrays


def sync(*values):
    return lax.optimization_barrier(values)


def sync_all(*values):
    leaves, tree = jax.tree.flatten([arrays_of(v) for v in values])
    kept = [k for k, leaf in enumerate(leaves) if isinstance(leaf, jax.Array)]
    for k, new in zip(kept, lax.optimization_barrier([leaves[k] for k in kept])):
        leaves[k] = new
    fresh = jax.tree.unflatten(tree, leaves)
    return tuple(with_arrays(v, a) for v, a in zip(values, fresh))


class Gather:
    def __init__(self, row):
        self.row = row
        self.half = row.shape[0] // 2

    def first(self):
        self.near1, self.near2 = flip(self.row, "m", 2), flip(self.row, "m", 4)
        self.core0 = flip(self.row, "m", 1)

    def second(self, core=True):
        self.top = flip(self.near2[: self.half], "m", 2)
        self.low = flip(self.near1[self.half :], "m", 4)
        if core:
            self.core1, self.core2 = flip(self.near1, "m", 1), flip(self.near2, "m", 1)

    def third(self):
        self.core_top, self.core_low = flip(self.top, "m", 1), flip(self.low, "m", 1)

    def result(self):
        return (
            self.row,
            self.core0,
            self.near1,
            self.core1,
            self.near2,
            self.core2,
            self.top,
            self.low,
            self.core_top,
            self.core_low,
        )


class Reduce:
    def __init__(self, parts):
        self.parts = parts
        self.half = parts[0].shape[0] // 2

    def first(self):
        own, core0, near1, core1, near2, core2, top, low, core_top, core_low = self.parts
        self.own = own.astype(F32) + flip(core0, "m", 1).astype(F32)
        self.near1 = near1.astype(F32) + flip(core1, "m", 1).astype(F32)
        self.near2 = near2.astype(F32) + flip(core2, "m", 1).astype(F32)
        self.top = (top.astype(F32) + flip(core_top, "m", 1).astype(F32)).astype(BF)
        self.low = (low.astype(F32) + flip(core_low, "m", 1).astype(F32)).astype(BF)

    def second(self):
        half = self.half
        got_top = flip(self.top, "m", 2).astype(F32)
        got_low = flip(self.low, "m", 4).astype(F32)
        near1, near2 = self.near1, self.near2
        self.near1 = jnp.concatenate([near1[:half], near1[half:] + got_low], axis=0).astype(BF)
        self.near2 = jnp.concatenate([near2[:half] + got_top, near2[half:]], axis=0).astype(BF)

    def third(self):
        return self.own, flip(self.near1, "m", 2), flip(self.near2, "m", 4)


def gather_l(x):
    size = lax.axis_size("l")
    if size != 2:
        return lax.all_gather(x, "l", axis=0, tiled=True)
    peer = flip(x, "l", 1)
    first = lax.axis_index("l") == 0
    return jnp.concatenate([jnp.where(first, x, peer), jnp.where(first, peer, x)], axis=0)


def scatter_l(x, axis):
    size = lax.axis_size("l")
    if size != 2:
        return lax.psum_scatter(x.astype(F32), "l", scatter_dimension=axis, tiled=True)
    part = x.shape[axis] // 2
    mine = lax.axis_index("l")
    kept = lax.dynamic_slice_in_dim(x, mine * part, part, axis)
    sent = lax.dynamic_slice_in_dim(x, (1 - mine) * part, part, axis)
    return kept.astype(F32) + flip(sent.astype(BF), "l", 1).astype(F32)


def sum_direct(x, axes, bits):
    total = x
    size = 1
    for axis in axes:
        size *= lax.axis_size(axis)
    for mask in range(1, size):
        if mask & ~bits == 0:
            total = total + lax.ppermute(x, axes, [(i, i ^ mask) for i in range(size)])
    return total


def sum_peers(x):
    size = HALVES * lax.axis_size("l")
    if size == 4:
        return sum_direct(x, ("h", "l"), 3)
    step = 1
    while step < size:
        x = x + lax.ppermute(x, ("h", "l"), [(i, i ^ step) for i in range(size)])
        step *= 2
    return x


def two_parts(values, rows):
    high = values.astype(BF)
    low = (values - high.astype(F32)).astype(BF)
    return jnp.pad(jnp.concatenate([high, low], axis=0), ((0, rows - 4), (0, 0)))[None]


def whole_of(block):
    return block[0:2].astype(F32) + block[2:4].astype(F32)


def tables_kernel(base_ref, fwd_ref, bwd_ref):
    rows, width = fwd_ref.shape[1], fwd_ref.shape[2]
    span = base_ref.shape[1]
    odd = (
        lax.broadcasted_iota(jnp.int32, (rows, width), 0)
        + lax.broadcasted_iota(jnp.int32, (rows, width), 1)
    ) % 2
    sign = (1 - 2 * odd).astype(F32)
    for index in range(4):
        for which, out in ((0, fwd_ref), (1, bwd_ref)):
            line = jnp.broadcast_to(base_ref[pl.ds(which * 4 + index, 1), :], (rows, span))
            rolled = pltpu.roll(line, 0, 1, stride=1, stride_axis=0)[:, :width]
            out[2 * index] = rolled.astype(BF)
            out[2 * index + 1] = (rolled * sign).astype(BF)


def build_tables(filters, h, m):
    seq_len, count = filters.shape
    phi = jnp.transpose(filters.astype(BF).astype(F32))
    zeros = jnp.zeros((count, BLOCK), F32)
    bwd = jnp.concatenate([phi, zeros], axis=1)
    back = jnp.flip(phi, axis=1)
    fwd = jnp.concatenate(
        [
            back[:, seq_len - 1 - BLOCK :],
            jnp.zeros((count, BLOCK), F32),
            back[:, : seq_len - 1 - BLOCK],
        ],
        axis=1,
    )
    rows = []
    for table in (fwd, bwd):
        for rel in range(HALVES):
            first = 12 * (h ^ rel) + (3 * m) // 2
            rows.append(lax.dynamic_slice_in_dim(table, first, 2, 0))
    base = jnp.concatenate(rows, axis=0)
    shape = jax.ShapeDtypeStruct((8, BLOCK, seq_len), BF)
    return pl.pallas_call(
        tables_kernel,
        out_shape=(shape, shape),
        in_specs=[VM],
        out_specs=(VM, VM),
        compiler_params=pltpu.CompilerParams(vmem_limit_bytes=VMEM_LIMIT),
        cost_estimate=pl.CostEstimate(flops=20_000_000, bytes_accessed=5_000_000, transcendentals=0),
    )(base)


def load_rows(refs, scratch, sem):
    started = []
    for j in range(MEMBERS):
        for ref, first, size in used_parts(refs, j, scratch.shape[1]):
            into = scratch.at[j, pl.ds(first, size)]
            started.append(pltpu.make_async_copy(ref, into, sem.at[len(started)]))
            started[-1].start()
    return started


def row_stores(scratch, refs, j, sem):
    copies = []
    for k, (ref, first) in enumerate(halves_of(refs, j)):
        source = scratch.at[j, pl.ds(first, ref.shape[0])]
        copies.append(pltpu.make_async_copy(source, ref, sem.at[j, k]))
    return copies


def halves_of(refs, j):
    if j < 6:
        return [(refs[j], 0)]
    return [(refs[2 * j - 6], 0), (refs[2 * j - 5], refs[2 * j - 6].shape[0])]


def used_parts(refs, j, tokens):
    found = []
    for ref, first in halves_of(refs, j):
        size = min(ref.shape[0], tokens - first)
        if size > 0:
            found.append((ref.at[pl.ds(0, size)], first, size))
    return found


def unused_parts(refs, j, tokens):
    found = []
    for ref, first in halves_of(refs, j):
        start = max(tokens - first, 0)
        if start < ref.shape[0]:
            found.append((ref.at[pl.ds(start, ref.shape[0] - start)], ref.shape[0] - start))
    return found


def place(info, r):
    return pl.multiple_of(info[19 + r], 128)


def packed_copies(info, refs, packed, sem, act):
    for j in range(MEMBERS):

        def run(tokens, j=j):
            for k, (ref, first, size) in enumerate(used_parts(refs, j, tokens)):
                into = packed.at[pl.ds(place(info, j) + first, size)]
                act(pltpu.make_async_copy(ref, into, sem.at[j, k]))

        by_length(info[j], run)


def unpacked_copies(info, packed, zeros, refs, sem, act, low=None, high=None):
    for j in range(MEMBERS):

        def run(tokens, j=j):
            k = 0
            for ref, first, size in used_parts(refs, j, tokens):
                source = packed.at[pl.ds(place(info, j) + first, size)]
                act(pltpu.make_async_copy(source, ref, sem.at[j, k]))
                k += 1
            for ref, size in unused_parts(refs, j, tokens):
                act(pltpu.make_async_copy(zeros.at[pl.ds(0, size)], ref, sem.at[j, k]))
                k += 1

        if low is None:
            by_length(info[j], run)
        else:
            end = info[20 + j]
            pl.when((end > low) & (end <= high))(functools.partial(by_length, info[j], run))


def chunk_copies(info, spec_in, spec, sem, act):
    count, rows = spec.shape[0], spec.shape[1]
    for c in range(count):

        @pl.when(c * rows < info[27])
        def _(c=c):
            act(pltpu.make_async_copy(spec_in.at[pl.ds(c * rows, rows)], spec.at[c], sem.at[c]))


def chunks_of(info, rows):
    return lax.div(info[27] + (rows - 1), rows)


def weight_copies(info, plan, pieces, weight, sem):
    copies = []
    for piece, (rel, l, begin, size, own, source) in zip(pieces, plan):
        l = info[18] if l == "mine" else 1 - info[18] if l == "other" else l
        end = begin + size
        areas = [(0, own, rel * 6 * BLOCK), (own, 2 * own, (rel * 2 + 1) * 3 * BLOCK)]
        if end > 2 * own:
            lags = end - 2 * own
            areas.append((2 * own, end, 12 * BLOCK + rel * 2 * lags))
        for first, last, target in areas:
            low, high = max(first, begin), min(last, end)
            if low < high:
                to = target + l * (last - first) + (low - first)
                if not isinstance(to, int):
                    to = pl.multiple_of(to, 16)
                copies.append(
                    pltpu.make_async_copy(
                        piece.at[pl.ds(source + low - begin, high - low)],
                        weight.at[pl.ds(to, high - low)],
                        sem.at[len(copies)],
                    )
                )
    return copies


def start(copy):
    copy.start()


def finish(copy):
    copy.wait()


def by_length(length, run):
    for tokens in range(128, 513, 128):
        pl.when((length > tokens - 128) & (length <= tokens))(functools.partial(run, tokens))


def combos(info):
    middle = info[8]
    for rel in range(HALVES):
        for sign in range(2):
            for pos, which in enumerate((0, middle, 1)):
                block = (rel * 2 + sign) * 3 + pos
                yield block, rel * 4 + which * 2 + sign, pos % 2


def gain_columns(table_ref, feature, own):
    devices = table_ref.shape[0]
    shift = own.bit_length() - 1
    rows = feature.shape[0]
    device = lax.broadcasted_iota(jnp.int32, (rows, devices), 1)
    chosen = (device == (feature >> shift)).astype(BF)
    found = dot(chosen, table_ref[...].astype(BF))
    lane = lax.broadcasted_iota(jnp.int32, found.shape, 1)
    return jnp.sum(jnp.where(lane == (feature & (own - 1)), found, 0.0), axis=1, keepdims=True)


def feature_places(info, model, lag_span):
    line = lax.broadcasted_iota(jnp.int32, (BLOCK, 1), 0)
    rel = (line >= lag_span).astype(jnp.int32)
    source = lag_span * (MEMBERS * (info[17] ^ rel) + info[9]) + line - rel * lag_span
    return [line + info[8] * BLOCK, line + (1 - info[8]) * BLOCK, source & (model - 1)]


def feature_gains(info, table_ref, model, own, lag_span):
    return [
        gain_columns(table_ref, feature, own) for feature in feature_places(info, model, lag_span)
    ]


def read_lines(own, place_ref, lines, info, gains, seq_len):
    lane = lax.broadcasted_iota(jnp.int32, (1, 128), 1)
    weights = jnp.where(lane == 0, 16.0, jnp.where(lane == 1, 1.0, 0.0))
    total = jnp.int32(0)
    size_l = gains.shape[0] // (HALVES * MEMBERS)
    for k in range(11):
        info[8 + k] = place_ref[k]
    for j in range(MEMBERS):
        line = lines[j, :, :256].astype(F32)[0:1]
        length = jnp.sum(line[:, 128:] * weights).astype(jnp.int32)
        info[j] = length
        info[19 + j] = total
        total = total + ((length + 127) >> 7 << 7)
        for peer in range(HALVES * size_l):
            device = (peer // size_l * MEMBERS + info[9 + j]) * size_l + peer % size_l
            gains[pl.ds(device, 1), pl.ds(0, 2 * own)] = line[
                :, 2 * own * peer : 2 * own * (peer + 1)
            ]
    info[27] = total


def conv_kernel(own, place_ref, table_ref, pick_ref, *refs):
    rows_in = refs[:10]
    spec_out, info, gains = refs[10:13]
    stack, lines, normed, spec, sem_in, sem_line, sem_spec = refs[13:]
    seq_len = stack.shape[1]
    line_copies = []
    for j in range(MEMBERS):
        ref, first = halves_of(rows_in, j)[-1]
        source = ref.at[pl.ds(seq_len - first, lines.shape[1])]
        line_copies.append(pltpu.make_async_copy(source, lines.at[j], sem_line.at[j]))
        line_copies[-1].start()
    loads = load_rows(rows_in, stack, sem_in)
    gains[...] = jnp.zeros_like(gains)
    for copy in line_copies:
        copy.wait()
    read_lines(own, place_ref, lines, info, gains, seq_len)
    for copy in loads:
        copy.wait()
    odd = info[8] == 1

    def spec_copy(r, tokens):
        slot = lax.rem(r, 2)
        return pltpu.make_async_copy(
            spec.at[slot, pl.ds(0, tokens)],
            spec_out.at[pl.ds(place(info, r), tokens)],
            sem_spec.at[slot],
        )

    def row(r, carry):
        slot = lax.rem(r, 2)

        @pl.when(r >= 2)
        def _():
            by_length(info[r - 2], lambda tokens: spec_copy(r - 2, tokens).wait())

        def run(tokens):
            left = stack[r, pl.ds(0, tokens), :BLOCK]
            right = stack[r, pl.ds(0, tokens), BLOCK:]
            normed[pl.ds(0, tokens), :BLOCK] = jnp.where(odd, right, left)
            normed[pl.ds(0, tokens), BLOCK:] = jnp.where(odd, left, right)
            first = min(tokens, BLOCK)
            for block, table, side in combos(info):
                cols = pl.ds(side * BLOCK, BLOCK)
                into = pl.ds(block * BLOCK, BLOCK)
                spec[slot, pl.ds(0, first), into] = dot(
                    table_ref[table, pl.ds(0, first), pl.ds(BLOCK, first)],
                    normed[pl.ds(0, first), cols],
                ).astype(BF)
                if tokens > BLOCK:
                    rest = pl.ds(0, tokens - BLOCK)
                    spec[slot, pl.ds(BLOCK, tokens - BLOCK), into] = dot(
                        table_ref[table, rest, pl.ds(0, tokens)], normed[pl.ds(0, tokens), cols]
                    ).astype(BF)
            lagged = None
            for lag in range(LAGS):
                moved = dot(normed[pl.ds(0, tokens)], pick_ref[lag])
                if lag:
                    moved = jnp.concatenate(
                        [jnp.zeros((lag, BLOCK), F32), moved[: tokens - lag]], axis=0
                    )
                lagged = moved if lagged is None else lagged + moved
            spec[slot, pl.ds(0, tokens), pl.ds(12 * BLOCK, BLOCK)] = lagged.astype(BF)
            spec_copy(r, tokens).start()

        by_length(info[r], run)
        return carry

    lax.fori_loop(0, MEMBERS, row, 0)
    for r in (MEMBERS - 2, MEMBERS - 1):
        by_length(info[r], lambda tokens, r=r: spec_copy(r, tokens).wait())


def row_shapes(seq_len, model):
    whole = jax.ShapeDtypeStruct((seq_len, model), BF)
    half = jax.ShapeDtypeStruct((seq_len // 2, model), BF)
    return (whole,) * 6 + (half,) * 4


def params(flops, data):
    return dict(
        compiler_params=pltpu.CompilerParams(vmem_limit_bytes=VMEM_LIMIT),
        cost_estimate=pl.CostEstimate(flops=flops, bytes_accessed=data, transcendentals=0),
    )


def conv_call(own, devices, place, table, pick, rows, seq_len):
    model = rows[0].shape[1]
    features = 13 * BLOCK
    return pl.pallas_call(
        functools.partial(conv_kernel, own),
        out_shape=(
            jax.ShapeDtypeStruct((MEMBERS * seq_len, features), BF),
            jax.ShapeDtypeStruct((32,), jnp.int32),
            jax.ShapeDtypeStruct((devices, 128), F32),
        ),
        in_specs=[SM, VM, VM] + [ANY] * 10,
        out_specs=(ANY, SM, VM),
        scratch_shapes=[
            pltpu.VMEM((MEMBERS, seq_len, model), BF),
            pltpu.VMEM((MEMBERS, 16, model), BF),
            pltpu.VMEM((seq_len, model), BF),
            pltpu.VMEM((2, seq_len, features), BF),
            pltpu.SemaphoreType.DMA((10,)),
            pltpu.SemaphoreType.DMA((MEMBERS,)),
            pltpu.SemaphoreType.DMA((2,)),
        ],
        **params(5_000_000_000, 20_000_000),
    )(place, table, pick, *rows)


def mix_kernel(plan, own, lag_span, info, gain_ref, lag_ref, spec_in, *refs):
    pieces, refs = refs[: len(plan)], refs[len(plan) :]
    parts_out = refs[:10]
    weight, spec, parts, zeros, sem_in, sem_out, sem_spec = refs[10:]
    weight[pl.ds(12 * BLOCK, BLOCK)] = lag_ref[...]
    copies = weight_copies(info, plan, pieces, weight, sem_in)
    for copy in copies:
        copy.start()
    chunk_copies(info, spec_in, spec, sem_spec, start)
    zeros[...] = jnp.zeros_like(zeros)
    rows = spec.shape[1]
    for copy in copies:
        copy.wait()
    columns = feature_gains(info, gain_ref, weight.shape[1], own, lag_span)
    for block in range(weight.shape[0] // BLOCK):
        at = pl.ds(block * BLOCK, BLOCK)
        column = columns[2 if block == 12 else block % 3 % 2]
        weight[at] = (weight[at].astype(F32) * column).astype(BF)

    def chunk(c, carry):
        here = pl.ds(pl.multiple_of(c * rows, rows), rows)
        pltpu.make_async_copy(spec_in.at[here], spec.at[c], sem_spec.at[c]).wait()
        parts[here] = dot(spec[c], weight[...]).astype(BF)
        unpacked_copies(
            info, parts, zeros, parts_out, sem_out, start, c * rows, c * rows + rows
        )
        return carry

    lax.fori_loop(0, chunks_of(info, rows), chunk, 0)
    unpacked_copies(info, parts, zeros, parts_out, sem_out, finish)


def mix_call(info, plan, own, lag_span, gain, lag_weight, spec, pieces):
    tokens, features = spec.shape
    model = pieces[0].shape[-1]
    seq_len = tokens // MEMBERS
    return pl.pallas_call(
        functools.partial(mix_kernel, plan, own, lag_span),
        out_shape=row_shapes(seq_len, model),
        in_specs=[SM, VM, VM, ANY] + [ANY] * len(plan),
        out_specs=(ANY,) * 10,
        scratch_shapes=[
            pltpu.VMEM((features, model), BF),
            pltpu.VMEM((MEMBERS, seq_len, features), BF),
            pltpu.VMEM((tokens, model), BF),
            pltpu.VMEM((seq_len, model), BF),
            pltpu.SemaphoreType.DMA((3 * len(plan),)),
            pltpu.SemaphoreType.DMA((MEMBERS, 3)),
            pltpu.SemaphoreType.DMA((MEMBERS,)),
        ],
        **params(8_000_000_000, 30_000_000),
    )(info, gain, lag_weight, spec, *pieces)


def back_conv_kernel(plan, info, table_ref, pick_ref, lag_ref, *refs):
    pieces, refs = refs[: len(plan)], refs[len(plan) :]
    rows_in, parts_out = refs[:10], refs[10:20]
    d_mix, d_spec, parts, weight, sem_in, sem_out, sem_w = refs[20:]
    packed_copies(info, rows_in, d_mix, sem_in, start)
    weight[pl.ds(12 * BLOCK, BLOCK)] = lag_ref[...]
    copies = weight_copies(info, plan, pieces, weight, sem_w)
    for copy in copies:
        copy.start()
    _, seq_len, model = parts.shape
    features = d_spec.shape[1]
    odd = info[8] == 1
    packed_copies(info, rows_in, d_mix, sem_in, finish)
    for copy in copies:
        copy.wait()

    def chunk(c, carry):
        here = pl.ds(pl.multiple_of(c * seq_len, seq_len), seq_len)
        dm = d_mix[here]
        for block in range(features // BLOCK):
            cols = pl.ds(block * BLOCK, BLOCK)
            d_spec[here, cols] = dot_nt(dm, weight[cols]).astype(BF)
        return carry

    lax.fori_loop(0, chunks_of(info, seq_len), chunk, 0)

    def row(r, carry):
        at_row = place(info, r)

        def run(tokens):
            here = pl.ds(at_row, tokens)
            first = min(tokens, BLOCK)
            sides = [[None, None], [None, None]]
            for block, table, side in combos(info):
                cols = pl.ds(block * BLOCK, BLOCK)
                term = dot(table_ref[table, pl.ds(0, first), pl.ds(0, tokens)], d_spec[here, cols])
                sides[side][0] = term if sides[side][0] is None else sides[side][0] + term
                if tokens > BLOCK:
                    rest = pl.ds(0, tokens - BLOCK)
                    term = dot(
                        table_ref[table, rest, rest],
                        d_spec[pl.ds(at_row + BLOCK, tokens - BLOCK), cols],
                    )
                    sides[side][1] = term if sides[side][1] is None else sides[side][1] + term
            d_lag = d_spec[here, pl.ds(12 * BLOCK, BLOCK)]
            back = None
            for lag in range(LAGS):
                moved = dot_nt(d_lag, pick_ref[lag])
                if lag:
                    moved = jnp.concatenate(
                        [moved[lag:], jnp.zeros((lag, model), F32)], axis=0
                    )
                back = moved if back is None else back + moved
            for begin in range(0, tokens, BLOCK):
                size = min(BLOCK, tokens - begin)
                k = begin // BLOCK
                at = pl.ds(begin, size)
                d_a = sides[0][k] + back[begin : begin + size, :BLOCK]
                d_b = sides[1][k] + back[begin : begin + size, BLOCK:]
                left, right = jnp.where(odd, d_b, d_a), jnp.where(odd, d_a, d_b)
                parts[r, at, :BLOCK] = left.astype(BF)
                parts[r, at, BLOCK:] = right.astype(BF)
            if tokens < parts.shape[1]:
                rest = parts.shape[1] - tokens
                parts[r, pl.ds(tokens, rest)] = jnp.zeros((rest, model), BF)

        by_length(info[r], run)
        for j in range(MEMBERS):

            @pl.when(r == j)
            def _(j=j):
                for copy in row_stores(parts, parts_out, j, sem_out):
                    copy.start()

        return carry

    lax.fori_loop(0, MEMBERS, row, 0)
    for j in range(MEMBERS):
        for copy in row_stores(parts, parts_out, j, sem_out):
            copy.wait()


def back_conv_call(info, plan, table, pick, lag_weight, pieces, rows):
    seq_len, model = rows[0].shape
    features = 13 * BLOCK
    return pl.pallas_call(
        functools.partial(back_conv_kernel, plan),
        out_shape=row_shapes(seq_len, model),
        in_specs=[SM, VM, VM, VM] + [ANY] * (10 + len(plan)),
        out_specs=(ANY,) * 10,
        scratch_shapes=[
            pltpu.VMEM((MEMBERS * seq_len, model), BF),
            pltpu.VMEM((MEMBERS * seq_len, features), BF),
            pltpu.VMEM((MEMBERS, seq_len, model), BF),
            pltpu.VMEM((features, model), BF),
            pltpu.SemaphoreType.DMA((MEMBERS, 2)),
            pltpu.SemaphoreType.DMA((MEMBERS, 2)),
            pltpu.SemaphoreType.DMA((3 * len(plan),)),
        ],
        **params(12_000_000_000, 20_000_000),
    )(info, table, pick, lag_weight, *pieces, *rows)


def spread(value, feature, model):
    lane = lax.broadcasted_iota(jnp.int32, (value.shape[0], model), 1)
    return jnp.sum(jnp.where(lane == feature, value, 0.0), axis=0, keepdims=True)


def grad_kernel(plan, size_l, gain_own, lags, cuts, info, gain_ref, lag_ref, spec_in, *refs):
    pieces, refs = refs[: len(plan)], refs[len(plan) :]
    rows_in, refs = refs[:10], refs[10:]
    count = len(cuts)
    outs, gain_out, refs = refs[:count], refs[count], refs[count + 1 :]
    shares, d_mix, spec, total, weight, sem_in, sem_spec, sem_w, sem_out = refs
    features = total.shape[1]
    model = total.shape[0]
    rows = spec.shape[1]
    own = 3 * BLOCK // size_l

    def share_of(rel, l):
        return rel * size_l + (info[18] ^ l if size_l == 2 else l)

    packed_copies(info, rows_in, d_mix, sem_in, start)
    chunk_copies(info, spec_in, spec, sem_spec, start)
    weight[pl.ds(12 * BLOCK, BLOCK)] = lag_ref[...]
    weights = weight_copies(info, plan, pieces, weight, sem_w)
    for copy in weights:
        copy.start()
    total[...] = jnp.zeros_like(total)
    packed_copies(info, rows_in, d_mix, sem_in, finish)

    def chunk(c, carry):
        base = pl.multiple_of(c * rows, rows)
        here = pl.ds(base, rows)
        pltpu.make_async_copy(spec_in.at[here], spec.at[c], sem_spec.at[c]).wait()
        for tile in range(0, rows, 128):

            @pl.when(base + tile >= info[27])
            def _(tile=tile):
                spec[c, pl.ds(tile, 128)] = jnp.zeros((128, features), BF)
                d_mix[pl.ds(base + tile, 128)] = jnp.zeros((128, d_mix.shape[1]), BF)

        dm_t = jnp.transpose(d_mix[here].astype(F32)).astype(BF)
        for block in range(features // BLOCK):
            cols = pl.ds(block * BLOCK, BLOCK)
            total[:, cols] += dot(dm_t, spec[c, :, cols])
        return carry

    lax.fori_loop(0, chunks_of(info, rows), chunk, 0)
    for copy in weights:
        copy.wait()
    lag_span = lags * size_l
    columns = feature_gains(info, gain_ref, model, gain_own, lag_span)
    places = feature_places(info, model, lag_span)
    sums = [None, None, None]
    for block in range(features // BLOCK):
        kind = 2 if block == 12 else block % 3 % 2
        value = jnp.transpose(total[:, pl.ds(block * BLOCK, BLOCK)])
        part = jnp.sum(
            value * weight[pl.ds(block * BLOCK, BLOCK)].astype(F32), axis=1, keepdims=True
        )
        sums[kind] = part if sums[kind] is None else sums[kind] + part
        value = (value * columns[kind]).astype(BF)
        if block < 12:
            rel, branch, first = block // 6, block // 3 % 2, block % 3 * BLOCK
            at = first
            while at < first + BLOCK:
                l, inside = at // own, at % own
                size = min(own - inside, first + BLOCK - at)
                shares[share_of(rel, l), pl.ds(branch * own + inside, size)] = value[
                    at - first : at - first + size
                ]
                at += size
        else:
            for rel in range(HALVES):
                for l in range(size_l):
                    at = (rel * size_l + l) * lags
                    shares[share_of(rel, l), pl.ds(2 * own, lags)] = value[at : at + lags]
    copies = []
    for out, parts in zip(outs, cuts):
        at = 0
        for k, a, b in parts:
            source, into = shares.at[k, pl.ds(a, b - a)], out.at[pl.ds(at, b - a)]
            if len(parts) == 1:
                into = out
            copies.append(pltpu.make_async_copy(source, into, sem_out.at[len(copies)]))
            copies[-1].start()
            at += b - a
    gain_out[...] = jnp.zeros_like(gain_out)
    for kind in range(3):
        gain_out[0:1] += spread(sums[kind], places[kind], model)
    for copy in copies:
        copy.wait()


def grad_call(info, plan, gain_own, gain, lag_weight, spec, pieces, rows, size_l, lags, cuts):
    seq_len, model = rows[0].shape
    tokens, features = spec.shape
    share_rows = 6 * BLOCK // size_l + lags
    shapes = tuple(
        jax.ShapeDtypeStruct((sum(b - a for _, a, b in parts), model), BF) for parts in cuts
    )
    return pl.pallas_call(
        functools.partial(grad_kernel, plan, size_l, gain_own, lags, cuts),
        out_shape=shapes + (jax.ShapeDtypeStruct((8, model), F32),),
        in_specs=[SM, VM, VM] + [ANY] * (11 + len(plan)),
        out_specs=(ANY,) * len(shapes) + (VM,),
        scratch_shapes=[
            pltpu.VMEM((HALVES * size_l, share_rows, model), BF),
            pltpu.VMEM((tokens, model), BF),
            pltpu.VMEM((MEMBERS, seq_len, features), BF),
            pltpu.VMEM((model, features), F32),
            pltpu.VMEM((features, model), BF),
            pltpu.SemaphoreType.DMA((MEMBERS, 2)),
            pltpu.SemaphoreType.DMA((MEMBERS,)),
            pltpu.SemaphoreType.DMA((3 * len(plan),)),
            pltpu.SemaphoreType.DMA((sum(len(parts) for parts in cuts),)),
        ],
        **params(8_000_000_000, 30_000_000),
    )(info, gain, lag_weight, spec, *pieces, *rows)


def mlp_kernel(info, gain_ref, x_ref, own_ref, got1_ref, got2_ref, cot_ref, *refs):
    packs, refs = refs[:10], refs[10:]
    wide_out, (normed_ref, d_out_ref, d_middle_out, row_out, output, gain_out) = refs[:3], refs[3:9]
    held, wide, middle_ref, back_ref, ahead_ref, sem, sem_out = refs[9:]
    seq_len, model = x_ref.shape
    devices, blocks, _, _ = held.shape
    count = blocks // 3
    size_l = devices // (HALVES * MEMBERS)
    half = HALVES * size_l // 2
    copies = []
    for j in range(MEMBERS):
        for ref, first in halves_of(packs, j):
            first = first // blocks
            for k in range(ref.shape[0] // blocks):
                rel, l = (first + k) // size_l, (first + k) % size_l
                l = info[18] ^ l if size_l == 2 else l
                device = ((info[17] ^ rel) * MEMBERS + info[9 + j]) * size_l + l
                source = ref.at[pl.ds(k * blocks, blocks)]
                copies.append(pltpu.make_async_copy(source, held.at[device], sem.at[len(copies)]))
    for copy in copies:
        copy.start()
    gain = gain_ref[...]
    middle = x_ref[...] + (
        own_ref[...] + got1_ref[...].astype(F32) + got2_ref[...].astype(F32)
    )
    middle_ref[...] = middle
    scale = rms_scale(middle)
    normed_ref[...] = (middle * scale * gain).astype(BF)
    keep = lax.broadcasted_iota(jnp.int32, (seq_len, 1), 0) < info[0]
    d_out_ref[...] = jnp.where(keep, cot_ref[...], 0.0).astype(BF)
    for copy in copies:
        copy.wait()
    root, cubic = 0.7978845608028654, 0.044715
    out_copies = []
    for s in range(count):
        cols = pl.ds(s * model, model)
        normed, d_out = normed_ref[...], d_out_ref[...]
        gate_s = held[:, s].reshape(model, model)
        up_s = held[:, count + s].reshape(model, model)
        pre = dot(normed, gate_s)
        upward = dot(normed, up_s)
        share = devices // count
        down_s = held[pl.ds(s * share, share), 2 * count :].reshape(model, model)
        d_hidden = dot_nt(d_out, down_s)
        square = pre * pre
        tanh = jnp.tanh(root * pre * (1.0 + cubic * square))
        half = 0.5 * (1.0 + tanh)
        slope = half + 0.5 * pre * (1.0 - tanh * tanh) * (root * (1.0 + 3.0 * cubic * square))
        active = pre * half
        hidden = (active * upward).astype(BF)
        d_gate = (d_hidden * upward * slope).astype(BF)
        d_up = (d_hidden * active).astype(BF)
        for k, value in enumerate((hidden, d_gate, d_up)):
            wide[k, :, cols] = value
            copy = pltpu.make_async_copy(
                wide.at[k, :, cols], wide_out[k].at[:, cols], sem_out.at[k, s]
            )
            copy.start()
            out_copies.append(copy)
        back = dot_nt(d_gate, gate_s) + dot_nt(d_up, up_s)
        ahead = dot(hidden, down_s)
        if s == 0:
            back_ref[...] = back
            ahead_ref[...] = ahead
        else:
            back_ref[...] += back
            ahead_ref[...] += ahead
    middle, back = middle_ref[...], back_ref[...]
    d_middle = jnp.where(keep, cot_ref[...], 0.0) + rms_back(middle, scale, back * gain)
    d_middle_out[...] = d_middle
    row_out[...] = d_middle.astype(BF)
    output[...] = jnp.where(keep, middle + ahead_ref[...], 0.0)
    gain_out[...] = jnp.zeros_like(gain_out)
    gain_out[0:1] = jnp.sum(back * (middle * scale), axis=0, keepdims=True)
    for copy in out_copies:
        copy.wait()


def mlp_call(info, gain, x, sums, cotangent, packs, devices):
    seq_len, model = x.shape
    blocks = packs[0].shape[0] * MEMBERS // devices
    own = packs[0].shape[1]
    inner = blocks // 3 * model
    wide = jax.ShapeDtypeStruct((seq_len, inner), BF)
    whole = jax.ShapeDtypeStruct((seq_len, model), F32)
    short = jax.ShapeDtypeStruct((seq_len, model), BF)
    count = inner // model
    return pl.pallas_call(
        mlp_kernel,
        out_shape=(wide, wide, wide, short, short, whole, short, whole)
        + (jax.ShapeDtypeStruct((8, model), F32),),
        in_specs=[SM] + [VM] * 6 + [ANY] * 10,
        out_specs=(ANY, ANY, ANY) + (VM,) * 6,
        scratch_shapes=[
            pltpu.VMEM((devices, blocks, own, model), BF),
            pltpu.VMEM((3, seq_len, inner), BF),
            pltpu.VMEM((seq_len, model), F32),
            pltpu.VMEM((seq_len, model), F32),
            pltpu.VMEM((seq_len, model), F32),
            pltpu.SemaphoreType.DMA((devices,)),
            pltpu.SemaphoreType.DMA((3, count)),
        ],
        **params(6_500_000_000, 16_000_000),
    )(info, gain, x, *sums, cotangent, *packs)


def mlp_grad_kernel(normed_ref, d_out_ref, hidden, d_gate, d_up, out, wide, total, sem, sem_out):
    model = normed_ref.shape[1]
    inner = wide.shape[2]
    count = inner // model
    groups, size_l, _, blocks, own, _ = total.shape
    copies = [
        pltpu.make_async_copy(source, wide.at[k], sem.at[k])
        for k, source in enumerate((d_gate, d_up, hidden))
    ]
    for copy in copies:
        copy.start()

    def turned(value):
        return jnp.transpose(value.astype(F32)).astype(BF)

    normed_t = turned(normed_ref[...])
    for k in range(2):
        copies[k].wait()
        for s in range(count):
            value = dot(normed_t, wide[k, :, pl.ds(s * model, model)]).astype(BF)
            value = value.reshape(HALVES, groups, size_l, own, model)
            for h in range(HALVES):
                total[:, :, h, k * count + s] = value[h]
    copies[2].wait()
    share = HALVES * groups // count
    for s in range(count):
        value = dot(turned(wide[2, :, pl.ds(s * model, model)]), d_out_ref[...]).astype(BF)
        h, at = s * share // groups, s * share % groups
        total[pl.ds(at, share), :, h, 2 * count :] = value.reshape(
            share, size_l, count, own, model
        )
    copy = pltpu.make_async_copy(total, out, sem_out)
    copy.start()
    copy.wait()


def mlp_grad_call(normed, d_out, hidden, d_gate, d_up, size_l):
    seq_len, inner = hidden.shape
    model = normed.shape[1]
    count = inner // model
    own = model // (HALVES * MEMBERS * size_l)
    shape = (MEMBERS, size_l, HALVES, 3 * count, own, model)
    return pl.pallas_call(
        mlp_grad_kernel,
        out_shape=jax.ShapeDtypeStruct(shape, BF),
        in_specs=[VM, VM, ANY, ANY, ANY],
        out_specs=ANY,
        scratch_shapes=[
            pltpu.VMEM((3, seq_len, inner), BF),
            pltpu.VMEM(shape, BF),
            pltpu.SemaphoreType.DMA((3,)),
            pltpu.SemaphoreType.DMA,
        ],
        **params(3_200_000_000, 14_000_000),
    )(normed, d_out, hidden, d_gate, d_up)


def body(
    inputs,
    cotangent,
    lengths,
    filters,
    gain_first,
    mix_plus,
    mix_minus,
    auto_weight,
    gain_second,
    w_gate,
    w_upward,
    w_down,
):
    _, seq_len, model = inputs.shape
    size_l = lax.axis_size("l")
    n = HALVES * MEMBERS * size_l
    h, m, l = lax.axis_index("h"), lax.axis_index(GROUP), lax.axis_index("l")
    me = (h * MEMBERS + m) * size_l + l
    own = gain_first.shape[0]
    inner = w_gate.shape[1]
    count = inner // model

    def blocks(w):
        return jnp.transpose(w.astype(BF).reshape(own, count, model), (1, 0, 2))

    pack = jnp.concatenate(
        [blocks(w_gate), blocks(w_upward), w_down.astype(BF).reshape(count, own, model)], axis=0
    )
    pack_rows = 3 * count * own
    plus, minus, auto = mix_plus.astype(BF), mix_minus.astype(BF), auto_weight.astype(BF)
    own_rows, lag_rows = plus.shape[0], auto.shape[0]
    share_rows = 2 * own_rows + lag_rows
    sizes, cuts = [], [0]
    if size_l == 2:
        a, b = own_rows * 13 // 24, own_rows // 3
        chunks = [
            pack.reshape(pack_rows, model),
            plus[:a],
            jnp.concatenate([plus[a:], minus[:b]], axis=0),
            jnp.concatenate([minus[b:], auto], axis=0),
        ]
        cuts = [0, 0, a, own_rows + b, share_rows]
        sizes = [part.shape[0] for part in chunks]
    far, pairs = [None] * 4, [None] * 5

    def cross(k):
        if size_l == 2:
            far[k] = flip(chunks[k], "h", 1)

    def cross_l(k):
        if size_l == 2:
            both = ([chunks[k]] if k < 4 else []) + ([far[k - 1]] if k else [])
            pairs[k] = flip(jnp.concatenate(both, axis=0) if len(both) > 1 else both[0], "l", 1)

    x = inputs[0]
    scale_one = rms_scale(x)
    pre_one = x * scale_one
    gains = jnp.concatenate([gain_first.astype(BF), gain_second.astype(BF)]).astype(F32)
    peers = HALVES * size_l
    here = lax.broadcasted_iota(jnp.int32, (peers, 1), 0) == h * size_l + l
    gains = jnp.where(here, gains[None], 0.0).reshape(1, -1)
    gains = sum_peers(gains)[0]
    line = jnp.concatenate(
        [
            gains.astype(BF),
            (lengths // 16).astype(BF),
            (lengths % 16).astype(BF),
            jnp.zeros((model - 2 * own * peers - 2,), BF),
        ]
    )
    below = lax.broadcasted_iota(jnp.int32, (32, 1), 0) == 0
    below = jnp.where(below, line[None, :], 0.0).astype(BF)
    row = Gather(jnp.concatenate([pre_one.astype(BF), below], axis=0))

    cross(0)
    cross_l(0)
    if size_l == 2:
        row.row, filters, far[0], pairs[0], *chunks[1:] = sync_all(
            row.row, filters, far[0], pairs[0], *chunks[1:]
        )
    cross(1)
    cross_l(1)
    row.first()
    fwd_table, bwd_table = build_tables(filters, h, m)

    far, pairs, row, fwd_table = sync_all(far, pairs, row, fwd_table)
    if size_l == 2:
        *chunks[2:], far[1] = sync_all(*chunks[2:], far[1])
    cross(2)
    cross_l(2)
    row.second(core=False)
    row.core1 = flip(row.near1, "m", 1)
    late = sync_all(m, row.near1)[0]
    members = late ^ lax.iota(jnp.int32, MEMBERS)
    place = jnp.concatenate([jnp.stack([late % 2]), members, jnp.stack([h, l])])

    col = lax.broadcasted_iota(jnp.int32, (LAGS, model, BLOCK), 2)
    feature = lax.broadcasted_iota(jnp.int32, (LAGS, model, BLOCK), 1)
    feature = (feature + (late % 2) * BLOCK) % model
    lag = lax.broadcasted_iota(jnp.int32, (LAGS, model, BLOCK), 0)
    lag_span = lag_rows * size_l
    rel = col // lag_span
    source = lag_span * (MEMBERS * (h ^ rel) + late) + col % lag_span
    pick = ((rel < 2) & (source == lag * model + feature)).astype(BF)

    far, pairs, row, pick, place = sync_all(far, pairs, row, pick, place)
    if size_l == 2:
        chunks[3], far[2] = sync_all(chunks[3], far[2])
    cross(3)
    cross_l(3)
    row.third()
    row.core2 = flip(row.near2, "m", 1)
    if size_l == 2:
        held = [chunks[0], pairs[0], far[0], pairs[1][sizes[1] :]]
    else:
        held = [lax.all_gather(part, "l", axis=0) for part in (pack, flip(pack, "h", 1))]
    pack = Gather(jnp.concatenate(held, axis=0).reshape(-1, own, model))
    pack.first()
    x_rows = row.result()
    spec, info, gains = conv_call(own, n, place, fwd_table, pick, x_rows, seq_len)

    far, pairs, gains, spec = sync_all(far, pairs, gains, spec)
    cross_l(4)
    pack = sync_all(pack, spec)[0]
    pack.second()

    pairs, gains, spec = sync_all(pairs, gains, spec)
    gain_one = gains[:, :own].reshape(1, model)
    gain_two = gains[:, own : 2 * own].reshape(1, model)
    plan, pieces = [], []
    if size_l == 2:
        for k in (1, 2, 3):
            at, size = cuts[k], sizes[k]
            plan.append((0, "mine", at, size, own_rows, 0))
            plan.append((1, "mine", at, size, own_rows, 0))
            plan.append((0, "other", at, size, own_rows, 0))
            plan.append((1, "other", at, size, own_rows, sizes[k + 1] if k < 3 else 0))
            pieces += [chunks[k], far[k], pairs[k], pairs[k + 1]]
        lag_weight = jnp.zeros((BLOCK, model), BF)
    else:
        share = jnp.concatenate([plus, minus, auto], axis=0)
        shares = lax.all_gather(share, ("h", "l"), axis=0)
        shares = shares.reshape((HALVES, size_l) + share.shape)
        lag_weight = []
        for rel in range(HALVES):
            half = lax.dynamic_index_in_dim(shares, h ^ rel, 0, keepdims=False)
            lag_weight.append(half[:, 2 * own_rows :])
            for k in range(size_l):
                plan.append((rel, k, 0, 2 * own_rows, own_rows, 0))
                pieces.append(half[k, : 2 * own_rows])
        lag_weight = jnp.stack(lag_weight).reshape(HALVES * lag_span, model)
        lag_weight = jnp.pad(lag_weight, ((0, BLOCK - HALVES * lag_span), (0, 0)))
    plan = tuple(plan)
    mixed = Reduce(mix_call(info, plan, own, lag_span, gains, lag_weight, spec, pieces))

    mixed, pack = sync_all(mixed, pack)
    mixed.first()
    mixed = sync_all(mixed)[0]
    mixed.second()
    pack.third()
    mixed = sync_all(mixed)[0]
    mixed = mixed.third()

    hidden, d_gate, d_up, normed_two, d_out_b, d_middle, d_row, output, grad_gain_two = mlp_call(
        info, gain_two, x, mixed, cotangent[0], pack.result(), n
    )
    grad_gain_two = grad_gain_two[0:1]

    row = Gather(d_row)
    row.first()

    mlp = mlp_grad_call(normed_two, d_out_b, hidden, d_gate, d_up, size_l)

    row, mlp = sync_all(row, mlp)
    row.second()

    row, grad_gain_two, mlp = sync_all(row, grad_gain_two, mlp)
    mlp = lax.psum_scatter(mlp, GROUP, scatter_dimension=0)
    row.third()
    d_rows = row.result()
    if size_l == 2:
        cut = share_rows * 5 // 8 - 14
        cuts = (
            ((3, 0, cut),),
            ((3, cut, share_rows), (1, 0, share_rows)),
            ((2, 0, cut),),
            ((2, cut, share_rows),),
            ((0, 0, share_rows),),
        )
    else:
        cuts = tuple(((k, 0, share_rows),) for k in range(HALVES * size_l))
    *grad_mix, gain_mix = grad_call(
        info, plan, own, gains, lag_weight, spec, pieces, d_rows, size_l, lag_rows, cuts
    )

    grad_mix, d_rows = sync_all(grad_mix, d_rows)
    grad_gains = jnp.concatenate([gain_mix[0:1], grad_gain_two], axis=0)
    grad_gains = sum_direct(grad_gains, GROUP, 3)
    grad_gains = sum_direct(grad_gains, GROUP, 4)
    if size_l == 2:
        got_far, got_rest = flip(grad_mix[0], "l", 1), flip(grad_mix[1], "l", 1)
        d_rows, got_far, grad_gains = sync_all(d_rows, got_far, grad_gains)
        back = [flip((grad_mix[2].astype(F32) + got_far.astype(F32)).astype(BF), "h", 1)]
    d_normed = Reduce(back_conv_call(info, plan, bwd_table, pick, lag_weight, pieces, d_rows))

    if size_l == 2:
        d_normed, back, got_rest = sync_all(d_normed, back, got_rest)
    d_normed.first()

    d_normed, grad_gains, mlp = sync_all(d_normed, grad_gains, mlp)
    d_normed.second()
    if size_l == 2:
        got_rest = sync_all(got_rest, d_normed.own)[0]
        left = share_rows - cut
        part = (grad_mix[3].astype(F32) + got_rest[:left].astype(F32)).astype(BF)
        back.append(flip(part, "h", 1))
        other = lax.dynamic_index_in_dim(mlp, 1 - l, 0, keepdims=False)
        mlp = lax.dynamic_index_in_dim(mlp, l, 0, keepdims=False).astype(F32)
        blocks_left = other.shape[0] * other.shape[1]
        other = jnp.concatenate(
            [other.reshape((blocks_left,) + other.shape[2:]), two_parts(grad_gains, own)], axis=0
        )
        other = flip(other, "l", 1)
        grad_gains = grad_gains + whole_of(other[blocks_left])
        mlp = mlp + other[:blocks_left].reshape(mlp.shape).astype(F32)
    else:
        grad_gains = lax.psum(grad_gains, "l")
        mlp = lax.psum_scatter(mlp.astype(F32), "l", scatter_dimension=0)

    d_normed = sync_all(d_normed)[0]
    if size_l == 2:
        grad_gains, mlp = sync_all(grad_gains, mlp, d_normed.near1, d_normed.near2)[:2]
        back, got_rest = sync_all(back, got_rest, d_normed.near1, mlp)[:2]
    else:
        grad_gains, mlp = sync_all(grad_gains, mlp, d_normed.near1)[:2]
    d_normed = d_normed.third()
    if size_l == 2:
        other = lax.dynamic_index_in_dim(mlp, 1 - h, 0, keepdims=False).astype(BF)
        other = flip(jnp.concatenate([other, two_parts(grad_gains, own)], axis=0), "h", 1)
        mlp = lax.dynamic_index_in_dim(mlp, h, 0, keepdims=False) + other[:-1].astype(F32)
        grad_gains = grad_gains + whole_of(other[-1])
    else:
        mlp_far = lax.dynamic_index_in_dim(mlp, 1 - h, 0, keepdims=False).astype(BF)
        mlp_near = lax.dynamic_index_in_dim(mlp, h, 0, keepdims=False)
        mlp = mlp_near + flip(mlp_far, "h", 1).astype(F32)
        grad_gains = grad_gains + flip(grad_gains, "h", 1)
    grad_gains = lax.dynamic_slice_in_dim(grad_gains, me * own, own, 1)
    own_sum, got1, got2 = d_normed
    d_normed = own_sum + got1.astype(F32) + got2.astype(F32)
    input_grad = d_middle + rms_back(x, scale_one, d_normed * gain_one)
    if size_l == 2:
        near = grad_mix[4].astype(F32) + got_rest[left:].astype(F32)
        grad_mix = near + jnp.concatenate(back, axis=0).astype(F32)
    else:
        both = jnp.stack(grad_mix).reshape((HALVES, size_l) + grad_mix[0].shape)
        grad_mix = jnp.where(h == 0, both, both[::-1]).reshape((-1,) + both.shape[2:])
        grad_mix = lax.psum_scatter(grad_mix, ("h", "l"), scatter_dimension=0).astype(F32)
    mlp = mlp.reshape(3, count, own, model)
    grad_gate, grad_up = [
        jnp.transpose(mlp[k], (1, 0, 2)).reshape(own, inner) for k in range(2)
    ]
    grad_down = mlp[2].reshape(count * own, model)

    return (
        output[None],
        input_grad[None],
        grad_gains[0],
        grad_mix[:own_rows],
        grad_mix[own_rows : 2 * own_rows],
        grad_mix[2 * own_rows :],
        grad_gains[1],
        grad_gate,
        grad_up,
        grad_down,
    )


def solution(mesh):
    shape = (HALVES, 2, 2, 2, mesh.size // (HALVES * MEMBERS))
    inner = Mesh(mesh.devices.reshape(shape), ALL)
    row, vec, mat = P(ALL, None, None), P(ALL), P(ALL, None)
    in_specs = (row, row, vec, P(), vec, mat, mat, mat, vec, mat, mat, mat)
    out_specs = (row, row, vec, mat, mat, mat, vec, mat, mat, mat)
    return jax.shard_map(body, mesh=inner, in_specs=in_specs, out_specs=out_specs, check_vma=False)
```

```python
import functools

import jax
import jax.numpy as jnp
from jax import lax
from jax.experimental import pallas as pl
from jax.experimental.pallas import tpu as pltpu
from jax.sharding import Mesh, PartitionSpec as P

EPSILON = 1e-05
MEMBERS = 8
HALVES = 2
BLOCK = 256
LAGS = 3
VMEM_LIMIT = 60 * 1024 * 1024
BF = jnp.bfloat16
F32 = jnp.float32
GROUP = ("z", "y", "c")
ALL = ("h",) + GROUP + ("l",)
ANY = pl.BlockSpec(memory_space=pl.ANY)
VM = pl.BlockSpec(memory_space=pltpu.VMEM)
SM = pl.BlockSpec(memory_space=pltpu.SMEM)


def rms_scale(values):
    return lax.rsqrt(jnp.mean(values * values, axis=-1, keepdims=True) + EPSILON)


def rms_back(values, scale, d_pre):
    return scale * d_pre - values * (scale * scale * scale) * jnp.mean(
        d_pre * values, axis=-1, keepdims=True
    )


def flip(x, axis, bit):
    if axis == "m":
        axis, bit = {1: "c", 2: "y", 4: "z"}[bit], 1
    size = lax.axis_size(axis)
    return lax.ppermute(x, axis, [(i, i ^ bit) for i in range(size)])


def after(x, *earlier):
    return lax.optimization_barrier((x, earlier))[0]


def dot(a, b):
    return jnp.dot(a, b, preferred_element_type=F32)


def dot_nt(a, b):
    return lax.dot_general(a, b, (((1,), (1,)), ((), ())), preferred_element_type=F32)


def arrays_of(value):
    if hasattr(value, "__dict__"):
        return {k: v for k, v in vars(value).items() if not isinstance(v, (int, str))}
    if isinstance(value, (list, tuple)):
        return [arrays_of(v) for v in value]
    return value


def with_arrays(value, arrays):
    if hasattr(value, "__dict__"):
        fresh = object.__new__(type(value))
        fresh.__dict__.update(vars(value))
        fresh.__dict__.update(arrays)
        return fresh
    if isinstance(value, (list, tuple)):
        return type(value)(with_arrays(v, a) for v, a in zip(value, arrays))
    return arrays


def sync(*values):
    return lax.optimization_barrier(values)


def sync_all(*values):
    leaves, tree = jax.tree.flatten([arrays_of(v) for v in values])
    kept = [k for k, leaf in enumerate(leaves) if isinstance(leaf, jax.Array)]
    for k, new in zip(kept, lax.optimization_barrier([leaves[k] for k in kept])):
        leaves[k] = new
    fresh = jax.tree.unflatten(tree, leaves)
    return tuple(with_arrays(v, a) for v, a in zip(values, fresh))


class Gather:
    def __init__(self, row):
        self.row = row
        self.half = row.shape[0] // 2

    def first(self):
        self.near1, self.near2 = flip(self.row, "m", 2), flip(self.row, "m", 4)
        self.core0 = flip(self.row, "m", 1)

    def second(self, core=True):
        self.top = flip(self.near2[: self.half], "m", 2)
        self.low = flip(self.near1[self.half :], "m", 4)
        if core:
            self.core1, self.core2 = flip(self.near1, "m", 1), flip(self.near2, "m", 1)

    def third(self):
        self.core_top, self.core_low = flip(self.top, "m", 1), flip(self.low, "m", 1)

    def result(self):
        return (
            self.row,
            self.core0,
            self.near1,
            self.core1,
            self.near2,
            self.core2,
            self.top,
            self.low,
            self.core_top,
            self.core_low,
        )


class Reduce:
    def __init__(self, parts):
        self.parts = parts
        self.half = parts[0].shape[0] // 2

    def first(self):
        own, core0, near1, core1, near2, core2, top, low, core_top, core_low = self.parts
        self.own = own.astype(F32) + flip(core0, "m", 1).astype(F32)
        self.near1 = near1.astype(F32) + flip(core1, "m", 1).astype(F32)
        self.near2 = near2.astype(F32) + flip(core2, "m", 1).astype(F32)
        self.top = (top.astype(F32) + flip(core_top, "m", 1).astype(F32)).astype(BF)
        self.low = (low.astype(F32) + flip(core_low, "m", 1).astype(F32)).astype(BF)

    def second(self):
        half = self.half
        got_top = flip(self.top, "m", 2).astype(F32)
        got_low = flip(self.low, "m", 4).astype(F32)
        near1, near2 = self.near1, self.near2
        self.near1 = jnp.concatenate([near1[:half], near1[half:] + got_low], axis=0).astype(BF)
        self.near2 = jnp.concatenate([near2[:half] + got_top, near2[half:]], axis=0).astype(BF)

    def third(self):
        return self.own, flip(self.near1, "m", 2), flip(self.near2, "m", 4)


def gather_l(x):
    size = lax.axis_size("l")
    if size != 2:
        return lax.all_gather(x, "l", axis=0, tiled=True)
    peer = flip(x, "l", 1)
    first = lax.axis_index("l") == 0
    return jnp.concatenate([jnp.where(first, x, peer), jnp.where(first, peer, x)], axis=0)


def scatter_l(x, axis):
    size = lax.axis_size("l")
    if size != 2:
        return lax.psum_scatter(x.astype(F32), "l", scatter_dimension=axis, tiled=True)
    part = x.shape[axis] // 2
    mine = lax.axis_index("l")
    kept = lax.dynamic_slice_in_dim(x, mine * part, part, axis)
    sent = lax.dynamic_slice_in_dim(x, (1 - mine) * part, part, axis)
    return kept.astype(F32) + flip(sent.astype(BF), "l", 1).astype(F32)


def sum_direct(x, axes, bits):
    total = x
    size = 1
    for axis in axes:
        size *= lax.axis_size(axis)
    for mask in range(1, size):
        if mask & ~bits == 0:
            total = total + lax.ppermute(x, axes, [(i, i ^ mask) for i in range(size)])
    return total


def sum_peers(x):
    size = HALVES * lax.axis_size("l")
    if size == 4:
        return sum_direct(x, ("h", "l"), 3)
    step = 1
    while step < size:
        x = x + lax.ppermute(x, ("h", "l"), [(i, i ^ step) for i in range(size)])
        step *= 2
    return x


def two_parts(values, rows):
    high = values.astype(BF)
    low = (values - high.astype(F32)).astype(BF)
    return jnp.pad(jnp.concatenate([high, low], axis=0), ((0, rows - 4), (0, 0)))[None]


def whole_of(block):
    return block[0:2].astype(F32) + block[2:4].astype(F32)


def tables_kernel(base_ref, fwd_ref, bwd_ref):
    rows, width = fwd_ref.shape[1], fwd_ref.shape[2]
    span = base_ref.shape[1]
    odd = (
        lax.broadcasted_iota(jnp.int32, (rows, width), 0)
        + lax.broadcasted_iota(jnp.int32, (rows, width), 1)
    ) % 2
    sign = (1 - 2 * odd).astype(F32)
    for index in range(4):
        for which, out in ((0, fwd_ref), (1, bwd_ref)):
            line = jnp.broadcast_to(base_ref[pl.ds(which * 4 + index, 1), :], (rows, span))
            rolled = pltpu.roll(line, 0, 1, stride=1, stride_axis=0)[:, :width]
            out[2 * index] = rolled.astype(BF)
            out[2 * index + 1] = (rolled * sign).astype(BF)


def build_tables(filters, h, m):
    seq_len, count = filters.shape
    phi = jnp.transpose(filters.astype(BF).astype(F32))
    zeros = jnp.zeros((count, BLOCK), F32)
    bwd = jnp.concatenate([phi, zeros], axis=1)
    back = jnp.flip(phi, axis=1)
    fwd = jnp.concatenate(
        [
            back[:, seq_len - 1 - BLOCK :],
            jnp.zeros((count, BLOCK), F32),
            back[:, : seq_len - 1 - BLOCK],
        ],
        axis=1,
    )
    rows = []
    for table in (fwd, bwd):
        for rel in range(HALVES):
            first = 12 * (h ^ rel) + (3 * m) // 2
            rows.append(lax.dynamic_slice_in_dim(table, first, 2, 0))
    base = jnp.concatenate(rows, axis=0)
    shape = jax.ShapeDtypeStruct((8, BLOCK, seq_len), BF)
    return pl.pallas_call(
        tables_kernel,
        out_shape=(shape, shape),
        in_specs=[VM],
        out_specs=(VM, VM),
        compiler_params=pltpu.CompilerParams(vmem_limit_bytes=VMEM_LIMIT),
        cost_estimate=pl.CostEstimate(flops=20_000_000, bytes_accessed=5_000_000, transcendentals=0),
    )(base)


def load_rows(refs, scratch, sem):
    started = []
    for j in range(MEMBERS):
        for ref, first, size in used_parts(refs, j, scratch.shape[1]):
            into = scratch.at[j, pl.ds(first, size)]
            started.append(pltpu.make_async_copy(ref, into, sem.at[len(started)]))
            started[-1].start()
    return started


def row_stores(scratch, refs, j, sem):
    copies = []
    for k, (ref, first) in enumerate(halves_of(refs, j)):
        source = scratch.at[j, pl.ds(first, ref.shape[0])]
        copies.append(pltpu.make_async_copy(source, ref, sem.at[j, k]))
    return copies


def halves_of(refs, j):
    if j < 6:
        return [(refs[j], 0)]
    return [(refs[2 * j - 6], 0), (refs[2 * j - 5], refs[2 * j - 6].shape[0])]


def used_parts(refs, j, tokens):
    found = []
    for ref, first in halves_of(refs, j):
        size = min(ref.shape[0], tokens - first)
        if size > 0:
            found.append((ref.at[pl.ds(0, size)], first, size))
    return found


def unused_parts(refs, j, tokens):
    found = []
    for ref, first in halves_of(refs, j):
        start = max(tokens - first, 0)
        if start < ref.shape[0]:
            found.append((ref.at[pl.ds(start, ref.shape[0] - start)], ref.shape[0] - start))
    return found


def place(info, r):
    return pl.multiple_of(info[19 + r], 128)


def packed_copies(info, refs, packed, sem, act):
    for j in range(MEMBERS):

        def run(tokens, j=j):
            for k, (ref, first, size) in enumerate(used_parts(refs, j, tokens)):
                into = packed.at[pl.ds(place(info, j) + first, size)]
                act(pltpu.make_async_copy(ref, into, sem.at[j, k]))

        by_length(info[j], run)


def unpacked_copies(info, packed, zeros, refs, sem, act, low=None, high=None):
    for j in range(MEMBERS):

        def run(tokens, j=j):
            k = 0
            for ref, first, size in used_parts(refs, j, tokens):
                source = packed.at[pl.ds(place(info, j) + first, size)]
                act(pltpu.make_async_copy(source, ref, sem.at[j, k]))
                k += 1
            for ref, size in unused_parts(refs, j, tokens):
                act(pltpu.make_async_copy(zeros.at[pl.ds(0, size)], ref, sem.at[j, k]))
                k += 1

        if low is None:
            by_length(info[j], run)
        else:
            end = info[20 + j]
            pl.when((end > low) & (end <= high))(functools.partial(by_length, info[j], run))


def chunk_copies(info, spec_in, spec, sem, act):
    count, rows = spec.shape[0], spec.shape[1]
    for c in range(count):

        @pl.when(c * rows < info[27])
        def _(c=c):
            act(pltpu.make_async_copy(spec_in.at[pl.ds(c * rows, rows)], spec.at[c], sem.at[c]))


def chunks_of(info, rows):
    return lax.div(info[27] + (rows - 1), rows)


def weight_copies(info, plan, pieces, weight, sem):
    copies = []
    for piece, (rel, l, begin, size, own, source) in zip(pieces, plan):
        l = info[18] if l == "mine" else 1 - info[18] if l == "other" else l
        end = begin + size
        areas = [(0, own, rel * 6 * BLOCK), (own, 2 * own, (rel * 2 + 1) * 3 * BLOCK)]
        if end > 2 * own:
            lags = end - 2 * own
            areas.append((2 * own, end, 12 * BLOCK + rel * 2 * lags))
        for first, last, target in areas:
            low, high = max(first, begin), min(last, end)
            if low < high:
                to = target + l * (last - first) + (low - first)
                if not isinstance(to, int):
                    to = pl.multiple_of(to, 16)
                copies.append(
                    pltpu.make_async_copy(
                        piece.at[pl.ds(source + low - begin, high - low)],
                        weight.at[pl.ds(to, high - low)],
                        sem.at[len(copies)],
                    )
                )
    return copies


def start(copy):
    copy.start()


def finish(copy):
    copy.wait()


def by_length(length, run):
    for tokens in range(128, 513, 128):
        pl.when((length > tokens - 128) & (length <= tokens))(functools.partial(run, tokens))


def combos(info):
    middle = info[8]
    for rel in range(HALVES):
        for sign in range(2):
            for pos, which in enumerate((0, middle, 1)):
                block = (rel * 2 + sign) * 3 + pos
                yield block, rel * 4 + which * 2 + sign, pos % 2


def gain_columns(table_ref, feature, own):
    devices = table_ref.shape[0]
    shift = own.bit_length() - 1
    rows = feature.shape[0]
    device = lax.broadcasted_iota(jnp.int32, (rows, devices), 1)
    chosen = (device == (feature >> shift)).astype(BF)
    found = dot(chosen, table_ref[...].astype(BF))
    lane = lax.broadcasted_iota(jnp.int32, found.shape, 1)
    return jnp.sum(jnp.where(lane == (feature & (own - 1)), found, 0.0), axis=1, keepdims=True)


def feature_places(info, model, lag_span):
    line = lax.broadcasted_iota(jnp.int32, (BLOCK, 1), 0)
    rel = (line >= lag_span).astype(jnp.int32)
    source = lag_span * (MEMBERS * (info[17] ^ rel) + info[9]) + line - rel * lag_span
    return [line + info[8] * BLOCK, line + (1 - info[8]) * BLOCK, source & (model - 1)]


def feature_gains(info, table_ref, model, own, lag_span):
    return [
        gain_columns(table_ref, feature, own) for feature in feature_places(info, model, lag_span)
    ]


def read_lines(own, place_ref, lines, info, gains, seq_len):
    lane = lax.broadcasted_iota(jnp.int32, (1, 128), 1)
    weights = jnp.where(lane == 0, 16.0, jnp.where(lane == 1, 1.0, 0.0))
    total = jnp.int32(0)
    size_l = gains.shape[0] // (HALVES * MEMBERS)
    for k in range(11):
        info[8 + k] = place_ref[k]
    for j in range(MEMBERS):
        line = lines[j, :, :256].astype(F32)[0:1]
        length = jnp.sum(line[:, 128:] * weights).astype(jnp.int32)
        info[j] = length
        info[19 + j] = total
        total = total + ((length + 127) >> 7 << 7)
        for peer in range(HALVES * size_l):
            device = (peer // size_l * MEMBERS + info[9 + j]) * size_l + peer % size_l
            gains[pl.ds(device, 1), pl.ds(0, 2 * own)] = line[
                :, 2 * own * peer : 2 * own * (peer + 1)
            ]
    info[27] = total


def conv_kernel(own, place_ref, table_ref, pick_ref, *refs):
    rows_in = refs[:10]
    spec_out, info, gains = refs[10:13]
    stack, lines, normed, spec, sem_in, sem_line, sem_spec = refs[13:]
    seq_len = stack.shape[1]
    line_copies = []
    for j in range(MEMBERS):
        ref, first = halves_of(rows_in, j)[-1]
        source = ref.at[pl.ds(seq_len - first, lines.shape[1])]
        line_copies.append(pltpu.make_async_copy(source, lines.at[j], sem_line.at[j]))
        line_copies[-1].start()
    loads = load_rows(rows_in, stack, sem_in)
    gains[...] = jnp.zeros_like(gains)
    for copy in line_copies:
        copy.wait()
    read_lines(own, place_ref, lines, info, gains, seq_len)
    for copy in loads:
        copy.wait()
    odd = info[8] == 1

    def spec_copy(r, tokens):
        slot = lax.rem(r, 2)
        return pltpu.make_async_copy(
            spec.at[slot, pl.ds(0, tokens)],
            spec_out.at[pl.ds(place(info, r), tokens)],
            sem_spec.at[slot],
        )

    def row(r, carry):
        slot = lax.rem(r, 2)

        @pl.when(r >= 2)
        def _():
            by_length(info[r - 2], lambda tokens: spec_copy(r - 2, tokens).wait())

        def run(tokens):
            left = stack[r, pl.ds(0, tokens), :BLOCK]
            right = stack[r, pl.ds(0, tokens), BLOCK:]
            normed[pl.ds(0, tokens), :BLOCK] = jnp.where(odd, right, left)
            normed[pl.ds(0, tokens), BLOCK:] = jnp.where(odd, left, right)
            first = min(tokens, BLOCK)
            for block, table, side in combos(info):
                cols = pl.ds(side * BLOCK, BLOCK)
                into = pl.ds(block * BLOCK, BLOCK)
                spec[slot, pl.ds(0, first), into] = dot(
                    table_ref[table, pl.ds(0, first), pl.ds(BLOCK, first)],
                    normed[pl.ds(0, first), cols],
                ).astype(BF)
                if tokens > BLOCK:
                    rest = pl.ds(0, tokens - BLOCK)
                    spec[slot, pl.ds(BLOCK, tokens - BLOCK), into] = dot(
                        table_ref[table, rest, pl.ds(0, tokens)], normed[pl.ds(0, tokens), cols]
                    ).astype(BF)
            lagged = None
            for lag in range(LAGS):
                moved = dot(normed[pl.ds(0, tokens)], pick_ref[lag])
                if lag:
                    moved = jnp.concatenate(
                        [jnp.zeros((lag, BLOCK), F32), moved[: tokens - lag]], axis=0
                    )
                lagged = moved if lagged is None else lagged + moved
            spec[slot, pl.ds(0, tokens), pl.ds(12 * BLOCK, BLOCK)] = lagged.astype(BF)
            spec_copy(r, tokens).start()

        by_length(info[r], run)
        return carry

    lax.fori_loop(0, MEMBERS, row, 0)
    for r in (MEMBERS - 2, MEMBERS - 1):
        by_length(info[r], lambda tokens, r=r: spec_copy(r, tokens).wait())


def row_shapes(seq_len, model):
    whole = jax.ShapeDtypeStruct((seq_len, model), BF)
    half = jax.ShapeDtypeStruct((seq_len // 2, model), BF)
    return (whole,) * 6 + (half,) * 4


def params(flops, data):
    return dict(
        compiler_params=pltpu.CompilerParams(vmem_limit_bytes=VMEM_LIMIT),
        cost_estimate=pl.CostEstimate(flops=flops, bytes_accessed=data, transcendentals=0),
    )


def conv_call(own, devices, place, table, pick, rows, seq_len):
    model = rows[0].shape[1]
    features = 13 * BLOCK
    return pl.pallas_call(
        functools.partial(conv_kernel, own),
        out_shape=(
            jax.ShapeDtypeStruct((MEMBERS * seq_len, features), BF),
            jax.ShapeDtypeStruct((32,), jnp.int32),
            jax.ShapeDtypeStruct((devices, 128), F32),
        ),
        in_specs=[SM, VM, VM] + [ANY] * 10,
        out_specs=(ANY, SM, VM),
        scratch_shapes=[
            pltpu.VMEM((MEMBERS, seq_len, model), BF),
            pltpu.VMEM((MEMBERS, 16, model), BF),
            pltpu.VMEM((seq_len, model), BF),
            pltpu.VMEM((2, seq_len, features), BF),
            pltpu.SemaphoreType.DMA((10,)),
            pltpu.SemaphoreType.DMA((MEMBERS,)),
            pltpu.SemaphoreType.DMA((2,)),
        ],
        **params(5_000_000_000, 20_000_000),
    )(place, table, pick, *rows)


def mix_kernel(plan, own, lag_span, info, gain_ref, lag_ref, spec_in, *refs):
    pieces, refs = refs[: len(plan)], refs[len(plan) :]
    parts_out = refs[:10]
    weight, spec, parts, zeros, sem_in, sem_out, sem_spec = refs[10:]
    weight[pl.ds(12 * BLOCK, BLOCK)] = lag_ref[...]
    copies = weight_copies(info, plan, pieces, weight, sem_in)
    for copy in copies:
        copy.start()
    chunk_copies(info, spec_in, spec, sem_spec, start)
    zeros[...] = jnp.zeros_like(zeros)
    rows = spec.shape[1]
    for copy in copies:
        copy.wait()
    columns = feature_gains(info, gain_ref, weight.shape[1], own, lag_span)
    for block in range(weight.shape[0] // BLOCK):
        at = pl.ds(block * BLOCK, BLOCK)
        column = columns[2 if block == 12 else block % 3 % 2]
        weight[at] = (weight[at].astype(F32) * column).astype(BF)

    def chunk(c, carry):
        here = pl.ds(pl.multiple_of(c * rows, rows), rows)
        pltpu.make_async_copy(spec_in.at[here], spec.at[c], sem_spec.at[c]).wait()
        parts[here] = dot(spec[c], weight[...]).astype(BF)
        unpacked_copies(
            info, parts, zeros, parts_out, sem_out, start, c * rows, c * rows + rows
        )
        return carry

    lax.fori_loop(0, chunks_of(info, rows), chunk, 0)
    unpacked_copies(info, parts, zeros, parts_out, sem_out, finish)


def mix_call(info, plan, own, lag_span, gain, lag_weight, spec, pieces):
    tokens, features = spec.shape
    model = pieces[0].shape[-1]
    seq_len = tokens // MEMBERS
    return pl.pallas_call(
        functools.partial(mix_kernel, plan, own, lag_span),
        out_shape=row_shapes(seq_len, model),
        in_specs=[SM, VM, VM, ANY] + [ANY] * len(plan),
        out_specs=(ANY,) * 10,
        scratch_shapes=[
            pltpu.VMEM((features, model), BF),
            pltpu.VMEM((MEMBERS, seq_len, features), BF),
            pltpu.VMEM((tokens, model), BF),
            pltpu.VMEM((seq_len, model), BF),
            pltpu.SemaphoreType.DMA((3 * len(plan),)),
            pltpu.SemaphoreType.DMA((MEMBERS, 3)),
            pltpu.SemaphoreType.DMA((MEMBERS,)),
        ],
        **params(8_000_000_000, 30_000_000),
    )(info, gain, lag_weight, spec, *pieces)


def back_conv_kernel(plan, info, table_ref, pick_ref, lag_ref, *refs):
    pieces, refs = refs[: len(plan)], refs[len(plan) :]
    rows_in, parts_out = refs[:10], refs[10:20]
    d_mix, d_spec, parts, weight, sem_in, sem_out, sem_w = refs[20:]
    packed_copies(info, rows_in, d_mix, sem_in, start)
    weight[pl.ds(12 * BLOCK, BLOCK)] = lag_ref[...]
    copies = weight_copies(info, plan, pieces, weight, sem_w)
    for copy in copies:
        copy.start()
    _, seq_len, model = parts.shape
    features = d_spec.shape[1]
    odd = info[8] == 1
    packed_copies(info, rows_in, d_mix, sem_in, finish)
    for copy in copies:
        copy.wait()

    def chunk(c, carry):
        here = pl.ds(pl.multiple_of(c * seq_len, seq_len), seq_len)
        dm = d_mix[here]
        for block in range(features // BLOCK):
            cols = pl.ds(block * BLOCK, BLOCK)
            d_spec[here, cols] = dot_nt(dm, weight[cols]).astype(BF)
        return carry

    lax.fori_loop(0, chunks_of(info, seq_len), chunk, 0)

    def row(r, carry):
        at_row = place(info, r)

        def run(tokens):
            here = pl.ds(at_row, tokens)
            first = min(tokens, BLOCK)
            sides = [[None, None], [None, None]]
            for block, table, side in combos(info):
                cols = pl.ds(block * BLOCK, BLOCK)
                term = dot(table_ref[table, pl.ds(0, first), pl.ds(0, tokens)], d_spec[here, cols])
                sides[side][0] = term if sides[side][0] is None else sides[side][0] + term
                if tokens > BLOCK:
                    rest = pl.ds(0, tokens - BLOCK)
                    term = dot(
                        table_ref[table, rest, rest],
                        d_spec[pl.ds(at_row + BLOCK, tokens - BLOCK), cols],
                    )
                    sides[side][1] = term if sides[side][1] is None else sides[side][1] + term
            d_lag = d_spec[here, pl.ds(12 * BLOCK, BLOCK)]
            back = None
            for lag in range(LAGS):
                moved = dot_nt(d_lag, pick_ref[lag])
                if lag:
                    moved = jnp.concatenate(
                        [moved[lag:], jnp.zeros((lag, model), F32)], axis=0
                    )
                back = moved if back is None else back + moved
            for begin in range(0, tokens, BLOCK):
                size = min(BLOCK, tokens - begin)
                k = begin // BLOCK
                at = pl.ds(begin, size)
                d_a = sides[0][k] + back[begin : begin + size, :BLOCK]
                d_b = sides[1][k] + back[begin : begin + size, BLOCK:]
                left, right = jnp.where(odd, d_b, d_a), jnp.where(odd, d_a, d_b)
                parts[r, at, :BLOCK] = left.astype(BF)
                parts[r, at, BLOCK:] = right.astype(BF)
            if tokens < parts.shape[1]:
                rest = parts.shape[1] - tokens
                parts[r, pl.ds(tokens, rest)] = jnp.zeros((rest, model), BF)

        by_length(info[r], run)
        for j in range(MEMBERS):

            @pl.when(r == j)
            def _(j=j):
                for copy in row_stores(parts, parts_out, j, sem_out):
                    copy.start()

        return carry

    lax.fori_loop(0, MEMBERS, row, 0)
    for j in range(MEMBERS):
        for copy in row_stores(parts, parts_out, j, sem_out):
            copy.wait()


def back_conv_call(info, plan, table, pick, lag_weight, pieces, rows):
    seq_len, model = rows[0].shape
    features = 13 * BLOCK
    return pl.pallas_call(
        functools.partial(back_conv_kernel, plan),
        out_shape=row_shapes(seq_len, model),
        in_specs=[SM, VM, VM, VM] + [ANY] * (10 + len(plan)),
        out_specs=(ANY,) * 10,
        scratch_shapes=[
            pltpu.VMEM((MEMBERS * seq_len, model), BF),
            pltpu.VMEM((MEMBERS * seq_len, features), BF),
            pltpu.VMEM((MEMBERS, seq_len, model), BF),
            pltpu.VMEM((features, model), BF),
            pltpu.SemaphoreType.DMA((MEMBERS, 2)),
            pltpu.SemaphoreType.DMA((MEMBERS, 2)),
            pltpu.SemaphoreType.DMA((3 * len(plan),)),
        ],
        **params(12_000_000_000, 20_000_000),
    )(info, table, pick, lag_weight, *pieces, *rows)


def spread(value, feature, model):
    lane = lax.broadcasted_iota(jnp.int32, (value.shape[0], model), 1)
    return jnp.sum(jnp.where(lane == feature, value, 0.0), axis=0, keepdims=True)


def grad_kernel(plan, size_l, gain_own, lags, cuts, info, gain_ref, lag_ref, spec_in, *refs):
    pieces, refs = refs[: len(plan)], refs[len(plan) :]
    rows_in, refs = refs[:10], refs[10:]
    count = len(cuts)
    outs, gain_out, refs = refs[:count], refs[count], refs[count + 1 :]
    shares, d_mix, spec, total, weight, sem_in, sem_spec, sem_w, sem_out = refs
    features = total.shape[1]
    model = total.shape[0]
    rows = spec.shape[1]
    own = 3 * BLOCK // size_l

    def share_of(rel, l):
        return rel * size_l + (info[18] ^ l if size_l == 2 else l)

    packed_copies(info, rows_in, d_mix, sem_in, start)
    chunk_copies(info, spec_in, spec, sem_spec, start)
    weight[pl.ds(12 * BLOCK, BLOCK)] = lag_ref[...]
    weights = weight_copies(info, plan, pieces, weight, sem_w)
    for copy in weights:
        copy.start()
    total[...] = jnp.zeros_like(total)
    packed_copies(info, rows_in, d_mix, sem_in, finish)

    def chunk(c, carry):
        base = pl.multiple_of(c * rows, rows)
        here = pl.ds(base, rows)
        pltpu.make_async_copy(spec_in.at[here], spec.at[c], sem_spec.at[c]).wait()
        for tile in range(0, rows, 128):

            @pl.when(base + tile >= info[27])
            def _(tile=tile):
                spec[c, pl.ds(tile, 128)] = jnp.zeros((128, features), BF)
                d_mix[pl.ds(base + tile, 128)] = jnp.zeros((128, d_mix.shape[1]), BF)

        dm_t = jnp.transpose(d_mix[here].astype(F32)).astype(BF)
        for block in range(features // BLOCK):
            cols = pl.ds(block * BLOCK, BLOCK)
            total[:, cols] += dot(dm_t, spec[c, :, cols])
        return carry

    lax.fori_loop(0, chunks_of(info, rows), chunk, 0)
    for copy in weights:
        copy.wait()
    lag_span = lags * size_l
    columns = feature_gains(info, gain_ref, model, gain_own, lag_span)
    places = feature_places(info, model, lag_span)
    sums = [None, None, None]
    for block in range(features // BLOCK):
        kind = 2 if block == 12 else block % 3 % 2
        value = jnp.transpose(total[:, pl.ds(block * BLOCK, BLOCK)])
        part = jnp.sum(
            value * weight[pl.ds(block * BLOCK, BLOCK)].astype(F32), axis=1, keepdims=True
        )
        sums[kind] = part if sums[kind] is None else sums[kind] + part
        value = (value * columns[kind]).astype(BF)
        if block < 12:
            rel, branch, first = block // 6, block // 3 % 2, block % 3 * BLOCK
            at = first
            while at < first + BLOCK:
                l, inside = at // own, at % own
                size = min(own - inside, first + BLOCK - at)
                shares[share_of(rel, l), pl.ds(branch * own + inside, size)] = value[
                    at - first : at - first + size
                ]
                at += size
        else:
            for rel in range(HALVES):
                for l in range(size_l):
                    at = (rel * size_l + l) * lags
                    shares[share_of(rel, l), pl.ds(2 * own, lags)] = value[at : at + lags]
    copies = []
    for out, parts in zip(outs, cuts):
        at = 0
        for k, a, b in parts:
            source, into = shares.at[k, pl.ds(a, b - a)], out.at[pl.ds(at, b - a)]
            if len(parts) == 1:
                into = out
            copies.append(pltpu.make_async_copy(source, into, sem_out.at[len(copies)]))
            copies[-1].start()
            at += b - a
    gain_out[...] = jnp.zeros_like(gain_out)
    for kind in range(3):
        gain_out[0:1] += spread(sums[kind], places[kind], model)
    for copy in copies:
        copy.wait()


def grad_call(info, plan, gain_own, gain, lag_weight, spec, pieces, rows, size_l, lags, cuts):
    seq_len, model = rows[0].shape
    tokens, features = spec.shape
    share_rows = 6 * BLOCK // size_l + lags
    shapes = tuple(
        jax.ShapeDtypeStruct((sum(b - a for _, a, b in parts), model), BF) for parts in cuts
    )
    return pl.pallas_call(
        functools.partial(grad_kernel, plan, size_l, gain_own, lags, cuts),
        out_shape=shapes + (jax.ShapeDtypeStruct((8, model), F32),),
        in_specs=[SM, VM, VM] + [ANY] * (11 + len(plan)),
        out_specs=(ANY,) * len(shapes) + (VM,),
        scratch_shapes=[
            pltpu.VMEM((HALVES * size_l, share_rows, model), BF),
            pltpu.VMEM((tokens, model), BF),
            pltpu.VMEM((MEMBERS, seq_len, features), BF),
            pltpu.VMEM((model, features), F32),
            pltpu.VMEM((features, model), BF),
            pltpu.SemaphoreType.DMA((MEMBERS, 2)),
            pltpu.SemaphoreType.DMA((MEMBERS,)),
            pltpu.SemaphoreType.DMA((3 * len(plan),)),
            pltpu.SemaphoreType.DMA((sum(len(parts) for parts in cuts),)),
        ],
        **params(8_000_000_000, 30_000_000),
    )(info, gain, lag_weight, spec, *pieces, *rows)


def mlp_kernel(info, gain_ref, x_ref, own_ref, got1_ref, got2_ref, cot_ref, *refs):
    packs, refs = refs[:10], refs[10:]
    wide_out, (normed_ref, d_out_ref, d_middle_out, row_out, output, gain_out) = refs[:3], refs[3:9]
    held, wide, middle_ref, back_ref, ahead_ref, sem, sem_out = refs[9:]
    seq_len, model = x_ref.shape
    devices, blocks, _, _ = held.shape
    count = blocks // 3
    size_l = devices // (HALVES * MEMBERS)
    half = HALVES * size_l // 2
    copies = []
    for j in range(MEMBERS):
        for ref, first in halves_of(packs, j):
            first = first // blocks
            for k in range(ref.shape[0] // blocks):
                rel, l = (first + k) // size_l, (first + k) % size_l
                l = info[18] ^ l if size_l == 2 else l
                device = ((info[17] ^ rel) * MEMBERS + info[9 + j]) * size_l + l
                source = ref.at[pl.ds(k * blocks, blocks)]
                copies.append(pltpu.make_async_copy(source, held.at[device], sem.at[len(copies)]))
    for copy in copies:
        copy.start()
    gain = gain_ref[...]
    middle = x_ref[...] + (
        own_ref[...] + got1_ref[...].astype(F32) + got2_ref[...].astype(F32)
    )
    middle_ref[...] = middle
    scale = rms_scale(middle)
    normed_ref[...] = (middle * scale * gain).astype(BF)
    keep = lax.broadcasted_iota(jnp.int32, (seq_len, 1), 0) < info[0]
    d_out_ref[...] = jnp.where(keep, cot_ref[...], 0.0).astype(BF)
    for copy in copies:
        copy.wait()
    root, cubic = 0.7978845608028654, 0.044715
    out_copies = []
    for s in range(count):
        cols = pl.ds(s * model, model)
        normed, d_out = normed_ref[...], d_out_ref[...]
        gate_s = held[:, s].reshape(model, model)
        up_s = held[:, count + s].reshape(model, model)
        pre = dot(normed, gate_s)
        upward = dot(normed, up_s)
        share = devices // count
        down_s = held[pl.ds(s * share, share), 2 * count :].reshape(model, model)
        d_hidden = dot_nt(d_out, down_s)
        square = pre * pre
        tanh = jnp.tanh(root * pre * (1.0 + cubic * square))
        half = 0.5 * (1.0 + tanh)
        slope = half + 0.5 * pre * (1.0 - tanh * tanh) * (root * (1.0 + 3.0 * cubic * square))
        active = pre * half
        hidden = (active * upward).astype(BF)
        d_gate = (d_hidden * upward * slope).astype(BF)
        d_up = (d_hidden * active).astype(BF)
        for k, value in enumerate((hidden, d_gate, d_up)):
            wide[k, :, cols] = value
            copy = pltpu.make_async_copy(
                wide.at[k, :, cols], wide_out[k].at[:, cols], sem_out.at[k, s]
            )
            copy.start()
            out_copies.append(copy)
        back = dot_nt(d_gate, gate_s) + dot_nt(d_up, up_s)
        ahead = dot(hidden, down_s)
        if s == 0:
            back_ref[...] = back
            ahead_ref[...] = ahead
        else:
            back_ref[...] += back
            ahead_ref[...] += ahead
    middle, back = middle_ref[...], back_ref[...]
    d_middle = jnp.where(keep, cot_ref[...], 0.0) + rms_back(middle, scale, back * gain)
    d_middle_out[...] = d_middle
    row_out[...] = d_middle.astype(BF)
    output[...] = jnp.where(keep, middle + ahead_ref[...], 0.0)
    gain_out[...] = jnp.zeros_like(gain_out)
    gain_out[0:1] = jnp.sum(back * (middle * scale), axis=0, keepdims=True)
    for copy in out_copies:
        copy.wait()


def mlp_call(info, gain, x, sums, cotangent, packs, devices):
    seq_len, model = x.shape
    blocks = packs[0].shape[0] * MEMBERS // devices
    own = packs[0].shape[1]
    inner = blocks // 3 * model
    wide = jax.ShapeDtypeStruct((seq_len, inner), BF)
    whole = jax.ShapeDtypeStruct((seq_len, model), F32)
    short = jax.ShapeDtypeStruct((seq_len, model), BF)
    count = inner // model
    return pl.pallas_call(
        mlp_kernel,
        out_shape=(wide, wide, wide, short, short, whole, short, whole)
        + (jax.ShapeDtypeStruct((8, model), F32),),
        in_specs=[SM] + [VM] * 6 + [ANY] * 10,
        out_specs=(ANY, ANY, ANY) + (VM,) * 6,
        scratch_shapes=[
            pltpu.VMEM((devices, blocks, own, model), BF),
            pltpu.VMEM((3, seq_len, inner), BF),
            pltpu.VMEM((seq_len, model), F32),
            pltpu.VMEM((seq_len, model), F32),
            pltpu.VMEM((seq_len, model), F32),
            pltpu.SemaphoreType.DMA((devices,)),
            pltpu.SemaphoreType.DMA((3, count)),
        ],
        **params(6_500_000_000, 16_000_000),
    )(info, gain, x, *sums, cotangent, *packs)


def mlp_grad_kernel(normed_ref, d_out_ref, hidden, d_gate, d_up, out, wide, total, sem, sem_out):
    model = normed_ref.shape[1]
    inner = wide.shape[2]
    count = inner // model
    groups, size_l, _, blocks, own, _ = total.shape
    copies = [
        pltpu.make_async_copy(source, wide.at[k], sem.at[k])
        for k, source in enumerate((d_gate, d_up, hidden))
    ]
    for copy in copies:
        copy.start()

    def turned(value):
        return jnp.transpose(value.astype(F32)).astype(BF)

    normed_t = turned(normed_ref[...])
    for k in range(2):
        copies[k].wait()
        for s in range(count):
            value = dot(normed_t, wide[k, :, pl.ds(s * model, model)]).astype(BF)
            value = value.reshape(HALVES, groups, size_l, own, model)
            for h in range(HALVES):
                total[:, :, h, k * count + s] = value[h]
    copies[2].wait()
    share = HALVES * groups // count
    for s in range(count):
        value = dot(turned(wide[2, :, pl.ds(s * model, model)]), d_out_ref[...]).astype(BF)
        h, at = s * share // groups, s * share % groups
        total[pl.ds(at, share), :, h, 2 * count :] = value.reshape(
            share, size_l, count, own, model
        )
    copy = pltpu.make_async_copy(total, out, sem_out)
    copy.start()
    copy.wait()


def mlp_grad_call(normed, d_out, hidden, d_gate, d_up, size_l):
    seq_len, inner = hidden.shape
    model = normed.shape[1]
    count = inner // model
    own = model // (HALVES * MEMBERS * size_l)
    shape = (MEMBERS, size_l, HALVES, 3 * count, own, model)
    return pl.pallas_call(
        mlp_grad_kernel,
        out_shape=jax.ShapeDtypeStruct(shape, BF),
        in_specs=[VM, VM, ANY, ANY, ANY],
        out_specs=ANY,
        scratch_shapes=[
            pltpu.VMEM((3, seq_len, inner), BF),
            pltpu.VMEM(shape, BF),
            pltpu.SemaphoreType.DMA((3,)),
            pltpu.SemaphoreType.DMA,
        ],
        **params(3_200_000_000, 14_000_000),
    )(normed, d_out, hidden, d_gate, d_up)


def body(
    inputs,
    cotangent,
    lengths,
    filters,
    gain_first,
    mix_plus,
    mix_minus,
    auto_weight,
    gain_second,
    w_gate,
    w_upward,
    w_down,
):
    _, seq_len, model = inputs.shape
    size_l = lax.axis_size("l")
    n = HALVES * MEMBERS * size_l
    h, m, l = lax.axis_index("h"), lax.axis_index(GROUP), lax.axis_index("l")
    me = (h * MEMBERS + m) * size_l + l
    own = gain_first.shape[0]
    inner = w_gate.shape[1]
    count = inner // model

    def blocks(w):
        return jnp.transpose(w.astype(BF).reshape(own, count, model), (1, 0, 2))

    pack = jnp.concatenate(
        [blocks(w_gate), blocks(w_upward), w_down.astype(BF).reshape(count, own, model)], axis=0
    )
    pack_rows = 3 * count * own
    plus, minus, auto = mix_plus.astype(BF), mix_minus.astype(BF), auto_weight.astype(BF)
    own_rows, lag_rows = plus.shape[0], auto.shape[0]
    share_rows = 2 * own_rows + lag_rows
    sizes, cuts = [], [0]
    if size_l == 2:
        a, b = own_rows * 13 // 24, own_rows // 3
        chunks = [
            pack.reshape(pack_rows, model),
            plus[:a],
            jnp.concatenate([plus[a:], minus[:b]], axis=0),
            jnp.concatenate([minus[b:], auto], axis=0),
        ]
        cuts = [0, 0, a, own_rows + b, share_rows]
        sizes = [part.shape[0] for part in chunks]
    far, pairs = [None] * 4, [None] * 5

    def cross(k):
        if size_l == 2:
            far[k] = flip(chunks[k], "h", 1)

    def cross_l(k):
        if size_l == 2:
            both = ([chunks[k]] if k < 4 else []) + ([far[k - 1]] if k else [])
            pairs[k] = flip(jnp.concatenate(both, axis=0) if len(both) > 1 else both[0], "l", 1)

    x = inputs[0]
    scale_one = rms_scale(x)
    pre_one = x * scale_one
    gains = jnp.concatenate([gain_first.astype(BF), gain_second.astype(BF)]).astype(F32)
    peers = HALVES * size_l
    here = lax.broadcasted_iota(jnp.int32, (peers, 1), 0) == h * size_l + l
    gains = jnp.where(here, gains[None], 0.0).reshape(1, -1)
    gains = sum_peers(gains)[0]
    line = jnp.concatenate(
        [
            gains.astype(BF),
            (lengths // 16).astype(BF),
            (lengths % 16).astype(BF),
            jnp.zeros((model - 2 * own * peers - 2,), BF),
        ]
    )
    below = lax.broadcasted_iota(jnp.int32, (32, 1), 0) == 0
    below = jnp.where(below, line[None, :], 0.0).astype(BF)
    row = Gather(jnp.concatenate([pre_one.astype(BF), below], axis=0))

    cross(0)
    cross_l(0)
    if size_l == 2:
        row.row, filters, far[0], pairs[0], *chunks[1:] = sync_all(
            row.row, filters, far[0], pairs[0], *chunks[1:]
        )
    cross(1)
    cross_l(1)
    row.first()
    fwd_table, bwd_table = build_tables(filters, h, m)

    far, pairs, row, fwd_table = sync_all(far, pairs, row, fwd_table)
    if size_l == 2:
        *chunks[2:], far[1] = sync_all(*chunks[2:], far[1])
    cross(2)
    cross_l(2)
    row.second(core=False)
    row.core1 = flip(row.near1, "m", 1)
    late = sync_all(m, row.near1)[0]
    members = late ^ lax.iota(jnp.int32, MEMBERS)
    place = jnp.concatenate([jnp.stack([late % 2]), members, jnp.stack([h, l])])

    col = lax.broadcasted_iota(jnp.int32, (LAGS, model, BLOCK), 2)
    feature = lax.broadcasted_iota(jnp.int32, (LAGS, model, BLOCK), 1)
    feature = (feature + (late % 2) * BLOCK) % model
    lag = lax.broadcasted_iota(jnp.int32, (LAGS, model, BLOCK), 0)
    lag_span = lag_rows * size_l
    rel = col // lag_span
    source = lag_span * (MEMBERS * (h ^ rel) + late) + col % lag_span
    pick = ((rel < 2) & (source == lag * model + feature)).astype(BF)

    if size_l == 2:
        held = [chunks[0], pairs[0], far[0], pairs[1][sizes[1] :]]
    else:
        held = [lax.all_gather(part, "l", axis=0) for part in (pack, flip(pack, "h", 1))]
    pack = Gather(jnp.concatenate(held, axis=0).reshape(-1, own, model))

    far, pairs, row, pick, place, pack = sync_all(far, pairs, row, pick, place, pack)
    if size_l == 2:
        chunks[3], far[2] = sync_all(chunks[3], far[2])
    cross(3)
    cross_l(3)
    row.third()
    row.core2 = flip(row.near2, "m", 1)
    pack.first()
    x_rows = row.result()
    spec, info, gains = conv_call(own, n, place, fwd_table, pick, x_rows, seq_len)

    far, pairs, gains, spec = sync_all(far, pairs, gains, spec)
    cross_l(4)
    pack = sync_all(pack, spec)[0]
    pack.second()

    pairs, gains, spec = sync_all(pairs, gains, spec)
    gain_one = gains[:, :own].reshape(1, model)
    gain_two = gains[:, own : 2 * own].reshape(1, model)
    plan, pieces = [], []
    if size_l == 2:
        for k in (1, 2, 3):
            at, size = cuts[k], sizes[k]
            plan.append((0, "mine", at, size, own_rows, 0))
            plan.append((1, "mine", at, size, own_rows, 0))
            plan.append((0, "other", at, size, own_rows, 0))
            plan.append((1, "other", at, size, own_rows, sizes[k + 1] if k < 3 else 0))
            pieces += [chunks[k], far[k], pairs[k], pairs[k + 1]]
        lag_weight = jnp.zeros((BLOCK, model), BF)
    else:
        share = jnp.concatenate([plus, minus, auto], axis=0)
        shares = lax.all_gather(share, ("h", "l"), axis=0)
        shares = shares.reshape((HALVES, size_l) + share.shape)
        lag_weight = []
        for rel in range(HALVES):
            half = lax.dynamic_index_in_dim(shares, h ^ rel, 0, keepdims=False)
            lag_weight.append(half[:, 2 * own_rows :])
            for k in range(size_l):
                plan.append((rel, k, 0, 2 * own_rows, own_rows, 0))
                pieces.append(half[k, : 2 * own_rows])
        lag_weight = jnp.stack(lag_weight).reshape(HALVES * lag_span, model)
        lag_weight = jnp.pad(lag_weight, ((0, BLOCK - HALVES * lag_span), (0, 0)))
    plan = tuple(plan)
    mixed = Reduce(mix_call(info, plan, own, lag_span, gains, lag_weight, spec, pieces))

    mixed, pack = sync_all(mixed, pack)
    mixed.first()
    mixed = sync_all(mixed)[0]
    mixed.second()
    pack.third()
    mixed = sync_all(mixed)[0]
    mixed = mixed.third()

    hidden, d_gate, d_up, normed_two, d_out_b, d_middle, d_row, output, grad_gain_two = mlp_call(
        info, gain_two, x, mixed, cotangent[0], pack.result(), n
    )
    grad_gain_two = grad_gain_two[0:1]

    row = Gather(d_row)
    row.first()

    mlp = mlp_grad_call(normed_two, d_out_b, hidden, d_gate, d_up, size_l)

    row, mlp = sync_all(row, mlp)
    row.second()

    row, grad_gain_two, mlp = sync_all(row, grad_gain_two, mlp)
    mlp = lax.psum_scatter(mlp, GROUP, scatter_dimension=0)
    row.third()
    d_rows = row.result()
    if size_l == 2:
        cut = share_rows * 5 // 8 - 14
        cuts = (
            ((3, 0, cut),),
            ((3, cut, share_rows), (1, 0, share_rows)),
            ((2, 0, cut),),
            ((2, cut, share_rows),),
            ((0, 0, share_rows),),
        )
    else:
        cuts = tuple(((k, 0, share_rows),) for k in range(HALVES * size_l))
    *grad_mix, gain_mix = grad_call(
        info, plan, own, gains, lag_weight, spec, pieces, d_rows, size_l, lag_rows, cuts
    )

    grad_mix, d_rows = sync_all(grad_mix, d_rows)
    grad_gains = jnp.concatenate([gain_mix[0:1], grad_gain_two], axis=0)
    grad_gains = sum_direct(grad_gains, GROUP, 3)
    grad_gains = sum_direct(grad_gains, GROUP, 4)
    if size_l == 2:
        got_far, got_rest = flip(grad_mix[0], "l", 1), flip(grad_mix[1], "l", 1)
        d_rows, got_far, grad_gains = sync_all(d_rows, got_far, grad_gains)
        back = [flip((grad_mix[2].astype(F32) + got_far.astype(F32)).astype(BF), "h", 1)]
    d_normed = Reduce(back_conv_call(info, plan, bwd_table, pick, lag_weight, pieces, d_rows))

    if size_l == 2:
        d_normed, back, got_rest = sync_all(d_normed, back, got_rest)
    d_normed.first()

    d_normed, grad_gains, mlp = sync_all(d_normed, grad_gains, mlp)
    d_normed.second()
    if size_l == 2:
        got_rest = sync_all(got_rest, d_normed.own)[0]
        left = share_rows - cut
        part = (grad_mix[3].astype(F32) + got_rest[:left].astype(F32)).astype(BF)
        back.append(flip(part, "h", 1))
        other = lax.dynamic_index_in_dim(mlp, 1 - l, 0, keepdims=False)
        mlp = lax.dynamic_index_in_dim(mlp, l, 0, keepdims=False).astype(F32)
        blocks_left = other.shape[0] * other.shape[1]
        other = jnp.concatenate(
            [other.reshape((blocks_left,) + other.shape[2:]), two_parts(grad_gains, own)], axis=0
        )
        other = flip(other, "l", 1)
        grad_gains = grad_gains + whole_of(other[blocks_left])
        mlp = mlp + other[:blocks_left].reshape(mlp.shape).astype(F32)
    else:
        grad_gains = lax.psum(grad_gains, "l")
        mlp = lax.psum_scatter(mlp.astype(F32), "l", scatter_dimension=0)

    d_normed = sync_all(d_normed)[0]
    if size_l == 2:
        grad_gains, mlp = sync_all(grad_gains, mlp, d_normed.near1, d_normed.near2)[:2]
        back, got_rest = sync_all(back, got_rest, d_normed.near1, mlp)[:2]
    else:
        grad_gains, mlp = sync_all(grad_gains, mlp, d_normed.near1)[:2]
    d_normed = d_normed.third()
    if size_l == 2:
        other = lax.dynamic_index_in_dim(mlp, 1 - h, 0, keepdims=False).astype(BF)
        other = flip(jnp.concatenate([other, two_parts(grad_gains, own)], axis=0), "h", 1)
        mlp = lax.dynamic_index_in_dim(mlp, h, 0, keepdims=False) + other[:-1].astype(F32)
        grad_gains = grad_gains + whole_of(other[-1])
    else:
        mlp_far = lax.dynamic_index_in_dim(mlp, 1 - h, 0, keepdims=False).astype(BF)
        mlp_near = lax.dynamic_index_in_dim(mlp, h, 0, keepdims=False)
        mlp = mlp_near + flip(mlp_far, "h", 1).astype(F32)
        grad_gains = grad_gains + flip(grad_gains, "h", 1)
    grad_gains = lax.dynamic_slice_in_dim(grad_gains, me * own, own, 1)
    own_sum, got1, got2 = d_normed
    d_normed = own_sum + got1.astype(F32) + got2.astype(F32)
    input_grad = d_middle + rms_back(x, scale_one, d_normed * gain_one)
    if size_l == 2:
        near = grad_mix[4].astype(F32) + got_rest[left:].astype(F32)
        grad_mix = near + jnp.concatenate(back, axis=0).astype(F32)
    else:
        both = jnp.stack(grad_mix).reshape((HALVES, size_l) + grad_mix[0].shape)
        grad_mix = jnp.where(h == 0, both, both[::-1]).reshape((-1,) + both.shape[2:])
        grad_mix = lax.psum_scatter(grad_mix, ("h", "l"), scatter_dimension=0).astype(F32)
    mlp = mlp.reshape(3, count, own, model)
    grad_gate, grad_up = [
        jnp.transpose(mlp[k], (1, 0, 2)).reshape(own, inner) for k in range(2)
    ]
    grad_down = mlp[2].reshape(count * own, model)

    return (
        output[None],
        input_grad[None],
        grad_gains[0],
        grad_mix[:own_rows],
        grad_mix[own_rows : 2 * own_rows],
        grad_mix[2 * own_rows :],
        grad_gains[1],
        grad_gate,
        grad_up,
        grad_down,
    )


def solution(mesh):
    shape = (HALVES, 2, 2, 2, mesh.size // (HALVES * MEMBERS))
    inner = Mesh(mesh.devices.reshape(shape), ALL)
    row, vec, mat = P(ALL, None, None), P(ALL), P(ALL, None)
    in_specs = (row, row, vec, P(), vec, mat, mat, mat, vec, mat, mat, mat)
    out_specs = (row, row, vec, mat, mat, mat, vec, mat, mat, mat)
    return jax.shard_map(body, mesh=inner, in_specs=in_specs, out_specs=out_specs, check_vma=False)
```
